32 devices in a mesh: dp: 8 (over y, x, core), fsdp: 4 (over z).
Axes of the slice: x: 2, y: 2, z: 4, core: 2. Of those that a mesh axis runs over, the one named last changes fastest.
Arguments:
- hidden_in: bfloat16 [16384, 768], P(('dp', 'fsdp')), may hold values from -6 to 6
- lengths: int32 [1024], P(('dp', 'fsdp')), may hold values from 4 to 16
- images: bfloat16 [1024, 768], P(('dp', 'fsdp')), may hold values from -12 to 12
- labels: int32 [1024], P(('dp', 'fsdp')), may hold values from 0 to 1023, each once
- wide_master: float32 [768, 6144], P('fsdp'), may hold values from -0.18042196 to 0.18042196
- down_master: float32 [3072, 768], P('fsdp'), may hold values from -0.109375 to 0.109375
- vector_master: float32 [12, 768], P(None, 'fsdp'), may hold values from -0.5 to 1.5
- wide_momentum: float32 [768, 6144], P('fsdp'), may hold values from -7.68 to 7.68
- down_momentum: float32 [3072, 768], P('fsdp'), may hold values from -7.68 to 7.68
- vector_momentum: float32 [12, 768], P(None, 'fsdp'), may hold values from -38.4 to 38.4
- wide_average: float32 [768, 6144], P('fsdp'), may hold values from -0.18042196 to 0.18042196
- down_average: float32 [3072, 768], P('fsdp'), may hold values from -0.109375 to 0.109375
- vector_average: float32 [12, 768], P(None, 'fsdp'), may hold values from -0.5 to 1.5
Outputs:
- block_out: bfloat16 [16384, 768], P(('dp', 'fsdp'))
- input_grad: float32 [16384, 768], P(('dp', 'fsdp'))
- wide_new: float32 [768, 6144], P('fsdp')
- down_new: float32 [3072, 768], P('fsdp')
- vector_new: float32 [12, 768], P(None, 'fsdp')
- wide_momentum_new: float32 [768, 6144], P('fsdp')
- down_momentum_new: float32 [3072, 768], P('fsdp')
- vector_momentum_new: float32 [12, 768], P(None, 'fsdp')
- wide_average_new: float32 [768, 6144], P('fsdp')
- down_average_new: float32 [3072, 768], P('fsdp')
- vector_average_new: float32 [12, 768], P(None, 'fsdp')
- wide_copy: bfloat16 [768, 6144], P('fsdp')
- down_copy: bfloat16 [3072, 768], P('fsdp')
- vector_copy: bfloat16 [12, 768], P(None, 'fsdp')
The draws below stay inside these ranges and needn't reach their ends.
Inputs may be any that keep to these rules, and one draw needn't show every extreme that they name: labels name every caption exactly once.
All inputs are finite; a program needn't handle non-finite values.
Results may differ from the reference program's by a relative error of at most 0.017.
Values may be sent and summed in bfloat16 or wider, within the bound.
No kernel may reach another device: no remote copies, remote signals or barrier semaphores. Data moves between devices by JAX's collectives and lax.ppermute only.
A program may use at most 192 MiB of HBM per device.

```python
import math
import jax
import jax.numpy as jnp
from jax import lax

D = 768
HEADS = 12
HEAD_DIM = 64
FF = 3072
SEQ = 16
CAPTIONS = 1024
TOKENS = 16384


def wide_table(key):
    base = jax.random.uniform(key, (D, 4 * D + FF), jnp.float32, -1.7, 1.7)
    columns = jnp.arange(4 * D + FF)[None, :]
    factor = jnp.where((columns >= 3 * D) & (columns < 4 * D), 2.5, 1.0)
    return base * factor / jnp.sqrt(jnp.float32(D))


def vector_table(key):
    gain_key, bias_key = jax.random.split(key)
    gains = jax.random.uniform(gain_key, (12, D), jnp.float32, 0.6, 1.4)
    biases = jax.random.uniform(bias_key, (12, D), jnp.float32, -0.5, 0.5)
    row_ids = jnp.arange(12)[:, None]
    return jnp.where((row_ids == 0) | (row_ids == 5), gains, biases)


def draw_wide_master(key, part):
    key = jax.random.fold_in(key, 1)
    return wide_table(key)


def draw_wide_average(key, part):
    key = jax.random.fold_in(key, 2)
    return wide_table(key)


def draw_vector_master(key, part):
    key = jax.random.fold_in(key, 3)
    return vector_table(key)


def draw_vector_average(key, part):
    key = jax.random.fold_in(key, 4)
    return vector_table(key)


def touch_ends(values, stream_key, smallest, largest):
    place = [jax.random.randint(jax.random.fold_in(stream_key, axis), (), 0, length) for axis, length in enumerate(values.shape)]
    main_axis = values.shape.index(max(values.shape))
    neighbour = place[:main_axis] + [(place[main_axis] + 1) % values.shape[main_axis]] + place[main_axis + 1:]
    return values.at[tuple(place)].set(smallest).at[tuple(neighbour)].set(largest)


def block_levels(stream_key, dims, cuts, least, top_value):
    gain = 1.0
    for axis_at, shards_of in cuts:
        steps = jax.random.uniform(jax.random.fold_in(jax.random.fold_in(stream_key, 6), axis_at), (shards_of,), jnp.float32, least / len(cuts), top_value / len(cuts))
        gain = gain * jnp.repeat(jnp.exp(steps), dims[axis_at] // shards_of).reshape((-1,) + (1,) * (len(dims) - 1 - axis_at))
    return gain


def scatter_about(own_key, extent, deviation, bound, cuts=(), kind=jnp.bfloat16):
    level = block_levels(own_key, extent, cuts, -0.22, 0.18) if cuts else 1.0
    entries = jax.random.normal(own_key, extent, jnp.float32) * deviation * level
    return jnp.minimum(jnp.maximum(entries, -bound), bound).astype(kind)


def setup_inputs(seed: int = 0) -> dict:
    key_of = jax.random.split(jax.random.key(seed), 14)
    hidden_in = scatter_about(key_of[0], (TOKENS, D), 1.0, 6.0, ((0, 32),))
    lengths = touch_ends(jax.random.randint(key_of[1], (CAPTIONS,), SEQ // 4, SEQ + 1), jax.random.fold_in(key_of[1], 1), SEQ // 4, SEQ).astype(jnp.int32)
    images = scatter_about(key_of[2], (CAPTIONS, D), 2.0, 12.0, ((0, 32),))
    labels = jax.random.permutation(key_of[3], CAPTIONS).astype(jnp.int32)
    wide_master = draw_wide_master(jax.random.fold_in(key_of[13], 71), 0)
    down_master = scatter_about(key_of[5], (FF, D), FF ** -0.5, 0.109375, ((0, 4),), jnp.float32)
    vector_master = draw_vector_master(jax.random.fold_in(key_of[13], 71), 0)
    wide_momentum = scatter_about(key_of[7], (D, 4 * D + FF), (TOKENS ** 0.5 / 100), 7.68, ((0, 4),), jnp.float32)
    down_momentum = scatter_about(key_of[8], (FF, D), (TOKENS ** 0.5 / 100), 7.68, ((0, 4),), jnp.float32)
    vector_momentum = scatter_about(key_of[9], (12, D), (TOKENS ** 0.5 / 20), 38.4, ((1, 4),), jnp.float32)
    wide_average = draw_wide_average(jax.random.fold_in(key_of[13], 71), 0)
    down_average = scatter_about(key_of[11], (FF, D), FF ** -0.5, 0.109375, ((0, 4),), jnp.float32)
    vector_average = draw_vector_average(jax.random.fold_in(key_of[13], 71), 0)
    return {"hidden_in": hidden_in, "lengths": lengths, "images": images, "labels": labels, "wide_master": wide_master, "down_master": down_master, "vector_master": vector_master, "wide_momentum": wide_momentum, "down_momentum": down_momentum, "vector_momentum": vector_momentum, "wide_average": wide_average, "down_average": down_average, "vector_average": vector_average}


@jax.custom_vjp
def low(v):
    return lax.optimization_barrier(v.astype(jnp.bfloat16)).astype(jnp.float32)

@jax.custom_vjp
def low_back(v):
    return v

def low_keep(v):
    return (low(v), None)

def low_pass(kept, grad):
    return (grad,)

def back_keep(v):
    return (v, None)

def back_low(kept, grad):
    return (low(grad),)
low.defvjp(low_keep, low_pass)
low_back.defvjp(back_keep, back_low)
norm_epsilon = 1e-06
masked_score = -1e+30
learn_rate = 0.02
momentum_decay = 0.5
average_decay = 0.5

def wide_dot(left, right):
    return jnp.dot(left, right, precision=lax.Precision.HIGHEST, preferred_element_type=jnp.float32)

def layer_norm(values, scale_row, shift_row):
    centre = values - lax.optimization_barrier(jnp.mean(values, axis=-1, keepdims=True))
    spread = lax.optimization_barrier(jnp.mean(centre * centre, axis=-1, keepdims=True))
    return centre * lax.rsqrt(spread + norm_epsilon) * scale_row + shift_row

def tower(token_x, seq_lens, wide_w, down_w, vectors):
    captions = seq_lens.shape[0]
    normed = low(layer_norm(token_x, vectors[0], vectors[1]))
    qkv_bias = jnp.concatenate([vectors[2], jnp.zeros_like(vectors[2]), vectors[3]])
    joined = low(low_back(wide_dot(normed, wide_w[:, :3 * D]) + qkv_bias))
    queries = joined[:, :D].reshape(captions, SEQ, HEADS, HEAD_DIM)
    key_heads = joined[:, D:2 * D].reshape(captions, SEQ, HEADS, HEAD_DIM)
    value_heads = joined[:, 2 * D:].reshape(captions, SEQ, HEADS, HEAD_DIM)
    key_mask = jnp.arange(SEQ)[None, :] < seq_lens[:, None]
    scores = jnp.einsum('cqhd,ckhd->chqk', queries, key_heads, precision=lax.Precision.HIGHEST) * HEAD_DIM ** (-0.5)
    scores = low_back(jnp.where(key_mask[:, None, None, :], scores, masked_score))
    totals = jax.nn.logsumexp(scores, axis=-1, keepdims=True)
    attn_probs = low(jnp.exp(scores - totals))
    context = jnp.einsum('chqk,ckhd->cqhd', attn_probs, value_heads, precision=lax.Precision.HIGHEST)
    context = low(low_back(context.reshape(captions * SEQ, D)))
    residual = token_x + low_back(wide_dot(context, wide_w[:, 3 * D:4 * D]) + vectors[4])
    second = low(layer_norm(residual, vectors[5], vectors[6]))
    up_proj = low_back(wide_dot(second, wide_w[:, 4 * D:]) + vectors[8:].reshape(FF))
    gelu_out = low(jax.nn.gelu(up_proj))
    block_rows = residual + low_back(wide_dot(gelu_out, down_w) + vectors[7])
    mask_f = key_mask.astype(jnp.float32)
    pooled = lax.optimization_barrier(jnp.sum(block_rows.reshape(captions, SEQ, D) * mask_f[:, :, None], axis=1)) / seq_lens[:, None].astype(jnp.float32)
    inv_norm = lax.rsqrt(lax.optimization_barrier(jnp.sum(pooled * pooled, axis=-1, keepdims=True)) + norm_epsilon)
    return (block_rows, low(pooled * inv_norm))

def bf16_copy(values):
    return lax.optimization_barrier(values.astype(jnp.bfloat16)).astype(jnp.float32)

def renew_state(master, momentum, average, gradient):
    momentum_new = momentum_decay * momentum + gradient
    master_new = master - learn_rate * (gradient + momentum_decay * momentum_new)
    average_new = average_decay * average + (1.0 - average_decay) * master_new
    return (master_new, momentum_new, average_new, master_new.astype(jnp.bfloat16))

def reference(hidden_in, lengths, images, labels, wide_master, down_master, vector_master, wide_momentum, down_momentum, vector_momentum, wide_average, down_average, vector_average):
    blocks = math.gcd(CAPTIONS, max(1, 4096 // SEQ))
    group_size = math.gcd(CAPTIONS, 512)

    def total_loss(token_x, wide_w, down_w, vectors):
        pieces = token_x.reshape(CAPTIONS // blocks, blocks * SEQ, D)
        seq_parts = lengths.reshape(CAPTIONS // blocks, blocks)

        def one_block(block_item):
            return tower(block_item[0], block_item[1], wide_w, down_w, vectors)
        block_rows, all_texts = lax.map(jax.checkpoint(one_block), (pieces, seq_parts))
        all_texts = all_texts.reshape(CAPTIONS, D)
        pictures = images.astype(jnp.float32).reshape(CAPTIONS // group_size, group_size, D)
        marks = labels.reshape(CAPTIONS // group_size, group_size)

        def image_loss(block_item):
            logits = low_back(jnp.dot(block_item[0], all_texts.T, precision=lax.Precision.HIGHEST, preferred_element_type=jnp.float32))
            totals = jax.nn.logsumexp(logits, axis=-1)
            picked = lax.optimization_barrier(jnp.sum(jnp.where(jnp.arange(CAPTIONS)[None, :] == block_item[1][:, None], logits, 0.0), axis=-1))
            return jnp.sum(totals - picked)
        loss_total = jnp.sum(lax.map(jax.checkpoint(image_loss), (pictures, marks)))
        return (loss_total, block_rows.reshape(TOKENS, D))
    loss_total, pull_back, block_rows = jax.vjp(total_loss, hidden_in.astype(jnp.float32), bf16_copy(wide_master), bf16_copy(down_master), bf16_copy(vector_master), has_aux=True)
    input_grad, wide_grad, down_grad, vector_grad = pull_back(jnp.ones_like(loss_total))
    wide_state = renew_state(wide_master, wide_momentum, wide_average, wide_grad)
    down_state = renew_state(down_master, down_momentum, down_average, down_grad)
    vector_state = renew_state(vector_master, vector_momentum, vector_average, vector_grad)
    return (block_rows.astype(jnp.bfloat16), input_grad, wide_state[0], down_state[0], vector_state[0], wide_state[1], down_state[1], vector_state[1], wide_state[2], down_state[2], vector_state[2], wide_state[3], down_state[3], vector_state[3])
```

```python
import functools

import jax
import jax.numpy as jnp
from jax import lax
from jax.experimental import pallas as pl
from jax.experimental.pallas import tpu as pltpu
from jax.sharding import PartitionSpec as P

HEADS = 12
SEQ = 16
PIECE = 384
GROUP = 8

norm_epsilon = 1e-06
masked_score = -1e30
learn_rate = 0.02
momentum_decay = 0.5
average_decay = 0.5
gelu_scale = 0.7978845608028654
gelu_cube = 0.044715

f32 = jnp.float32
bf16 = jnp.bfloat16
VMEM = pl.BlockSpec(memory_space=pltpu.VMEM)
SMEM = pl.BlockSpec(memory_space=pltpu.SMEM)
ANY = pl.BlockSpec(memory_space=pl.ANY)
PARAMS = pltpu.CompilerParams(vmem_limit_bytes=50 * 1024 * 1024)


def dot(left, right):
    return lax.dot_general(left, right, (((1,), (0,)), ((), ())), preferred_element_type=f32)


def dot_nt(left, right):
    return lax.dot_general(left, right, (((1,), (1,)), ((), ())), preferred_element_type=f32)


def dot_tn(left, right):
    return lax.dot_general(left, right, (((0,), (0,)), ((), ())), preferred_element_type=f32)


def shape(dims, kind):
    return jax.ShapeDtypeStruct(dims, kind)


def cost(flops, moved):
    return pl.CostEstimate(flops=int(flops), bytes_accessed=int(moved), transcendentals=0)


def norm_parts(values):
    centre = values - jnp.mean(values, axis=-1, keepdims=True)
    inv = lax.rsqrt(jnp.mean(centre * centre, axis=-1, keepdims=True) + norm_epsilon)
    return centre * inv, inv


def norm_back(grad, scaled, inv, gain):
    d_scaled = grad * gain
    first = jnp.mean(d_scaled, axis=-1, keepdims=True)
    second = jnp.mean(d_scaled * scaled, axis=-1, keepdims=True)
    return inv * (d_scaled - first - scaled * second)


def piece_copies(info, fs, rows, sources, target, sems, is_down):
    copies = []
    for k in range(GROUP):
        for j in range(1, fs):
            shard = info[3 + j]
            place = info[3 + fs + k]
            low, high = (j - 1) * rows, j * rows
            for ref, first in sources[k]:
                start, end = max(low, first), min(high, first + ref.shape[0])
                if start >= end:
                    continue
                inner, count = start - low, end - start
                if is_down:
                    row = shard * (4 * rows) + (place % 4) * rows + inner
                    col = (place // 4) * PIECE
                else:
                    row = shard * rows + inner
                    col = place * PIECE
                copies.append(
                    pltpu.make_async_copy(
                        ref.at[pl.ds(start - first, count), :],
                        target.at[pl.ds(pl.multiple_of(row, 16), count), pl.ds(pl.multiple_of(col, 128), PIECE)],
                        sems.at[len(copies)],
                    )
                )
    return copies


def sources_of(refs):
    table = {}
    for core in range(2):
        own, over_x, over_y, diag_a, diag_b = refs[5 * core : 5 * core + 5]
        table[core] = [(own, 0)]
        table[2 + core] = [(over_x, 0)]
        table[4 + core] = [(over_y, 0)]
        table[6 + core] = [(diag_a, 0), (diag_b, diag_a.shape[0])]
    return table


def attend_forward(queries, keys, values, mask, half_low, half_high):
    both_q = jnp.concatenate([queries * half_low, queries * half_high], axis=0)
    scores = jnp.where(mask, dot_nt(both_q, keys) * 0.125, masked_score)
    top = jnp.max(scores, axis=-1, keepdims=True)
    raised = jnp.exp(scores - top)
    probs = raised / jnp.sum(raised, axis=-1, keepdims=True)
    return both_q, probs


def lane_halves():
    lane = lax.broadcasted_iota(jnp.int32, (1, 128), 1)
    low = (lane < 64).astype(f32)
    return low, low.astype(bf16), (1.0 - low).astype(bf16)


def caption_mask(valid_row):
    row = lax.broadcasted_iota(jnp.int32, (256, 128), 0)
    col = lax.broadcasted_iota(jnp.int32, (256, 128), 1)
    same = ((row & 127) // SEQ) == (col // SEQ)
    return same & (valid_row > 0.0)


def kernel_attention(fs, rows, info, hid, valid, vec, own, *rest):
    pieces, rest = rest[:10], rest[10:]
    qkv_ref, ctx_ref, h_ref, second_ref, w_out, w, own_buf, sems, own_sem, out_sem = rest
    tokens, width = hid.shape
    copies = piece_copies(info, fs, rows, sources_of(pieces), w, sems, False)
    for copy in copies:
        copy.start()
    own_copy = pltpu.make_async_copy(own.at[:, pl.ds(0, 4 * width)], own_buf, own_sem)
    own_copy.start()
    vecs = vec[...]
    scaled, _ = norm_parts(hid[...].astype(f32))
    normed = (scaled * vecs[0:1] + vecs[1:2]).astype(bf16)
    own_copy.wait()
    w[pl.ds(pl.multiple_of(info[0] * rows, 16), rows), :] = own_buf[...].astype(bf16)
    for copy in copies:
        copy.wait()
    out_copy = pltpu.make_async_copy(w, w_out, out_sem)
    out_copy.start()
    for part in range(3):
        cols = pl.ds(part * width, width)
        value = dot(normed, w[:, cols])
        if part == 0:
            value = value + vecs[2:3]
        if part == 2:
            value = value + vecs[3:4]
        qkv_ref[:, cols] = value.astype(bf16)
    low_f, low, high = lane_halves()

    def block(index, carry):
        at = pl.ds(pl.multiple_of(index * 128, 128), 128)
        mask = caption_mask(valid[:, at])
        for pair in range(width // 128):
            here = pair * 128
            queries = qkv_ref[at, here : here + 128]
            keys = qkv_ref[at, width + here : width + here + 128]
            values = qkv_ref[at, 2 * width + here : 2 * width + here + 128]
            _, probs = attend_forward(queries, keys, values, mask, low, high)
            context = dot(probs.astype(bf16), values)
            ctx_ref[at, here : here + 128] = jnp.where(low_f > 0.0, context[:128], context[128:]).astype(bf16)
        return carry

    lax.fori_loop(0, tokens // 128, block, 0)
    residual = hid[...].astype(f32) + (dot(ctx_ref[...], w[:, 3 * width :]) + vecs[4:5])
    h_ref[...] = residual
    scaled, _ = norm_parts(residual)
    second_ref[...] = (scaled * vecs[5:6] + vecs[6:7]).astype(bf16)
    out_copy.wait()


def kernel_up(fs, rows, info, second, bias, own, *rest):
    pieces, rest = rest[:10], rest[10:]
    u_ref, g_ref, w_out, w, own_buf, sems, own_sem, out_sem = rest
    width, hidden = w.shape
    copies = piece_copies(info, fs, rows, sources_of(pieces), w, sems, False)
    own_copy = pltpu.make_async_copy(own.at[:, pl.ds(4 * width, hidden)], own_buf, own_sem)
    own_copy.start()
    for copy in copies:
        copy.start()
    own_copy.wait()
    w[pl.ds(pl.multiple_of(info[0] * rows, 16), rows), :] = own_buf[...].astype(bf16)
    for copy in copies:
        copy.wait()
    out_copy = pltpu.make_async_copy(w, w_out, out_sem)
    out_copy.start()

    def block(index, carry):
        cols = pl.ds(pl.multiple_of(index * 512, 128), 512)
        value = dot(second[...], w[:, cols]) + bias[:, cols]
        u_ref[:, cols] = value
        inner = jnp.tanh(gelu_scale * (value + gelu_cube * value * value * value))
        g_ref[:, cols] = (0.5 * value * (1.0 + inner)).astype(bf16)
        return carry

    lax.fori_loop(0, hidden // 512, block, 0)
    out_copy.wait()


def kernel_down(fs, rows, info, g, h, vec, lens, keep, images, own, *rest):
    pieces, rest = rest[:10], rest[10:]
    out_ref, pooled_ref, inv_ref, logit_ref, stat_ref, w_out, w, own_buf, sems, own_sem, out_sem = rest
    tokens, width = h.shape
    captions = tokens // SEQ
    copies = piece_copies(info, fs, rows, sources_of(pieces), w, sems, True)
    own_copy = pltpu.make_async_copy(own, own_buf, own_sem)
    own_copy.start()
    for copy in copies:
        copy.start()
    own_copy.wait()
    w[pl.ds(pl.multiple_of(info[0] * 4 * rows, 16), 4 * rows), :] = own_buf[...].astype(bf16)
    for copy in copies:
        copy.wait()
    out_copy = pltpu.make_async_copy(w, w_out, out_sem)
    out_copy.start()
    block_rows = h[...] + (dot(g[...], w[...]) + vec[7:8, :])
    out_ref[...] = block_rows.astype(bf16)
    pooled = jnp.sum((block_rows * keep[...]).reshape(captions, SEQ, width), axis=1) / lens[...]
    inv = lax.rsqrt(jnp.sum(pooled * pooled, axis=-1, keepdims=True) + norm_epsilon)
    pooled_ref[...] = pooled
    inv_ref[...] = inv
    texts = (pooled * inv).astype(bf16)
    logits = dot_nt(texts, images[:, :width])
    logit_ref[...] = logits
    top = jnp.max(logits, axis=0, keepdims=True)
    stat_ref[0:1, :] = top
    stat_ref[1:2, :] = jnp.sum(jnp.exp(logits - top), axis=0, keepdims=True)
    out_copy.wait()


def put(info, half, place, value, mine, theirs):
    rows = value.shape[0]

    @pl.when(info[1] == half)
    def _():
        mine[place[0], pl.ds(place[1], rows), :] = value

    @pl.when(info[1] != half)
    def _():
        theirs[place[0], pl.ds(place[1], rows), :] = value


def kernel_loss(rows, info, logits, stats, labels, images, pooled, inv, lens, keep, g, dpl_ref, dy_ref, bias_ref, mine, theirs):
    captions, width = pooled.shape
    tokens, hidden = g.shape
    lse = stats[0:1, :] + jnp.log(stats[1:2, :])
    number = lax.broadcasted_iota(jnp.int32, logits.shape, 0) + info[2] * captions
    onehot = (labels[...] == number).astype(f32)
    slopes = (jnp.exp(logits[...] - lse) - onehot).astype(bf16)
    text_grad = dot(slopes, images[:, :width])
    pool, inv_v = pooled[...], inv[...]
    d_pooled = inv_v * text_grad - inv_v**3 * pool * jnp.sum(pool * text_grad, axis=-1, keepdims=True)
    dpl = d_pooled / lens[...]
    dpl_ref[...] = dpl
    d_out = jnp.broadcast_to(dpl[:, None, :], (captions, SEQ, width)).reshape(tokens, width) * keep[...]
    dy = d_out.astype(bf16)
    dy_ref[...] = dy
    bias_ref[...] = jnp.sum(dy.astype(f32), axis=0, keepdims=True)
    for part in range(hidden // width):
        grad = dot_tn(g[:, part * width : (part + 1) * width], dy).astype(bf16)
        for sub in range(width // rows):
            first = part * width + sub * rows
            shard, quarter = first // (4 * rows), (first % (4 * rows)) // rows
            for half in range(2):
                value = grad[sub * rows : (sub + 1) * rows, half * PIECE : (half + 1) * PIECE]
                put(info, half, (quarter, shard * rows), value, mine, theirs)


def kernel_up_back(info, dy, u, second, w_down, du_ref, bias_ref, mine, theirs):
    tokens, hidden = u.shape
    for part in range(hidden // 768):
        cols = slice(part * 768, (part + 1) * 768)
        d_gelu = dot_nt(dy[...], w_down[cols, :])
        value = u[:, cols]
        square = value * value
        inner = jnp.tanh(gelu_scale * (value + gelu_cube * value * square))
        slope = 0.5 * (1.0 + inner) + (0.5 * gelu_scale) * value * (1.0 - inner * inner) * (1.0 + (3.0 * gelu_cube) * square)
        du = (d_gelu * slope).astype(bf16)
        du_ref[:, cols] = du
        bias_ref[:, cols] = jnp.sum(du.astype(f32), axis=0, keepdims=True)
    turned = second[...].T
    for place in range(hidden // PIECE):
        grad = dot(turned, du_ref[:, place * PIECE : (place + 1) * PIECE]).astype(bf16)
        put(info, place // 4, (place % 4, 0), grad, mine, theirs)


def kernel_attention_back(info, dpl, keep, du, h, hid, qkv, ctx, valid, vec, w_up, w_att, dh_ref, dqkv_ref, grads_ref, mine, theirs):
    tokens, width = h.shape
    captions = tokens // SEQ
    vecs = vec[...]
    d_second = dot_nt(du[...], w_up[...])
    scaled, inv = norm_parts(h[...])
    d_out = jnp.broadcast_to(dpl[...][:, None, :], (captions, SEQ, width)).reshape(tokens, width) * keep[...]
    dh = d_out + norm_back(d_second, scaled, inv, vecs[5:6])
    dh_ref[...] = dh
    da = dh.astype(bf16)
    grads_ref[2:3, :] = jnp.sum(da.astype(f32), axis=0, keepdims=True)
    grads_ref[3:4, :] = jnp.sum(d_second * scaled, axis=0, keepdims=True)
    grads_ref[4:5, :] = jnp.sum(d_second, axis=0, keepdims=True)
    d_ctx = dot_nt(da, w_att[:, 3 * width :]).astype(bf16)
    dqkv_ref[:, :width] = d_ctx
    low_f, low, high = lane_halves()

    def block(index, carry):
        at = pl.ds(pl.multiple_of(index * 128, 128), 128)
        mask = caption_mask(valid[:, at])
        for pair in range(width // 128):
            here = pair * 128
            queries = qkv[at, here : here + 128]
            keys = qkv[at, width + here : width + here + 128]
            values = qkv[at, 2 * width + here : 2 * width + here + 128]
            both_q, probs = attend_forward(queries, keys, values, mask, low, high)
            d_context = dqkv_ref[at, here : here + 128]
            both_d = jnp.concatenate([d_context * low, d_context * high], axis=0)
            d_probs = dot_nt(both_d, values)
            weighted = probs * d_probs
            d_scores = (weighted - probs * jnp.sum(weighted, axis=-1, keepdims=True)).astype(bf16)
            d_both = dot(d_scores, keys) * 0.125
            d_queries = jnp.where(low_f > 0.0, d_both[:128], d_both[128:])
            d_keys = dot_tn(d_scores, both_q) * 0.125
            d_values = dot_tn(probs.astype(bf16), both_d)
            dqkv_ref[at, here : here + 128] = d_queries.astype(bf16)
            dqkv_ref[at, width + here : width + here + 128] = d_keys.astype(bf16)
            dqkv_ref[at, 2 * width + here : 2 * width + here + 128] = d_values.astype(bf16)
        return carry

    lax.fori_loop(0, tokens // 128, block, 0)
    grads_ref[0:1, :] = jnp.sum(dqkv_ref[:, :width].astype(f32), axis=0, keepdims=True)
    grads_ref[1:2, :] = jnp.sum(dqkv_ref[:, 2 * width :].astype(f32), axis=0, keepdims=True)
    scaled, _ = norm_parts(hid[...].astype(f32))
    normed = (scaled * vecs[0:1] + vecs[1:2]).astype(bf16)
    turned = normed.T
    for place in range(6):
        grad = dot(turned, dqkv_ref[:, place * PIECE : (place + 1) * PIECE]).astype(bf16)
        put(info, place // 4, (place % 4, 0), grad, mine, theirs)
    turned = ctx[...].T
    for place in range(6, 8):
        at = (place - 6) * PIECE
        grad = dot(turned, da[:, at : at + PIECE]).astype(bf16)
        put(info, place // 4, (place % 4, 0), grad, mine, theirs)


def kernel_input_back(dqkv, dh, hid, vec, w_att, out_ref, grads_ref):
    width = hid.shape[1]
    d_normed = dot_nt(dqkv[...], w_att[:, : 3 * width])
    scaled, inv = norm_parts(hid[...].astype(f32))
    out_ref[...] = dh[...] + norm_back(d_normed, scaled, inv, vec[0:1, :])
    grads_ref[0:1, :] = jnp.sum(d_normed * scaled, axis=0, keepdims=True)
    grads_ref[1:2, :] = jnp.sum(d_normed, axis=0, keepdims=True)


def renew_state(master, momentum, average, gradient):
    momentum_new = momentum_decay * momentum + gradient
    master_new = master - learn_rate * (gradient + momentum_decay * momentum_new)
    average_new = average_decay * average + (1.0 - average_decay) * master_new
    return (master_new, momentum_new, average_new, master_new.astype(bf16))


def kernel_renew(fs, info, grad_a, grad_b, master, momentum, average, *rest):
    outs = rest[-4:]
    step = pl.program_id(0)

    def write(grad):
        new = renew_state(master[...], momentum[...], average[...], grad[0].astype(f32))
        for ref, value in zip(outs, new):
            ref[...] = value

    @pl.when(step < 4)
    def _():
        write(grad_a)

    @pl.when(step >= 4)
    def _():
        write(grad_b)


def renew(info, fs, rows, grads, master, momentum, average, column, earlier):
    def place(step, info):
        rel = 2 * (step % 4) + step // 4
        spot = info[3 + fs + rel]
        if column is None:
            return (spot % 4, spot // 4)
        return (0, column + spot)

    block = pl.BlockSpec((rows, PIECE), place)
    in_specs = [
        pl.BlockSpec((1, rows, PIECE), lambda step, info: (jnp.minimum(step, 3), 0, 0)),
        pl.BlockSpec((1, rows, PIECE), lambda step, info: (jnp.maximum(step - 4, 0), 0, 0)),
        block,
        block,
        block,
    ]
    aliases = {}
    if earlier:
        in_specs += [ANY] * 4
        aliases = {6 + i: i for i in range(4)}
    kinds = [f32, f32, f32, bf16]
    return pl.pallas_call(
        functools.partial(kernel_renew, fs),
        grid_spec=pltpu.PrefetchScalarGridSpec(
            num_scalar_prefetch=1, grid=(GROUP,), in_specs=in_specs, out_specs=[block] * 4
        ),
        out_shape=[shape(master.shape, kind) for kind in kinds],
        input_output_aliases=aliases,
        compiler_params=PARAMS,
        cost_estimate=cost(0, rows * PIECE * GROUP * 28),
    )(info, grads[0], grads[1], master, momentum, average, *earlier)


def flip(count, bit):
    return [(i, i ^ bit) for i in range(count)]


def send(value, axis, count, bit):
    return lax.ppermute(value, axis, flip(count, bit))


def kernel_own(info, wide_a, wide_b, down, out_a, out_b, out_c):
    out_a[...] = wide_a[...].astype(bf16)
    out_b[...] = wide_b[...].astype(bf16)
    out_c[...] = down[...].astype(bf16)


def own_pieces(info, fs, rows, wide_master, down_master):
    def at(offset):
        return pl.BlockSpec((rows, PIECE), lambda step, info: (0, offset + info[3 + fs]))

    whole = pl.BlockSpec((rows, PIECE), lambda step, info: (0, 0))
    return pl.pallas_call(
        kernel_own,
        grid_spec=pltpu.PrefetchScalarGridSpec(
            num_scalar_prefetch=1,
            grid=(1,),
            in_specs=[
                at(0),
                at(GROUP),
                pl.BlockSpec((rows, PIECE), lambda step, info: (info[3 + fs] % 4, info[3 + fs] // 4)),
            ],
            out_specs=[whole] * 3,
        ),
        out_shape=[shape((rows, PIECE), bf16)] * 3,
        compiler_params=PARAMS,
    )(info, wide_master, wide_master, down_master)


def spread(piece, fs, dp):
    rows = piece.shape[0]
    near = jnp.concatenate([send(piece, "fsdp", fs, j) for j in range(1, fs)], axis=0)
    over_x = send(near, "dp", dp, 2)
    over_y = send(near, "dp", dp, 4)
    cut = (fs - 1) * rows // 32 * 16
    diag_a = send(over_x[:cut], "dp", dp, 4)
    diag_b = send(over_y[cut:], "dp", dp, 2)
    half = [near, over_x, over_y, diag_a, diag_b]
    return half + [send(value, "dp", dp, 1) for value in half]


def add(left, right):
    return (left.astype(f32) + right.astype(f32)).astype(bf16)


def pick(values, index, axis):
    return lax.dynamic_index_in_dim(values, index, axis, keepdims=False)


def reduce_pieces(mine, theirs, fs, dp, z, x, y):
    rows = mine.shape[1] // fs
    half = mine.shape[1] // 2
    total = add(mine, send(theirs, "dp", dp, 1)).reshape(2, 2, 2 * half, PIECE)
    upper, lower = total[:, :, :half], total[:, :, half:]
    upper = add(pick(upper, x, 1), send(pick(upper, 1 - x, 1), "dp", dp, 2))
    lower = add(pick(lower, y, 0), send(pick(lower, 1 - y, 0), "dp", dp, 4))
    upper = add(pick(upper, y, 0), send(pick(upper, 1 - y, 0), "dp", dp, 4))
    lower = add(pick(lower, x, 0), send(pick(lower, 1 - x, 0), "dp", dp, 2))
    own = jnp.concatenate([upper, lower], axis=0)
    bit = GROUP
    while bit < dp:
        own = add(own, send(own, "dp", dp, bit))
        bit *= 2
    own = own.reshape(fs, rows, PIECE)
    total = pick(own, z, 0).astype(f32)
    for j in range(1, fs):
        total = total + send(pick(own, z ^ j, 0), "fsdp", fs, j).astype(f32)
    return total.astype(bf16)


def share_pieces(piece, dp):
    rows = piece.shape[0]
    over_x = send(piece, "dp", dp, 2)
    over_y = send(piece, "dp", dp, 4)
    cut = rows // 32 * 16
    diag = jnp.concatenate([send(over_x[:cut], "dp", dp, 4), send(over_y[cut:], "dp", dp, 2)], axis=0)
    side = jnp.stack([piece, over_x, over_y, diag])
    return side, send(side, "dp", dp, 1)


def merge_stats(group):
    top = functools.reduce(jnp.maximum, [top for top, _ in group])
    return top, sum(mass * jnp.exp(old - top) for old, mass in group)


def exchange_stats(stats, fs, dp):
    def one_round(stats, hops):
        arrived = [stats] + [send(stats, axis, count, bit) for axis, count, bit in hops]
        top, mass = merge_stats([(a[0:1], a[1:2]) for a in arrived])
        return jnp.concatenate([top, mass], axis=0)

    stats = one_round(stats, [("dp", dp, 1)])
    stats = one_round(stats, [("fsdp", fs, j) for j in range(1, fs)])
    stats = one_round(stats, [("dp", dp, j) for j in range(2, dp, 2)])
    return stats


def body(
    fs,
    dp,
    hidden_in,
    lengths,
    images,
    labels,
    wide_master,
    down_master,
    vector_master,
    wide_momentum,
    down_momentum,
    vector_momentum,
    wide_average,
    down_average,
    vector_average,
):
    tokens, width = hidden_in.shape
    captions = lengths.shape[0]
    rows = wide_master.shape[0]
    hidden = wide_master.shape[1] - 4 * width
    rank, z = lax.axis_index("dp"), lax.axis_index("fsdp")
    core, x, y = rank % 2, rank // 2 % 2, rank // 4 % 2
    member = [rank ^ k for k in range(GROUP)]
    spots = [(m % 2) * 4 + (m // 4 % 2) * 2 + (m // 2 % 2) for m in member]
    info = jnp.stack([z, core, rank * fs + z] + [z ^ j for j in range(fs)] + spots).astype(jnp.int32)

    tags = jnp.stack([labels // 128, labels % 128], axis=1).astype(bf16)
    marked = jnp.concatenate([images, jnp.pad(tags, ((0, 0), (0, 126)))], axis=1)
    marked = lax.all_gather(marked, ("dp", "fsdp"), axis=0, tiled=True)
    total = marked.shape[0]
    all_labels = (marked[:, width].astype(jnp.int32) * 128 + marked[:, width + 1].astype(jnp.int32))[None, :]

    own_vec = vector_master.astype(bf16)
    shards = [own_vec] + [send(own_vec, "fsdp", fs, j) for j in range(1, fs)]
    slots = lax.broadcasted_iota(jnp.int32, (1, fs, 1), 1)
    vec = sum(jnp.where(slots == (z ^ j), shards[j].astype(f32)[:, None, :], 0.0) for j in range(fs))
    vec = jnp.pad(vec.reshape(12, width), ((0, 4), (0, 0)))
    up_bias = vec[8:12].reshape(1, hidden)

    place = jnp.arange(SEQ)
    keep = (place[None, :] < lengths[:, None]).astype(f32).reshape(tokens)
    valid, keep = keep[None, :], keep[:, None]
    lens = lengths.astype(f32)[:, None]

    piece_a, piece_b, piece_c = own_pieces(info, fs, rows, wide_master, down_master)
    parts_a = spread(piece_a, fs, dp)
    parts_b = spread(piece_b, fs, dp)
    parts_c = spread(piece_c, fs, dp)
    n_copies = GROUP * fs * 2
    scratch = [
        pltpu.SemaphoreType.DMA((n_copies,)),
        pltpu.SemaphoreType.DMA,
        pltpu.SemaphoreType.DMA,
    ]

    qkv, ctx, h, second, w_att = pl.pallas_call(
        functools.partial(kernel_attention, fs, rows),
        in_specs=[SMEM, VMEM, VMEM, VMEM, ANY] + [ANY] * 10,
        out_specs=[VMEM] * 4 + [ANY],
        out_shape=[
            shape((tokens, 3 * width), bf16),
            shape((tokens, width), bf16),
            shape((tokens, width), f32),
            shape((tokens, width), bf16),
            shape((width, 4 * width), bf16),
        ],
        scratch_shapes=[pltpu.VMEM((width, 4 * width), bf16), pltpu.VMEM((rows, 4 * width), f32)] + scratch,
        compiler_params=PARAMS,
        cost_estimate=cost(2 * tokens * width * width * 5, 16e6),
    )(info, hidden_in, valid, vec, wide_master, *parts_a)

    u, g, w_up = pl.pallas_call(
        functools.partial(kernel_up, fs, rows),
        in_specs=[SMEM, VMEM, VMEM, ANY] + [ANY] * 10,
        out_specs=[VMEM] * 2 + [ANY],
        out_shape=[
            shape((tokens, hidden), f32),
            shape((tokens, hidden), bf16),
            shape((width, hidden), bf16),
        ],
        scratch_shapes=[pltpu.VMEM((width, hidden), bf16), pltpu.VMEM((rows, hidden), f32)] + scratch,
        compiler_params=PARAMS,
        cost_estimate=cost(2 * tokens * width * hidden, 20e6),
    )(info, second, up_bias, wide_master, *parts_b)

    block_out, pooled, inv, logits, stats, w_down = pl.pallas_call(
        functools.partial(kernel_down, fs, rows),
        in_specs=[SMEM] + [VMEM] * 6 + [ANY] + [ANY] * 10,
        out_specs=[VMEM] * 5 + [ANY],
        out_shape=[
            shape((tokens, width), bf16),
            shape((captions, width), f32),
            shape((captions, 1), f32),
            shape((captions, total), f32),
            shape((2, total), f32),
            shape((hidden, width), bf16),
        ],
        scratch_shapes=[pltpu.VMEM((hidden, width), bf16), pltpu.VMEM(down_master.shape, f32)] + scratch,
        compiler_params=PARAMS,
        cost_estimate=cost(2 * tokens * width * hidden, 20e6),
    )(info, g, h, vec, lens, keep, marked, down_master, *parts_c)

    stats = exchange_stats(stats, fs, dp)

    halves = [shape((4, width, PIECE), bf16)] * 2
    dpl, dy, down_bias_grad, mine_c, theirs_c = pl.pallas_call(
        functools.partial(kernel_loss, rows),
        in_specs=[SMEM] + [VMEM] * 9,
        out_specs=[VMEM] * 5,
        out_shape=[shape((captions, width), f32), shape((tokens, width), bf16), shape((1, width), f32)] + halves,
        compiler_params=PARAMS,
        cost_estimate=cost(2 * tokens * width * hidden, 10e6),
    )(info, logits, stats, all_labels, marked, pooled, inv, lens, keep, g)
    grad_c = share_pieces(reduce_pieces(mine_c, theirs_c, fs, dp, z, x, y), dp)

    du, up_bias_grad, mine_b, theirs_b = pl.pallas_call(
        kernel_up_back,
        in_specs=[SMEM] + [VMEM] * 4,
        out_specs=[VMEM] * 4,
        out_shape=[shape((tokens, hidden), bf16), shape((1, hidden), f32)] + halves,
        compiler_params=PARAMS,
        cost_estimate=cost(4 * tokens * width * hidden, 20e6),
    )(info, dy, u, second, w_down)
    grad_b = share_pieces(reduce_pieces(mine_b, theirs_b, fs, dp, z, x, y), dp)

    dh, dqkv, some_grads, mine_a, theirs_a = pl.pallas_call(
        kernel_attention_back,
        in_specs=[SMEM] + [VMEM] * 11,
        out_specs=[VMEM] * 5,
        out_shape=[
            shape((tokens, width), f32),
            shape((tokens, 3 * width), bf16),
            shape((8, width), f32),
        ]
        + halves,
        compiler_params=PARAMS,
        cost_estimate=cost(2 * tokens * width * width * 12, 20e6),
    )(info, dpl, keep, du, h, hidden_in, qkv, ctx, valid, vec, w_up, w_att)
    grad_a = share_pieces(reduce_pieces(mine_a, theirs_a, fs, dp, z, x, y), dp)

    input_grad, norm_grads = pl.pallas_call(
        kernel_input_back,
        in_specs=[VMEM] * 5,
        out_specs=[VMEM] * 2,
        out_shape=[shape((tokens, width), f32), shape((2, width), f32)],
        compiler_params=PARAMS,
        cost_estimate=cost(2 * tokens * width * width * 3, 10e6),
    )(dqkv, dh, hidden_in, vec, w_att)

    vec_grad = jnp.concatenate(
        [norm_grads, some_grads[:5], down_bias_grad, up_bias_grad.reshape(4, width)], axis=0
    ).astype(bf16)
    bit = 1
    while bit < dp:
        vec_grad = add(vec_grad, send(vec_grad, "dp", dp, bit))
        bit *= 2
    vec_parts = vec_grad.reshape(12, fs, width // fs)
    vec_sum = pick(vec_parts, z, 1).astype(f32)
    for j in range(1, fs):
        vec_sum = vec_sum + send(pick(vec_parts, z ^ j, 1), "fsdp", fs, j).astype(f32)

    down_state = renew(info, fs, rows, grad_c, down_master, down_momentum, down_average, None, ())
    wide_state = renew(info, fs, rows, grad_b, wide_master, wide_momentum, wide_average, GROUP, ())
    wide_state = renew(info, fs, rows, grad_a, wide_master, wide_momentum, wide_average, 0, tuple(wide_state))
    vector_state = renew_state(vector_master, vector_momentum, vector_average, vec_sum)
    return (
        block_out,
        input_grad,
        wide_state[0],
        down_state[0],
        vector_state[0],
        wide_state[1],
        down_state[1],
        vector_state[1],
        wide_state[2],
        down_state[2],
        vector_state[2],
        wide_state[3],
        down_state[3],
        vector_state[3],
    )


def solution(mesh):
    tokens = P(("dp", "fsdp"), None)
    each = P(("dp", "fsdp"))
    by_row = P("fsdp", None)
    by_col = P(None, "fsdp")
    states = (by_row, by_row, by_col)
    return jax.shard_map(
        functools.partial(body, mesh.shape["fsdp"], mesh.shape["dp"]),
        mesh=mesh,
        in_specs=(tokens, each, tokens, each) + states * 3,
        out_specs=(tokens, tokens) + states * 4,
        check_vma=False,
    )
```

```python
import functools

import jax
import jax.numpy as jnp
from jax import lax
from jax.experimental import pallas as pl
from jax.experimental.pallas import tpu as pltpu
from jax.sharding import PartitionSpec as P

HEADS = 12
SEQ = 16
PIECE = 384
GROUP = 8
PICTURE_TAGS = 16

norm_epsilon = 1e-06
masked_score = -1e30
learn_rate = 0.02
momentum_decay = 0.5
average_decay = 0.5
gelu_scale = 0.7978845608028654
gelu_cube = 0.044715

f32 = jnp.float32
bf16 = jnp.bfloat16
VMEM = pl.BlockSpec(memory_space=pltpu.VMEM)
SMEM = pl.BlockSpec(memory_space=pltpu.SMEM)
ANY = pl.BlockSpec(memory_space=pl.ANY)
HBM = pl.BlockSpec(memory_space=pltpu.HBM)
PARAMS = pltpu.CompilerParams(vmem_limit_bytes=32 * 1024 * 1024)


def dot(left, right):
    return lax.dot_general(left, right, (((1,), (0,)), ((), ())), preferred_element_type=f32)


def dot_nt(left, right):
    return lax.dot_general(left, right, (((1,), (1,)), ((), ())), preferred_element_type=f32)


def dot_tn(left, right):
    return lax.dot_general(left, right, (((0,), (0,)), ((), ())), preferred_element_type=f32)


def shape(dims, kind):
    return jax.ShapeDtypeStruct(dims, kind)


class Order:
    def __init__(self):
        self.last = ()

    def __call__(self, kernel, in_specs, out_shape, args, after=(), out_specs=None, scratch=(), flops=0, moved=0, limit=16):
        after = [*self.last, *after]
        count, skip = len(in_specs), len(after)

        def run(*refs):
            kernel(*refs[:count], *refs[count + skip :])

        outs = pl.pallas_call(
            run,
            in_specs=list(in_specs) + [ANY] * skip,
            out_specs=out_specs or [VMEM] * len(out_shape),
            out_shape=out_shape,
            scratch_shapes=scratch,
            compiler_params=pltpu.CompilerParams(vmem_limit_bytes=limit * 1024 * 1024),
            cost_estimate=cost(10**11, 1),
        )(*args, *after)
        self.last = (min(outs, key=lambda value: value.size),)
        return outs


def cost(flops, moved):
    return pl.CostEstimate(flops=int(flops), bytes_accessed=int(moved), transcendentals=0)


def norm_parts(values):
    centre = values - jnp.mean(values, axis=-1, keepdims=True)
    inv = lax.rsqrt(jnp.mean(centre * centre, axis=-1, keepdims=True) + norm_epsilon)
    return centre * inv, inv


def norm_back(grad, scaled, inv, gain):
    d_scaled = grad * gain
    first = jnp.mean(d_scaled, axis=-1, keepdims=True)
    second = jnp.mean(d_scaled * scaled, axis=-1, keepdims=True)
    return inv * (d_scaled - first - scaled * second)


def piece_copies(info, fs, rows, sides, target, sems, is_down):
    copies = []
    for k in range(GROUP):
        for j in range(1, fs):
            shard = info[3 + j]
            place = info[3 + fs + k]
            row = shard * rows
            if is_down:
                row = row * 4 + (place % 4) * rows
                col = (place // 4) * PIECE
            else:
                col = place * PIECE
            first = ((k // 2) * (fs - 1) + j - 1) * rows
            copies.append(
                pltpu.make_async_copy(
                    sides[k % 2].at[pl.ds(first, rows), :],
                    target.at[pl.ds(pl.multiple_of(row, 16), rows), pl.ds(pl.multiple_of(col, 128), PIECE)],
                    sems.at[len(copies)],
                )
            )
    return copies


def picture_copies(info, fs, captions, sides, images, tags, image_sem, tag_sem):
    block = PICTURE_TAGS
    members = sides[0].shape[0] // (block + 2 * captions) // fs
    rank, z = info[info.shape[0] - 3], info[0]
    for side in range(2):
        for j in range(fs):
            for m in range(members):
                device = (rank ^ (2 * m + side)) * fs + (z ^ j)
                first = (j * members + m) * (block + 2 * captions)
                to = pl.ds(pl.multiple_of(device * captions, 16), captions)
                for half in range(2):
                    pltpu.make_async_copy(
                        sides[side].at[pl.ds(first + half * captions, captions), :],
                        images.at[to, pl.ds(half * PIECE, PIECE)],
                        image_sem,
                    ).start()
                pltpu.make_async_copy(
                    sides[side].at[pl.ds(first + 2 * captions, block), pl.ds(0, 128)],
                    tags.at[pl.ds(pl.multiple_of(device * block, 16), block), :],
                    tag_sem,
                ).start()


def attend_forward(queries, keys, values, mask, half_low, half_high):
    both_q = jnp.concatenate([queries * half_low, queries * half_high], axis=0)
    scores = jnp.where(mask, dot_nt(both_q, keys) * 0.125, masked_score)
    top = jnp.max(scores, axis=-1, keepdims=True)
    raised = jnp.exp(scores - top)
    probs = raised / jnp.sum(raised, axis=-1, keepdims=True)
    return both_q, probs


def lane_halves():
    lane = lax.broadcasted_iota(jnp.int32, (1, 128), 1)
    low = (lane < 64).astype(f32)
    return low, low.astype(bf16), (1.0 - low).astype(bf16)


def caption_mask(valid_row):
    row = lax.broadcasted_iota(jnp.int32, (256, 128), 0)
    col = lax.broadcasted_iota(jnp.int32, (256, 128), 1)
    same = ((row & 127) // SEQ) == (col // SEQ)
    return same & (valid_row > 0.0)


def kernel_qkv(fs, rows, info, hid, vec, own, near, far, qkv_ref, w, w_out, sems):
    width = hid.shape[1]
    copies = piece_copies(info, fs, rows, (near, far), w, sems, False)
    for copy in copies:
        copy.start()
    vecs = vec[...]
    scaled, _ = norm_parts(hid[...].astype(f32))
    normed = (scaled * vecs[0:1] + vecs[1:2]).astype(bf16)
    w[pl.ds(pl.multiple_of(info[0] * rows, 16), rows), :] = own[...]
    for copy in copies:
        copy.wait()
    for part in range(3):
        cols = pl.ds(part * width, width)
        value = dot(normed, w[:, cols])
        if part == 0:
            value = value + vecs[2:3]
        if part == 2:
            value = value + vecs[3:4]
        qkv_ref[:, cols] = value.astype(bf16)
    w_out[...] = w[:, 3 * width :]


def kernel_attention(hid, valid, vec, qkv, w, ctx_ref, h_ref, second_ref):
    tokens, width = hid.shape
    low_f, low, high = lane_halves()

    def block(index, carry):
        at = pl.ds(pl.multiple_of(index * 128, 128), 128)
        mask = caption_mask(valid[:, at])
        for pair in range(width // 128):
            here = pair * 128
            queries = qkv[at, here : here + 128]
            keys = qkv[at, width + here : width + here + 128]
            values = qkv[at, 2 * width + here : 2 * width + here + 128]
            _, probs = attend_forward(queries, keys, values, mask, low, high)
            context = dot(probs.astype(bf16), values)
            ctx_ref[at, here : here + 128] = jnp.where(low_f > 0.0, context[:128], context[128:]).astype(bf16)
        return carry

    lax.fori_loop(0, tokens // 128, block, 0)
    residual = hid[...].astype(f32) + (dot(ctx_ref[...], w[...]) + vec[4:5, :])
    h_ref[...] = residual
    scaled, _ = norm_parts(residual)
    second_ref[...] = (scaled * vec[5:6, :] + vec[6:7, :]).astype(bf16)


def kernel_up(fs, rows, info, second, bias, own, near, far, u_ref, g_ref, w, sems):
    width, hidden = w.shape
    copies = piece_copies(info, fs, rows, (near, far), w, sems, False)
    for copy in copies:
        copy.start()
    w[pl.ds(pl.multiple_of(info[0] * rows, 16), rows), :] = own[...]
    for copy in copies:
        copy.wait()

    def block(index, carry):
        cols = pl.ds(pl.multiple_of(index * 512, 128), 512)
        value = dot(second[...], w[:, cols]) + bias[:, cols]
        u_ref[:, cols] = value
        inner = jnp.tanh(gelu_scale * (value + gelu_cube * value * value * value))
        g_ref[:, cols] = (0.5 * value * (1.0 + inner)).astype(bf16)
        return carry

    lax.fori_loop(0, hidden // 512, block, 0)


def kernel_down(fs, rows, info, g, h, vec, lens, keep, own, near, far, near_images, far_images, *rest):
    out_ref, pooled_ref, inv_ref, logit_ref, stat_ref, images, tags, w, sems, image_sem, tag_sem = rest
    tokens, width = h.shape
    captions = tokens // SEQ
    copies = piece_copies(info, fs, rows, (near, far), w, sems, True)
    picture_copies(info, fs, captions, (near_images, far_images), images, tags, image_sem, tag_sem)
    for copy in copies:
        copy.start()
    w[pl.ds(pl.multiple_of(info[0] * 4 * rows, 16), 4 * rows), :] = own[...]
    for copy in copies:
        copy.wait()
    block_rows = h[...] + (dot(g[...], w[...]) + vec[7:8, :])
    out_ref[...] = block_rows.astype(bf16)
    pooled = jnp.sum((block_rows * keep[...]).reshape(captions, SEQ, width), axis=1) / lens[...]
    inv = lax.rsqrt(jnp.sum(pooled * pooled, axis=-1, keepdims=True) + norm_epsilon)
    pooled_ref[...] = pooled
    inv_ref[...] = inv
    texts = (pooled * inv).astype(bf16)
    pltpu.make_async_copy(images, images, image_sem).wait()
    pltpu.make_async_copy(tags, tags, tag_sem).wait()
    logits = dot_nt(texts, images[...])
    logit_ref[...] = logits
    top = jnp.max(logits, axis=0, keepdims=True)
    stat_ref[0:1, :] = top
    stat_ref[1:2, :] = jnp.sum(jnp.exp(logits - top), axis=0, keepdims=True)


def put(info, half, place, value, mine, theirs):
    rows = value.shape[0]

    @pl.when(info[1] == half)
    def _():
        mine[place[0], pl.ds(place[1], rows), :] = value

    @pl.when(info[1] != half)
    def _():
        theirs[place[0], pl.ds(place[1], rows), :] = value


def kernel_loss(rows, info, logits, stats, labels, images, pooled, inv, lens, keep, g, dpl_ref, dy_ref, bias_ref, mine, theirs):
    captions, width = pooled.shape
    tokens, hidden = g.shape
    lse = stats[0:1, :] + jnp.log(stats[1:2, :])
    number = lax.broadcasted_iota(jnp.int32, logits.shape, 0) + info[2] * captions
    onehot = (labels[...] == number).astype(f32)
    slopes = (jnp.exp(logits[...] - lse) - onehot).astype(bf16)
    text_grad = dot(slopes, images[...])
    pool, inv_v = pooled[...], inv[...]
    d_pooled = inv_v * text_grad - inv_v**3 * pool * jnp.sum(pool * text_grad, axis=-1, keepdims=True)
    dpl = d_pooled / lens[...]
    dpl_ref[...] = dpl
    d_out = jnp.broadcast_to(dpl[:, None, :], (captions, SEQ, width)).reshape(tokens, width) * keep[...]
    dy = d_out.astype(bf16)
    dy_ref[...] = dy
    bias_ref[...] = jnp.sum(dy.astype(f32), axis=0, keepdims=True)
    for part in range(hidden // width):
        grad = dot_tn(g[:, part * width : (part + 1) * width], dy).astype(bf16)
        for sub in range(width // rows):
            first = part * width + sub * rows
            shard, quarter = first // (4 * rows), (first % (4 * rows)) // rows
            for half in range(2):
                value = grad[sub * rows : (sub + 1) * rows, half * PIECE : (half + 1) * PIECE]
                put(info, half, (quarter, shard * rows), value, mine, theirs)


def kernel_gelu_back(dy, u, w_down, du_ref, bias_ref):
    tokens, hidden = u.shape
    for part in range(hidden // 768):
        cols = slice(part * 768, (part + 1) * 768)
        d_gelu = dot_nt(dy[...], w_down[cols, :])
        value = u[:, cols]
        square = value * value
        inner = jnp.tanh(gelu_scale * (value + gelu_cube * value * square))
        slope = 0.5 * (1.0 + inner) + (0.5 * gelu_scale) * value * (1.0 - inner * inner) * (1.0 + (3.0 * gelu_cube) * square)
        du = (d_gelu * slope).astype(bf16)
        du_ref[:, cols] = du
        bias_ref[:, cols] = jnp.sum(du.astype(f32), axis=0, keepdims=True)


def kernel_up_grad(info, du, second, mine, theirs):
    turned = second[...].T
    for place in range(du.shape[1] // PIECE):
        grad = dot(turned, du[:, place * PIECE : (place + 1) * PIECE]).astype(bf16)
        put(info, place // 4, (place % 4, 0), grad, mine, theirs)


def kernel_mid_back(dpl, keep, du, h, vec, w_up, w_out, dh_ref, da_ref, dctx_ref, grads_ref):
    tokens, width = h.shape
    captions = tokens // SEQ
    d_second = dot_nt(du[...], w_up[...])
    scaled, inv = norm_parts(h[...])
    d_out = jnp.broadcast_to(dpl[...][:, None, :], (captions, SEQ, width)).reshape(tokens, width) * keep[...]
    dh = d_out + norm_back(d_second, scaled, inv, vec[5:6, :])
    dh_ref[...] = dh
    da = dh.astype(bf16)
    da_ref[...] = da
    grads_ref[0:1, :] = jnp.sum(da.astype(f32), axis=0, keepdims=True)
    grads_ref[1:2, :] = jnp.sum(d_second * scaled, axis=0, keepdims=True)
    grads_ref[2:3, :] = jnp.sum(d_second, axis=0, keepdims=True)
    dctx_ref[...] = dot_nt(da, w_out[...]).astype(bf16)


def kernel_attention_back(dctx, qkv, valid, dqkv_ref, grads_ref):
    tokens, width = dctx.shape
    low_f, low, high = lane_halves()

    def block(index, carry):
        at = pl.ds(pl.multiple_of(index * 128, 128), 128)
        mask = caption_mask(valid[:, at])
        for pair in range(width // 128):
            here = pair * 128
            queries = qkv[at, here : here + 128]
            keys = qkv[at, width + here : width + here + 128]
            values = qkv[at, 2 * width + here : 2 * width + here + 128]
            both_q, probs = attend_forward(queries, keys, values, mask, low, high)
            d_context = dctx[at, here : here + 128]
            both_d = jnp.concatenate([d_context * low, d_context * high], axis=0)
            d_probs = dot_nt(both_d, values)
            weighted = probs * d_probs
            d_scores = (weighted - probs * jnp.sum(weighted, axis=-1, keepdims=True)).astype(bf16)
            d_both = dot(d_scores, keys) * 0.125
            d_queries = jnp.where(low_f > 0.0, d_both[:128], d_both[128:])
            d_keys = dot_tn(d_scores, both_q) * 0.125
            d_values = dot_tn(probs.astype(bf16), both_d)
            dqkv_ref[at, here : here + 128] = d_queries.astype(bf16)
            dqkv_ref[at, width + here : width + here + 128] = d_keys.astype(bf16)
            dqkv_ref[at, 2 * width + here : 2 * width + here + 128] = d_values.astype(bf16)
        return carry

    lax.fori_loop(0, tokens // 128, block, 0)
    grads_ref[0:1, :] = jnp.sum(dqkv_ref[:, :width].astype(f32), axis=0, keepdims=True)
    grads_ref[1:2, :] = jnp.sum(dqkv_ref[:, 2 * width :].astype(f32), axis=0, keepdims=True)


def kernel_attention_grad(info, hid, vec, ctx, dqkv, da, mine, theirs):
    scaled, _ = norm_parts(hid[...].astype(f32))
    turned = (scaled * vec[0:1, :] + vec[1:2, :]).astype(bf16).T
    for place in range(6):
        grad = dot(turned, dqkv[:, place * PIECE : (place + 1) * PIECE]).astype(bf16)
        put(info, place // 4, (place % 4, 0), grad, mine, theirs)
    turned = ctx[...].T
    for place in range(6, 8):
        at = (place - 6) * PIECE
        grad = dot(turned, da[:, at : at + PIECE]).astype(bf16)
        put(info, place // 4, (place % 4, 0), grad, mine, theirs)


def kernel_input_back(dqkv, dh, hid, vec, w_att, out_ref, grads_ref):
    width = hid.shape[1]
    d_normed = dot_nt(dqkv[...], w_att[:, : 3 * width])
    scaled, inv = norm_parts(hid[...].astype(f32))
    out_ref[...] = dh[...] + norm_back(d_normed, scaled, inv, vec[0:1, :])
    grads_ref[0:1, :] = jnp.sum(d_normed * scaled, axis=0, keepdims=True)
    grads_ref[1:2, :] = jnp.sum(d_normed, axis=0, keepdims=True)


def renew_state(master, momentum, average, gradient):
    momentum_new = momentum_decay * momentum + gradient
    master_new = master - learn_rate * (gradient + momentum_decay * momentum_new)
    average_new = average_decay * average + (1.0 - average_decay) * master_new
    return (master_new, momentum_new, average_new, master_new.astype(bf16))


def kernel_renew(fs, column, skip, info, near, far, *refs):
    states, outs, (buf, new_f, new_h, in_sem, out_sem) = refs[:3], refs[3 + skip : 7 + skip], refs[7 + skip :]
    rows = buf.shape[2]

    def at(k):
        spot = info[3 + fs + k]
        if column is None:
            row, col = pl.multiple_of((spot % 4) * rows, 16), (spot // 4) * PIECE
        else:
            row, col = 0, (column + spot) * PIECE
        return pl.ds(row, rows), pl.ds(pl.multiple_of(col, 128), PIECE)

    def read(k, i):
        return pltpu.make_async_copy(states[i].at[at(k)], buf.at[k, i], in_sem.at[k, i])

    def write(k, i):
        source = new_h.at[k] if i == 3 else new_f.at[k, i]
        return pltpu.make_async_copy(source, outs[i].at[at(k)], out_sem.at[k, i])

    for k in range(GROUP):
        for i in range(3):
            read(k, i).start()
    for k in range(GROUP):
        for i in range(3):
            read(k, i).wait()
        grad = (far if k % 2 else near)[k // 2 * rows : (k // 2 + 1) * rows, :].astype(f32)
        *new, half = renew_state(buf[k, 0], buf[k, 1], buf[k, 2], grad)
        for i in range(3):
            new_f[k, i] = new[i]
        new_h[k] = half
        for i in range(4):
            write(k, i).start()
    for k in range(GROUP):
        for i in range(4):
            write(k, i).wait()


def renew(order, info, fs, rows, grads, master, momentum, average, column, earlier=()):
    skip = len(earlier) + len(order.last)
    outs = pl.pallas_call(
        functools.partial(kernel_renew, fs, column, skip),
        in_specs=[SMEM] + [VMEM] * 2 + [HBM] * 3 + [HBM] * len(earlier) + [ANY] * len(order.last),
        out_specs=[HBM] * 4,
        out_shape=[shape(master.shape, kind) for kind in (f32, f32, f32, bf16)],
        scratch_shapes=[
            pltpu.VMEM((GROUP, 3, rows, PIECE), f32),
            pltpu.VMEM((GROUP, 3, rows, PIECE), f32),
            pltpu.VMEM((GROUP, rows, PIECE), bf16),
            pltpu.SemaphoreType.DMA((GROUP, 3)),
            pltpu.SemaphoreType.DMA((GROUP, 4)),
        ],
        input_output_aliases={6 + i: i for i in range(len(earlier))},
        compiler_params=pltpu.CompilerParams(vmem_limit_bytes=60 * 1024 * 1024),
        cost_estimate=cost(10**11, 1),
    )(info, *grads, master, momentum, average, *earlier, *order.last)
    order.last = (outs[3],)
    return outs


def flip(count, bit):
    return [(i, i ^ bit) for i in range(count)]


def send(value, axis, count, bit):
    return lax.ppermute(value, axis, flip(count, bit))


def kernel_pack(rows, *refs):
    *refs, near = refs
    for j, ref in enumerate(refs):
        near[j * rows : (j + 1) * rows, :] = ref[:rows, :]


def kernel_cast(wide, down, out_a, out_b, out_c):
    cols = out_a.shape[1]
    out_a[...] = wide[:, :cols].astype(bf16)
    out_b[...] = wide[:, cols:].astype(bf16)
    out_c[...] = down[...].astype(bf16)


def kernel_join(*refs):
    *parts, out = refs
    row = 0
    for part in parts:
        out[row : row + part.shape[0], :] = part[...]
        row += part.shape[0]


def kernel_pack_first(fs, rows, info, own, *refs):
    *refs, near, vec, bias, wide = refs
    width = vec.shape[1]
    wide[...] = jnp.zeros_like(wide)
    total = jnp.zeros(vec.shape, f32)
    for j, ref in enumerate([own, *refs]):
        if j:
            near[(j - 1) * rows : j * rows, :] = ref[:rows, :]
        wide[:, :PIECE] = ref[rows:, :].astype(f32)
        total = total + pltpu.roll(wide[...], info[3 + j] * (width // fs), 1)
    vec[...] = total
    for row in range(4):
        bias[:, row * width : (row + 1) * width] = total[8 + row : 9 + row, :]


def kernel_sorted(rows, places, *refs):
    *parts, out = refs
    for part, of_part in zip(parts, places):
        for i, place in enumerate(of_part):
            out[place * rows : (place + 1) * rows, :] = part[i * rows : (i + 1) * rows, :]


def kernel_halves(over_x, over_y, first, second):
    cut = first.shape[0]
    first[...] = over_x[:cut, :]
    second[...] = over_y[cut:, :]


def kernel_copy(value, out):
    out[...] = value[...]


def total_of(left, right):
    return (left.astype(f32) + right.astype(f32)).astype(bf16)


def kernel_add_core(fs, info, mine, came, *refs):
    *vecs, to_x, to_y, keep_x, keep_y = refs
    rows, step = mine.shape[1] // fs, to_x.shape[1] * 2 // fs
    x, y = info[info.shape[0] - 2], info[info.shape[0] - 1]
    for other in range(2):
        for ref, spot, first in (
            (to_x, other * 2 + (1 - x), 0),
            (to_y, (1 - y) * 2 + other, fs // 2),
            (keep_x, other * 2 + x, 0),
            (keep_y, y * 2 + other, fs // 2),
        ):
            for shard in range(fs // 2):
                at = pl.ds((first + shard) * rows, rows)
                ref[other, pl.ds(shard * step, rows), :] = total_of(mine[spot, at, :], came[spot, at, :])
                if vecs:
                    at = pl.ds((first + shard) * 16, 16)
                    ref[other, pl.ds(shard * step + rows, 16), :] = total_of(vecs[0][at, :], vecs[1][at, :])


def kernel_add_first(info, keep_x, keep_y, came_x, came_y, to_y, to_x, left_x, left_y):
    x, y = info[info.shape[0] - 2], info[info.shape[0] - 1]
    to_y[...] = total_of(keep_x[1 - y], came_x[1 - y])
    to_x[...] = total_of(keep_y[1 - x], came_y[1 - x])
    left_x[...] = total_of(keep_x[y], came_x[y])
    left_y[...] = total_of(keep_y[x], came_y[x])


def kernel_add_second(fs, rows, info, left_x, left_y, came_y, came_x, *refs):
    *outs, own = refs
    half = left_x.shape[0]
    own[:half, :] = total_of(left_x[...], came_y[...])
    own[half:, :] = total_of(left_y[...], came_x[...])
    for j, ref in enumerate(outs):
        ref[...] = own[pl.ds(pl.multiple_of(info[3 + j] * rows, 16), rows), :]


def kernel_add_second_half(fs, rows, info, left_x, left_y, came_y, came_x, keep, give, own):
    half = left_x.shape[0]
    own[:half, :] = total_of(left_x[...], came_y[...])
    own[half:, :] = total_of(left_y[...], came_x[...])
    for j in range(fs):
        ref = give if j % 2 else keep
        block = own[pl.ds(pl.multiple_of(info[3 + j] * rows, 16), rows), :]
        ref[j // 2 * rows : (j // 2 + 1) * rows, :] = block


def kernel_fold(rows, keep, came, left, give):
    for j in range(keep.shape[0] // rows):
        ref = give if j % 2 else left
        at = slice(j * rows, (j + 1) * rows)
        ref[j // 2 * rows : (j // 2 + 1) * rows, :] = total_of(keep[at, :], came[at, :])


def kernel_add_z(fs, *refs):
    parts, (out, *vectors) = refs[:fs], refs[fs:]
    rows = out.shape[0]
    out[...] = sum(part[:rows, :].astype(f32) for part in parts).astype(bf16)
    for ref in vectors:
        ref[...] = sum(part[rows:, :].astype(f32) for part in parts)


class Reduction:
    def __init__(self, order, info, fs, dp, mine, theirs):
        self.order, self.info, self.fs, self.dp = order, info, fs, dp
        self.width = mine.shape[1]
        self.rows = self.width // fs
        mine, theirs = self.beyond(mine), self.beyond(theirs)
        self.mine = [mine, send(theirs, "dp", dp, 1)]

    def beyond(self, value):
        bit = GROUP
        while bit < self.dp:
            value = total_of(value, send(value, "dp", self.dp, bit))
            bit *= 2
        return value

    def ride(self, vectors):
        self.mine += [vectors, send(vectors, "dp", self.dp, 1)]

    def core(self):
        self.rows = self.width // self.fs + (16 if len(self.mine) > 2 else 0)
        self.width = self.rows * self.fs
        to_x, to_y, *self.keep = self.order(
            functools.partial(kernel_add_core, self.fs),
            [SMEM] + [VMEM] * len(self.mine),
            [shape((2, self.width // 2, PIECE), bf16)] * 4,
            (self.info, *self.mine),
        )
        self.came = send(to_x, "dp", self.dp, 2), send(to_y, "dp", self.dp, 4)

    def first(self):
        half = self.width // 2
        to_y, to_x, *self.keep = self.order(
            kernel_add_first,
            [SMEM] + [VMEM] * 4,
            [shape((half, PIECE), bf16)] * 4,
            (self.info, *self.keep, *self.came),
            moved=3e6,
        )
        self.came = send(to_y, "dp", self.dp, 4), send(to_x, "dp", self.dp, 2)

    def second(self):
        parts = self.order(
            functools.partial(kernel_add_second, self.fs, self.rows),
            [SMEM] + [VMEM] * 4,
            [shape((self.rows, PIECE), bf16)] * self.fs,
            (self.info, *self.keep, *self.came),
            scratch=[pltpu.VMEM((self.width, PIECE), bf16)],
            moved=2e6,
        )
        self.came = [parts[0]] + [send(parts[j], "fsdp", self.fs, j) for j in range(1, self.fs)]

    def second_half(self):
        self.bit, count = 1, self.fs // 2
        keep, give = self.order(
            functools.partial(kernel_add_second_half, self.fs, self.rows),
            [SMEM] + [VMEM] * 4,
            [shape((count * self.rows, PIECE), bf16)] * 2,
            (self.info, *self.keep, *self.came),
            scratch=[pltpu.VMEM((self.width, PIECE), bf16)],
        )
        self.came = [keep, send(give, "fsdp", self.fs, 1)]

    def fold(self):
        while 2 * self.bit < self.fs:
            self.bit *= 2
            count = self.fs // self.bit // 2
            keep, give = self.order(
                functools.partial(kernel_fold, self.rows),
                [VMEM] * 2,
                [shape((count * self.rows, PIECE), bf16)] * 2,
                self.came,
            )
            self.came = [keep, send(give, "fsdp", self.fs, self.bit)]

    def line(self, grad_rows):
        count = len(self.came)
        extra = [shape((self.rows - grad_rows, PIECE), f32)] if self.rows > grad_rows else []
        piece, *self.vectors = self.order(
            functools.partial(kernel_add_z, count), [VMEM] * count, [shape((grad_rows, PIECE), bf16)] + extra, self.came
        )
        self.rows, self.piece = grad_rows, piece

    def share_first(self):
        self.came = [self.piece, send(self.piece, "dp", self.dp, 2)]

    def share_second(self):
        (pair,) = self.order(kernel_join, [VMEM] * 2, [shape((2 * self.rows, PIECE), bf16)], self.came)
        self.came = [pair, send(pair, "dp", self.dp, 4)]

    def share_all(self):
        self.came = [self.piece] + [send(self.piece, "dp", self.dp, k) for k in (2, 4, 6)]

    def share(self):
        (side,) = self.order(kernel_join, [VMEM] * len(self.came), [shape((4 * self.rows, PIECE), bf16)], self.came)
        self.pieces = side, send(side, "dp", self.dp, 1)


def merge_stats(group):
    top = functools.reduce(jnp.maximum, [top for top, _ in group])
    return top, sum(mass * jnp.exp(old - top) for old, mass in group)


def exchange_stats(stats, fs, dp):
    def one_round(stats, hops):
        arrived = [stats] + [send(stats, axis, count, bit) for axis, count, bit in hops]
        top, mass = merge_stats([(a[0:1], a[1:2]) for a in arrived])
        return jnp.concatenate([top, mass], axis=0)

    stats = one_round(stats, [("dp", dp, 1)])
    stats = one_round(stats, [("fsdp", fs, j) for j in range(1, fs)])
    stats = one_round(stats, [("dp", dp, j) for j in range(2, dp, 2)])
    return stats


def body(
    fs,
    dp,
    hidden_in,
    lengths,
    images,
    labels,
    wide_master,
    down_master,
    vector_master,
    wide_momentum,
    down_momentum,
    vector_momentum,
    wide_average,
    down_average,
    vector_average,
):
    tokens, width = hidden_in.shape
    captions = lengths.shape[0]
    rows = wide_master.shape[0]
    hidden = wide_master.shape[1] - 4 * width
    rank, z = lax.axis_index("dp"), lax.axis_index("fsdp")
    core, x, y = rank % 2, rank // 2 % 2, rank // 4 % 2
    member = [rank ^ k for k in range(GROUP)]
    spots = [(m % 2) * 4 + (m // 4 % 2) * 2 + (m // 2 % 2) for m in member]
    info = jnp.stack([z, core, rank * fs + z] + [z ^ j for j in range(fs)] + spots + [rank, x, y]).astype(jnp.int32)

    place = jnp.arange(SEQ)
    keep = (place[None, :] < lengths[:, None]).astype(f32).reshape(tokens)
    valid, keep = keep[None, :], keep[:, None]
    lens = lengths.astype(f32)[:, None]

    order = Order()
    piece_shape = shape((rows, PIECE), bf16)
    near_shape = shape(((fs - 1) * rows, PIECE), bf16)

    def along_z(piece):
        return [send(piece, "fsdp", fs, j) for j in range(1, fs)]

    def pack(came):
        return order(functools.partial(kernel_pack, rows), [VMEM] * (fs - 1), [near_shape], came)[0]

    def hold(value):
        return order(kernel_copy, [VMEM], [shape(value.shape, bf16)], (value,))[0]

    def joined(parts):
        length = sum(part.shape[0] for part in parts)
        return order(kernel_join, [VMEM] * len(parts), [shape((length, PIECE), bf16)], parts)[0]

    def z_first(piece):
        bit = fs // 2
        return [piece, send(piece, "fsdp", fs, bit)], [[0], [bit]], bit

    def z_next(state):
        parts, places, bit = state
        while bit > 1:
            bit //= 2
            parts = parts + [send(joined(parts), "fsdp", fs, bit)]
            places = places + [[place ^ bit for of_part in places for place in of_part]]
        return parts, places

    def z_last(state):
        parts, places = state
        places = [[place - 1 for place in of_part] for of_part in places[1:]]
        return order(
            functools.partial(kernel_sorted, rows, places), [VMEM] * (len(parts) - 1), [near_shape], parts[1:]
        )[0]

    def over_plane(near):
        return near, send(near, "dp", dp, 2), send(near, "dp", dp, 4)

    def corner(near, over_x, over_y):
        cut = near.shape[0] // 32 * 16
        diag_a, diag_b = order(
            kernel_halves,
            [VMEM] * 2,
            [shape((cut, PIECE), bf16), shape((near.shape[0] - cut, PIECE), bf16)],
            (over_x, over_y),
        )
        return near, over_x, over_y, send(diag_a, "dp", dp, 4), send(diag_b, "dp", dp, 2)

    def join(parts):
        side = joined(parts)
        return side, send(side, "dp", dp, 1)

    spot = spots[0]

    def piece_of(values, column):
        return lax.dynamic_slice(values, (0, column + spot * PIECE), (rows, PIECE)).astype(bf16)

    total = captions * fs * dp
    tags = jnp.pad(jnp.stack([labels // 128, labels % 128]), ((0, PICTURE_TAGS - 2), (0, PIECE - captions)))
    picture = hold(jnp.concatenate([images[:, :PIECE], images[:, PIECE:], tags.astype(bf16)], axis=0))
    pictures = [picture, send(picture, "dp", dp, 2)]

    own_vec = jnp.pad(vector_master.astype(bf16), ((0, 4), (0, PIECE - vector_master.shape[1])))
    piece = hold(jnp.concatenate([piece_of(wide_master, 0), own_vec], axis=0))
    piece_b = piece_of(wide_master, 4 * width)
    piece_c = lax.dynamic_slice(down_master, ((spot % 4) * rows, (spot // 4) * PIECE), (rows, PIECE)).astype(bf16)
    came = along_z(piece)
    own_a, own_b, own_c = order(
        kernel_cast,
        [VMEM] * 2,
        [shape((rows, 4 * width), bf16), shape((rows, hidden), bf16), shape(down_master.shape, bf16)],
        (wide_master, down_master),
        limit=28,
    )
    bit = 4
    while bit < dp:
        picture = joined(pictures)
        pictures = [picture, send(picture, "dp", dp, bit)]
        bit *= 2
    near_a, vec, up_bias = order(
        functools.partial(kernel_pack_first, fs, rows),
        [SMEM] + [VMEM] * fs,
        [near_shape, shape((16, width), f32), shape((1, hidden), f32)],
        (info, piece, *came),
        scratch=[pltpu.VMEM((16, width), f32)],
    )
    plane_a = over_plane(near_a)
    came = along_z(hold(piece_b))
    corner_a = corner(*plane_a)
    near_b = pack(came)
    plane_b = over_plane(near_b)
    line_c = z_first(hold(piece_c))
    parts_a = join(corner_a)
    gather_scratch = [pltpu.SemaphoreType.DMA((GROUP * fs * 2,))]

    qkv, w_att, w_out = order(
        functools.partial(kernel_qkv, fs, rows),
        [SMEM, VMEM, VMEM, VMEM] + [ANY] * 2,
        [shape((tokens, 3 * width), bf16), shape((width, 4 * width), bf16), shape((width, width), bf16)],
        (info, hidden_in, vec, own_a, *parts_a),
        scratch=gather_scratch,
        flops=6 * tokens * width * width,
        moved=10e6,
    )
    line_c = z_next(line_c)
    pictures = joined(pictures)
    pictures = [pictures] + along_z(pictures)
    corner_b = corner(*plane_b)
    ctx, h, second = order(
        kernel_attention,
        [VMEM] * 5,
        [shape((tokens, width), bf16), shape((tokens, width), f32), shape((tokens, width), bf16)],
        (hidden_in, valid, vec, qkv, w_out),
        flops=4 * tokens * width * width,
        moved=10e6,
    )
    near_c = z_last(line_c)
    plane_c = over_plane(near_c)
    parts_b = join(corner_b)
    u, g, w_up = order(
        functools.partial(kernel_up, fs, rows),
        [SMEM, VMEM, VMEM, VMEM] + [ANY] * 2,
        [shape((tokens, hidden), f32), shape((tokens, hidden), bf16), shape((width, hidden), bf16)],
        (info, second, up_bias, own_b, *parts_b),
        scratch=gather_scratch,
        flops=2 * tokens * width * hidden,
        moved=20e6,
    )
    corner_c = corner(*plane_c)
    pictures = join(pictures)
    parts_c = join(corner_c)
    block_out, pooled, inv, logits, stats, pictures, tags, w_down = order(
        functools.partial(kernel_down, fs, rows),
        [SMEM] + [VMEM] * 6 + [ANY] * 4,
        [
            shape((tokens, width), bf16),
            shape((captions, width), f32),
            shape((captions, 1), f32),
            shape((captions, total), f32),
            shape((2, total), f32),
            shape((total, width), bf16),
            shape((fs * dp * PICTURE_TAGS, 128), bf16),
            shape((hidden, width), bf16),
        ],
        (info, g, h, vec, lens, keep, own_c, *parts_c, *pictures),
        scratch=gather_scratch + [pltpu.SemaphoreType.DMA] * 2,
        limit=16 + (3 * total * width >> 20),
        flops=2 * tokens * width * hidden,
        moved=20e6,
    )

    tags = tags.reshape(fs * dp, PICTURE_TAGS, 128)[:, :2, :captions].astype(jnp.int32)
    all_labels = (tags[:, 0] * 128 + tags[:, 1]).reshape(1, total)
    stats = exchange_stats(stats, fs, dp)

    halves = [shape((4, width, PIECE), bf16)] * 2
    dpl, dy, down_bias_grad, mine, theirs = order(
        functools.partial(kernel_loss, rows),
        [SMEM] + [VMEM] * 9,
        [shape((captions, width), f32), shape((tokens, width), bf16), shape((1, width), f32)] + halves,
        (info, logits, stats, all_labels, pictures, pooled, inv, lens, keep, g),
        limit=16 + (3 * total * width >> 20),
        flops=2 * tokens * width * hidden,
        moved=10e6,
    )
    group_c = Reduction(order, info, fs, dp, mine, theirs)
    du, up_bias_grad = order(
        kernel_gelu_back,
        [VMEM] * 3,
        [shape((tokens, hidden), bf16), shape((1, hidden), f32)],
        (dy, u, w_down),
        flops=2 * tokens * width * hidden,
        moved=20e6,
    )
    group_c.core()
    mine, theirs = order(
        kernel_up_grad,
        [SMEM] + [VMEM] * 2,
        halves,
        (info, du, second),
        flops=2 * tokens * width * hidden,
        moved=10e6,
    )
    group_b = Reduction(order, info, fs, dp, mine, theirs)
    dh, da, dctx, mid_grads = order(
        kernel_mid_back,
        [VMEM] * 7,
        [
            shape((tokens, width), f32),
            shape((tokens, width), bf16),
            shape((tokens, width), bf16),
            shape((3, width), f32),
        ],
        (dpl, keep, du, h, vec, w_up, w_out),
        flops=10 * tokens * width * width,
        moved=20e6,
    )
    group_b.core()
    dqkv, bias_grads = order(
        kernel_attention_back,
        [VMEM] * 3,
        [shape((tokens, 3 * width), bf16), shape((2, width), f32)],
        (dctx, qkv, valid),
        flops=10 * tokens * width * width,
        moved=10e6,
    )
    group_c.first()
    mine, theirs = order(
        kernel_attention_grad,
        [SMEM] + [VMEM] * 5,
        halves,
        (info, hidden_in, vec, ctx, dqkv, da),
        flops=8 * tokens * width * width,
        moved=10e6,
    )
    group_a = Reduction(order, info, fs, dp, mine, theirs)
    input_grad, norm_grads = order(
        kernel_input_back,
        [VMEM] * 5,
        [shape((tokens, width), f32), shape((2, width), f32)],
        (dqkv, dh, hidden_in, vec, w_att),
        flops=6 * tokens * width * width,
        moved=10e6,
    )
    group_b.first()
    group_c.second_half()
    vec_grad = jnp.concatenate(
        [norm_grads, bias_grads, mid_grads, down_bias_grad, up_bias_grad.reshape(4, width)], axis=0
    ).astype(bf16)
    vec_grad = jnp.swapaxes(vec_grad.reshape(12, fs, width // fs), 0, 1)
    vec_grad = jnp.pad(vec_grad, ((0, 0), (0, 4), (0, PIECE - width // fs))).reshape(fs * 16, PIECE)
    group_a.ride(group_a.beyond(vec_grad))
    group_a.core()
    group_c.fold()
    group_b.second_half()
    group_c.line(rows)
    group_a.first()
    group_c.share_first()
    group_b.fold()
    group_c.share_second()
    group_a.second()
    group_b.line(rows)
    group_b.share_first()
    group_c.share()
    down_state = renew(order, info, fs, rows, group_c.pieces, down_master, down_momentum, down_average, None)
    group_b.share_second()
    group_b.share()
    group_a.line(rows)
    group_a.share_all()
    wide_state = renew(order, info, fs, rows, group_b.pieces, wide_master, wide_momentum, wide_average, GROUP)
    group_a.share()
    wide_state = renew(order, info, fs, rows, group_a.pieces, wide_master, wide_momentum, wide_average, 0, wide_state)

    vec_sum = group_a.vectors[0][:12, : width // fs]
    vector_state = renew_state(vector_master, vector_momentum, vector_average, vec_sum)
    return (
        block_out,
        input_grad,
        wide_state[0],
        down_state[0],
        vector_state[0],
        wide_state[1],
        down_state[1],
        vector_state[1],
        wide_state[2],
        down_state[2],
        vector_state[2],
        wide_state[3],
        down_state[3],
        vector_state[3],
    )


def solution(mesh):
    tokens = P(("dp", "fsdp"), None)
    each = P(("dp", "fsdp"))
    by_row = P("fsdp", None)
    by_col = P(None, "fsdp")
    states = (by_row, by_row, by_col)
    return jax.shard_map(
        functools.partial(body, mesh.shape["fsdp"], mesh.shape["dp"]),
        mesh=mesh,
        in_specs=(tokens, each, tokens, each) + states * 3,
        out_specs=(tokens, tokens) + states * 4,
        check_vma=False,
    )
```

```python
import functools

import jax
import jax.numpy as jnp
from jax import lax
from jax.experimental import pallas as pl
from jax.experimental.pallas import tpu as pltpu
from jax.sharding import PartitionSpec as P

HEADS = 12
SEQ = 16
PIECE = 384
GROUP = 8
PICTURE_TAGS = 16
LIGHT = (30,)

norm_epsilon = 1e-06
masked_score = -1e30
learn_rate = 0.02
momentum_decay = 0.5
average_decay = 0.5
gelu_scale = 0.7978845608028654
gelu_cube = 0.044715

f32 = jnp.float32
bf16 = jnp.bfloat16
VMEM = pl.BlockSpec(memory_space=pltpu.VMEM)
SMEM = pl.BlockSpec(memory_space=pltpu.SMEM)
ANY = pl.BlockSpec(memory_space=pl.ANY)
HBM = pl.BlockSpec(memory_space=pltpu.HBM)
PARAMS = pltpu.CompilerParams(vmem_limit_bytes=32 * 1024 * 1024)


def dot(left, right):
    return lax.dot_general(left, right, (((1,), (0,)), ((), ())), preferred_element_type=f32)


def dot_nt(left, right):
    return lax.dot_general(left, right, (((1,), (1,)), ((), ())), preferred_element_type=f32)


def dot_tn(left, right):
    return lax.dot_general(left, right, (((0,), (0,)), ((), ())), preferred_element_type=f32)


def shape(dims, kind):
    return jax.ShapeDtypeStruct(dims, kind)


class Order:
    def __init__(self, light):
        self.last, self.light, self.count = (), light, 0

    def weight(self):
        self.count += 1
        return cost(1 if self.count - 1 in self.light else 10**11, 1)

    def __call__(self, kernel, in_specs, out_shape, args, after=(), out_specs=None, scratch=(), flops=0, moved=0, limit=16):
        after = [*self.last, *after]
        count, skip = len(in_specs), len(after)

        def run(*refs):
            kernel(*refs[:count], *refs[count + skip :])

        outs = pl.pallas_call(
            run,
            in_specs=list(in_specs) + [ANY] * skip,
            out_specs=out_specs or [VMEM] * len(out_shape),
            out_shape=out_shape,
            scratch_shapes=scratch,
            compiler_params=pltpu.CompilerParams(vmem_limit_bytes=limit * 1024 * 1024),
            cost_estimate=self.weight(),
        )(*args, *after)
        self.last = (min(outs, key=lambda value: value.size),)
        return outs


def cost(flops, moved):
    return pl.CostEstimate(flops=int(flops), bytes_accessed=int(moved), transcendentals=0)


def norm_parts(values):
    centre = values - jnp.mean(values, axis=-1, keepdims=True)
    inv = lax.rsqrt(jnp.mean(centre * centre, axis=-1, keepdims=True) + norm_epsilon)
    return centre * inv, inv


def norm_back(grad, scaled, inv, gain):
    d_scaled = grad * gain
    first = jnp.mean(d_scaled, axis=-1, keepdims=True)
    second = jnp.mean(d_scaled * scaled, axis=-1, keepdims=True)
    return inv * (d_scaled - first - scaled * second)


def piece_copies(info, fs, rows, sides, target, sems, is_down):
    copies = []
    for k in range(GROUP):
        for j in range(1, fs):
            shard = info[3 + j]
            place = info[3 + fs + k]
            row = shard * rows
            if is_down:
                row = row * 4 + (place % 4) * rows
                col = (place // 4) * PIECE
            else:
                col = place * PIECE
            first = ((k // 2) * (fs - 1) + j - 1) * rows
            copies.append(
                pltpu.make_async_copy(
                    sides[k % 2].at[pl.ds(first, rows), :],
                    target.at[pl.ds(pl.multiple_of(row, 16), rows), pl.ds(pl.multiple_of(col, 128), PIECE)],
                    sems.at[len(copies)],
                )
            )
    return copies


def picture_copies(info, fs, captions, sides, images, tags, image_sem, tag_sem):
    block = PICTURE_TAGS
    members = sides[0].shape[0] // (block + 2 * captions) // fs
    rank, z = info[info.shape[0] - 3], info[0]
    for side in range(2):
        for j in range(fs):
            for m in range(members):
                device = (rank ^ (2 * m + side)) * fs + (z ^ j)
                first = (j * members + m) * (block + 2 * captions)
                to = pl.ds(pl.multiple_of(device * captions, 16), captions)
                for half in range(2):
                    pltpu.make_async_copy(
                        sides[side].at[pl.ds(first + half * captions, captions), :],
                        images.at[to, pl.ds(half * PIECE, PIECE)],
                        image_sem,
                    ).start()
                pltpu.make_async_copy(
                    sides[side].at[pl.ds(first + 2 * captions, block), pl.ds(0, 128)],
                    tags.at[pl.ds(pl.multiple_of(device * block, 16), block), :],
                    tag_sem,
                ).start()


def attend_forward(queries, keys, values, mask, half_low, half_high):
    both_q = jnp.concatenate([queries * half_low, queries * half_high], axis=0)
    scores = jnp.where(mask, dot_nt(both_q, keys) * 0.125, masked_score)
    top = jnp.max(scores, axis=-1, keepdims=True)
    raised = jnp.exp(scores - top)
    probs = raised / jnp.sum(raised, axis=-1, keepdims=True)
    return both_q, probs


def lane_halves():
    lane = lax.broadcasted_iota(jnp.int32, (1, 128), 1)
    low = (lane < 64).astype(f32)
    return low, low.astype(bf16), (1.0 - low).astype(bf16)


def caption_mask(valid_row):
    row = lax.broadcasted_iota(jnp.int32, (256, 128), 0)
    col = lax.broadcasted_iota(jnp.int32, (256, 128), 1)
    same = ((row & 127) // SEQ) == (col // SEQ)
    return same & (valid_row > 0.0)


def kernel_qkv(fs, rows, info, hid, vec, own, near, far, qkv_ref, w, w_out, sems):
    width = hid.shape[1]
    copies = piece_copies(info, fs, rows, (near, far), w, sems, False)
    for copy in copies:
        copy.start()
    vecs = vec[...]
    scaled, _ = norm_parts(hid[...].astype(f32))
    normed = (scaled * vecs[0:1] + vecs[1:2]).astype(bf16)
    w[pl.ds(pl.multiple_of(info[0] * rows, 16), rows), :] = own[...]
    for copy in copies:
        copy.wait()
    for part in range(3):
        cols = pl.ds(part * width, width)
        value = dot(normed, w[:, cols])
        if part == 0:
            value = value + vecs[2:3]
        if part == 2:
            value = value + vecs[3:4]
        qkv_ref[:, cols] = value.astype(bf16)
    w_out[...] = w[:, 3 * width :]


def kernel_attention(hid, valid, vec, qkv, w, ctx_ref, h_ref, second_ref):
    tokens, width = hid.shape
    low_f, low, high = lane_halves()

    def block(index, carry):
        at = pl.ds(pl.multiple_of(index * 128, 128), 128)
        mask = caption_mask(valid[:, at])
        for pair in range(width // 128):
            here = pair * 128
            queries = qkv[at, here : here + 128]
            keys = qkv[at, width + here : width + here + 128]
            values = qkv[at, 2 * width + here : 2 * width + here + 128]
            _, probs = attend_forward(queries, keys, values, mask, low, high)
            context = dot(probs.astype(bf16), values)
            ctx_ref[at, here : here + 128] = jnp.where(low_f > 0.0, context[:128], context[128:]).astype(bf16)
        return carry

    lax.fori_loop(0, tokens // 128, block, 0)
    residual = hid[...].astype(f32) + (dot(ctx_ref[...], w[...]) + vec[4:5, :])
    h_ref[...] = residual
    scaled, _ = norm_parts(residual)
    second_ref[...] = (scaled * vec[5:6, :] + vec[6:7, :]).astype(bf16)


def kernel_up(fs, rows, info, second, bias, own, near, far, u_ref, g_ref, w, sems):
    width, hidden = w.shape
    copies = piece_copies(info, fs, rows, (near, far), w, sems, False)
    for copy in copies:
        copy.start()
    w[pl.ds(pl.multiple_of(info[0] * rows, 16), rows), :] = own[...]
    for copy in copies:
        copy.wait()

    def block(index, carry):
        cols = pl.ds(index * 512, 512)
        value = dot(second[...], w[:, cols]) + bias[:, cols]
        u_ref[:, cols] = value
        inner = jnp.tanh(gelu_scale * (value + gelu_cube * value * value * value))
        g_ref[:, cols] = (0.5 * value * (1.0 + inner)).astype(bf16)
        return carry

    for index in range(hidden // 512):
        block(index, 0)


def kernel_down(fs, rows, info, g, h, vec, lens, keep, own, near, far, near_images, far_images, *rest):
    out_ref, pooled_ref, inv_ref, logit_ref, stat_ref, images, tags, w, sems, image_sem, tag_sem = rest
    tokens, width = h.shape
    captions = tokens // SEQ
    copies = piece_copies(info, fs, rows, (near, far), w, sems, True)
    picture_copies(info, fs, captions, (near_images, far_images), images, tags, image_sem, tag_sem)
    for copy in copies:
        copy.start()
    w[pl.ds(pl.multiple_of(info[0] * 4 * rows, 16), 4 * rows), :] = own[...]
    for copy in copies:
        copy.wait()
    block_rows = h[...] + (dot(g[...], w[...]) + vec[7:8, :])
    out_ref[...] = block_rows.astype(bf16)
    pooled = jnp.sum((block_rows * keep[...]).reshape(captions, SEQ, width), axis=1) / lens[...]
    inv = lax.rsqrt(jnp.sum(pooled * pooled, axis=-1, keepdims=True) + norm_epsilon)
    pooled_ref[...] = pooled
    inv_ref[...] = inv
    texts = (pooled * inv).astype(bf16)
    pltpu.make_async_copy(images, images, image_sem).wait()
    pltpu.make_async_copy(tags, tags, tag_sem).wait()
    logits = dot_nt(texts, images[...])
    logit_ref[...] = logits
    top = jnp.max(logits, axis=0, keepdims=True)
    stat_ref[0:1, :] = top
    stat_ref[1:2, :] = jnp.sum(jnp.exp(logits - top), axis=0, keepdims=True)


def put(info, half, place, value, mine, theirs):
    rows = value.shape[0]

    @pl.when(info[1] == half)
    def _():
        mine[place[0], pl.ds(place[1], rows), :] = value

    @pl.when(info[1] != half)
    def _():
        theirs[place[0], pl.ds(place[1], rows), :] = value


def kernel_loss(rows, info, logits, stats, labels, images, pooled, inv, lens, keep, g, dpl_ref, dy_ref, bias_ref, mine, theirs):
    captions, width = pooled.shape
    tokens, hidden = g.shape
    lse = stats[0:1, :] + jnp.log(stats[1:2, :])
    number = lax.broadcasted_iota(jnp.int32, logits.shape, 0) + info[2] * captions
    onehot = (labels[...] == number).astype(f32)
    slopes = (jnp.exp(logits[...] - lse) - onehot).astype(bf16)
    text_grad = dot(slopes, images[...])
    pool, inv_v = pooled[...], inv[...]
    d_pooled = inv_v * text_grad - inv_v**3 * pool * jnp.sum(pool * text_grad, axis=-1, keepdims=True)
    dpl = d_pooled / lens[...]
    dpl_ref[...] = dpl
    d_out = jnp.broadcast_to(dpl[:, None, :], (captions, SEQ, width)).reshape(tokens, width) * keep[...]
    dy = d_out.astype(bf16)
    dy_ref[...] = dy
    bias_ref[...] = jnp.sum(dy.astype(f32), axis=0, keepdims=True)
    for part in range(hidden // width):
        grad = dot_tn(g[:, part * width : (part + 1) * width], dy).astype(bf16)
        for sub in range(width // rows):
            first = part * width + sub * rows
            shard, quarter = first // (4 * rows), (first % (4 * rows)) // rows
            for half in range(2):
                value = grad[sub * rows : (sub + 1) * rows, half * PIECE : (half + 1) * PIECE]
                put(info, half, (quarter, shard * rows), value, mine, theirs)


def kernel_gelu_back(dy, u, w_down, du_ref, bias_ref):
    tokens, hidden = u.shape
    for part in range(hidden // 768):
        cols = slice(part * 768, (part + 1) * 768)
        d_gelu = dot_nt(dy[...], w_down[cols, :])
        value = u[:, cols]
        square = value * value
        inner = jnp.tanh(gelu_scale * (value + gelu_cube * value * square))
        slope = 0.5 * (1.0 + inner) + (0.5 * gelu_scale) * value * (1.0 - inner * inner) * (1.0 + (3.0 * gelu_cube) * square)
        du = (d_gelu * slope).astype(bf16)
        du_ref[:, cols] = du
        bias_ref[:, cols] = jnp.sum(du.astype(f32), axis=0, keepdims=True)


def kernel_up_grad(info, du, second, mine, theirs):
    turned = second[...].T
    for pair in range(du.shape[1] // PIECE // 2):
        grad = dot(turned, du[:, 2 * pair * PIECE : 2 * (pair + 1) * PIECE]).astype(bf16)
        for part in range(2):
            place = 2 * pair + part
            put(info, place // 4, (place % 4, 0), grad[:, part * PIECE : (part + 1) * PIECE], mine, theirs)


def kernel_mid_back(dpl, keep, du, h, vec, w_up, w_out, dh_ref, da_ref, dctx_ref, grads_ref):
    tokens, width = h.shape
    captions = tokens // SEQ
    d_second = dot_nt(du[...], w_up[...])
    scaled, inv = norm_parts(h[...])
    d_out = jnp.broadcast_to(dpl[...][:, None, :], (captions, SEQ, width)).reshape(tokens, width) * keep[...]
    dh = d_out + norm_back(d_second, scaled, inv, vec[5:6, :])
    dh_ref[...] = dh
    da = dh.astype(bf16)
    da_ref[...] = da
    grads_ref[0:1, :] = jnp.sum(da.astype(f32), axis=0, keepdims=True)
    grads_ref[1:2, :] = jnp.sum(d_second * scaled, axis=0, keepdims=True)
    grads_ref[2:3, :] = jnp.sum(d_second, axis=0, keepdims=True)
    dctx_ref[...] = dot_nt(da, w_out[...]).astype(bf16)


def kernel_attention_back(dctx, qkv, keep, dqkv_ref, grads_ref):
    tokens, width = dctx.shape
    low_f, low, high = lane_halves()
    row = lax.broadcasted_iota(jnp.int32, (128, 256), 0)
    col = lax.broadcasted_iota(jnp.int32, (128, 256), 1)
    same = (row // SEQ) == ((col & 127) // SEQ)

    def block(index, carry):
        at = pl.ds(pl.multiple_of(index * 128, 128), 128)
        mask = same & (keep[at, :] > 0.0)
        for pair in range(width // 128):
            here = pair * 128
            queries = qkv[at, here : here + 128]
            keys = qkv[at, width + here : width + here + 128]
            values = qkv[at, 2 * width + here : 2 * width + here + 128]
            d_context = dctx[at, here : here + 128]
            both_q = jnp.concatenate([queries * low, queries * high], axis=0)
            both_d = jnp.concatenate([d_context * low, d_context * high], axis=0)
            scores = jnp.where(mask, dot_nt(keys, both_q) * 0.125, masked_score)
            raised = jnp.exp(scores - jnp.max(scores, axis=0, keepdims=True))
            probs = raised / jnp.sum(raised, axis=0, keepdims=True)
            weighted = probs * dot_nt(values, both_d)
            d_scores = (weighted - probs * jnp.sum(weighted, axis=0, keepdims=True)).astype(bf16)
            d_both = dot_tn(d_scores, keys) * 0.125
            d_queries = jnp.where(low_f > 0.0, d_both[:128], d_both[128:])
            dqkv_ref[at, here : here + 128] = d_queries.astype(bf16)
            dqkv_ref[at, width + here : width + here + 128] = (dot(d_scores, both_q) * 0.125).astype(bf16)
            dqkv_ref[at, 2 * width + here : 2 * width + here + 128] = dot(probs.astype(bf16), both_d).astype(bf16)
        return carry

    lax.fori_loop(0, tokens // 128, block, 0)
    grads_ref[0:1, :] = jnp.sum(dqkv_ref[:, :width].astype(f32), axis=0, keepdims=True)
    grads_ref[1:2, :] = jnp.sum(dqkv_ref[:, 2 * width :].astype(f32), axis=0, keepdims=True)


def kernel_attention_grad(fs, info, hid, vec, ctx, dqkv, da, *refs):
    *vectors, up_bias, mine, theirs, held, block = refs
    width = hid.shape[1]
    scaled, _ = norm_parts(hid[...].astype(f32))
    turned = (scaled * vec[0:1, :] + vec[1:2, :]).astype(bf16).T
    for third in range(3):
        grad = dot(turned, dqkv[:, third * width : (third + 1) * width]).astype(bf16)
        for part in range(2):
            place = third * 2 + part
            put(info, place // 4, (place % 4, 0), grad[:, part * PIECE : (part + 1) * PIECE], mine, theirs)
    grad = dot_tn(ctx[...], da[...]).astype(bf16)
    for part in range(2):
        put(info, 1, (2 + part, 0), grad[:, part * PIECE : (part + 1) * PIECE], mine, theirs)
    held[...] = jnp.zeros_like(held)
    row = 0
    for ref in vectors:
        held[row : row + ref.shape[0], :] = ref[...]
        row += ref.shape[0]
    for part in range(4):
        held[row + part : row + part + 1, :] = up_bias[:, part * width : (part + 1) * width]
    block[...] = jnp.zeros_like(block)
    step = width // fs
    for shard in range(fs):
        block[:, :step] = held[:, shard * step : (shard + 1) * step].astype(bf16)
        for spot in range(4):
            for ref in (mine, theirs):
                ref[spot, width + 16 * shard : width + 16 * (shard + 1), :] = block[...]


def kernel_input_back(dqkv, dh, hid, vec, w_att, out_ref, grads_ref):
    width = hid.shape[1]
    d_normed = dot_nt(dqkv[...], w_att[:, : 3 * width])
    scaled, inv = norm_parts(hid[...].astype(f32))
    out_ref[...] = dh[...] + norm_back(d_normed, scaled, inv, vec[0:1, :])
    grads_ref[0:1, :] = jnp.sum(d_normed * scaled, axis=0, keepdims=True)
    grads_ref[1:2, :] = jnp.sum(d_normed, axis=0, keepdims=True)


def renew_state(master, momentum, average, gradient):
    momentum_new = momentum_decay * momentum + gradient
    master_new = master - learn_rate * (gradient + momentum_decay * momentum_new)
    average_new = average_decay * average + (1.0 - average_decay) * master_new
    return (master_new, momentum_new, average_new, master_new.astype(bf16))


def kernel_renew(fs, column, skip, info, near, far, *refs):
    states, outs, (token, buf, new_f, new_h, in_sem, out_sem) = refs[:3], refs[3 + skip : 7 + skip], refs[7 + skip :]
    rows = buf.shape[2]
    token[...] = jnp.zeros_like(token)

    def at(k):
        spot = info[3 + fs + k]
        if column is None:
            row, col = pl.multiple_of((spot % 4) * rows, 16), (spot // 4) * PIECE
        else:
            row, col = 0, (column + spot) * PIECE
        return pl.ds(row, rows), pl.ds(pl.multiple_of(col, 128), PIECE)

    def read(k, i):
        return pltpu.make_async_copy(states[i].at[at(k)], buf.at[k, i], in_sem.at[k, i])

    def write(k, i):
        source = new_h.at[k] if i == 3 else new_f.at[k, i]
        return pltpu.make_async_copy(source, outs[i].at[at(k)], out_sem.at[k, i])

    for k in range(GROUP):
        for i in range(3):
            read(k, i).start()
    for k in range(GROUP):
        for i in range(3):
            read(k, i).wait()
        source = far if k % 2 else near

        def step(index, carry):
            at = pl.ds(pl.multiple_of(index * 16, 16), 16)
            grad = source[pl.ds(pl.multiple_of(k // 2 * rows + index * 16, 16), 16), :].astype(f32)
            *new, half = renew_state(buf[k, 0, at], buf[k, 1, at], buf[k, 2, at], grad)
            for i in range(3):
                new_f[k, i, at] = new[i]
            new_h[k, at] = half
            return carry

        lax.fori_loop(0, rows // 16, step, 0, unroll=True)
        for i in range(4):
            write(k, i).start()
    for k in range(GROUP):
        for i in range(4):
            write(k, i).wait()


def renew(order, info, fs, rows, grads, master, momentum, average, column, earlier=()):
    skip = len(earlier) + len(order.last)
    *outs, token = pl.pallas_call(
        functools.partial(kernel_renew, fs, column, skip),
        in_specs=[SMEM] + [VMEM] * 2 + [HBM] * 3 + [HBM] * len(earlier) + [ANY] * len(order.last),
        out_specs=[HBM] * 4 + [VMEM],
        out_shape=[shape(master.shape, kind) for kind in (f32, f32, f32, bf16)] + [shape((8, 128), f32)],
        scratch_shapes=[
            pltpu.VMEM((GROUP, 3, rows, PIECE), f32),
            pltpu.VMEM((GROUP, 3, rows, PIECE), f32),
            pltpu.VMEM((GROUP, rows, PIECE), bf16),
            pltpu.SemaphoreType.DMA((GROUP, 3)),
            pltpu.SemaphoreType.DMA((GROUP, 4)),
        ],
        input_output_aliases={6 + i: i for i in range(len(earlier))},
        compiler_params=pltpu.CompilerParams(vmem_limit_bytes=60 * 1024 * 1024),
        cost_estimate=order.weight(),
    )(info, *grads, master, momentum, average, *earlier, *order.last)
    order.last = (token,)
    return outs


def flip(count, bit):
    return [(i, i ^ bit) for i in range(count)]


def send(value, axis, count, bit):
    return lax.ppermute(value, axis, flip(count, bit))


def kernel_pack(rows, *refs):
    *refs, own, near, piece = refs
    piece[...] = own[...]
    for j, ref in enumerate(refs):
        near[j * rows : (j + 1) * rows, :] = ref[:rows, :]


def kernel_cast(wide, down, out_a, out_b, out_c):
    cols = out_a.shape[1]
    out_a[...] = wide[:, :cols].astype(bf16)
    out_b[...] = wide[:, cols:].astype(bf16)
    out_c[...] = down[...].astype(bf16)


def kernel_join(*refs):
    *parts, out = refs
    row = 0
    for part in parts:
        out[row : row + part.shape[0], :] = part[...]
        row += part.shape[0]


def kernel_pack_first(fs, rows, info, own, *refs):
    *refs, near, vec, bias, wide = refs
    width = vec.shape[1]
    wide[...] = jnp.zeros_like(wide)
    total = jnp.zeros(vec.shape, f32)
    for j, ref in enumerate([own, *refs]):
        if j:
            near[(j - 1) * rows : j * rows, :] = ref[:rows, :]
        wide[:, :PIECE] = ref[rows:, :].astype(f32)
        total = total + pltpu.roll(wide[...], info[3 + j] * (width // fs), 1)
    vec[...] = total
    for row in range(4):
        bias[:, row * width : (row + 1) * width] = total[8 + row : 9 + row, :]


def kernel_sorted(rows, places, *refs):
    *parts, out = refs
    for part, of_part in zip(parts, places):
        for i, place in enumerate(of_part):
            out[place * rows : (place + 1) * rows, :] = part[i * rows : (i + 1) * rows, :]


def kernel_halves(over_x, over_y, first, second):
    cut = first.shape[0]
    first[...] = over_x[:cut, :]
    second[...] = over_y[cut:, :]


def kernel_copy(value, out):
    out[...] = value[...]


def total_of(left, right):
    return (left.astype(f32) + right.astype(f32)).astype(bf16)


def kernel_add_core(fs, rows, info, mine, came, *refs):
    to_x, to_y, keep_x, keep_y = refs
    step = to_x.shape[1] * 2 // fs
    x, y = info[info.shape[0] - 2], info[info.shape[0] - 1]
    for other in range(2):
        for ref, spot, first in (
            (to_x, other * 2 + (1 - x), 0),
            (to_y, (1 - y) * 2 + other, fs // 2),
            (keep_x, other * 2 + x, 0),
            (keep_y, y * 2 + other, fs // 2),
        ):
            for shard in range(fs // 2):
                at = pl.ds((first + shard) * rows, rows)
                ref[other, pl.ds(shard * step, rows), :] = total_of(mine[spot, at, :], came[spot, at, :])
                if step > rows:
                    at = pl.ds(fs * rows + (first + shard) * 16, 16)
                    ref[other, pl.ds(shard * step + rows, 16), :] = total_of(mine[spot, at, :], came[spot, at, :])


def kernel_add_first(info, keep_x, keep_y, came_x, came_y, to_y, to_x, left_x, left_y):
    x, y = info[info.shape[0] - 2], info[info.shape[0] - 1]
    to_y[...] = total_of(keep_x[1 - y], came_x[1 - y])
    to_x[...] = total_of(keep_y[1 - x], came_y[1 - x])
    left_x[...] = total_of(keep_x[y], came_x[y])
    left_y[...] = total_of(keep_y[x], came_y[x])


def kernel_add_second(fs, rows, info, left_x, left_y, came_y, came_x, *refs):
    *outs, own = refs
    half = left_x.shape[0]
    own[:half, :] = total_of(left_x[...], came_y[...])
    own[half:, :] = total_of(left_y[...], came_x[...])
    for j, ref in enumerate(outs):
        ref[...] = own[pl.ds(pl.multiple_of(info[3 + j] * rows, 16), rows), :]


def kernel_add_second_half(fs, rows, info, left_x, left_y, came_y, came_x, keep, give, own):
    half = left_x.shape[0]
    own[:half, :] = total_of(left_x[...], came_y[...])
    own[half:, :] = total_of(left_y[...], came_x[...])
    for j in range(fs):
        ref = give if j % 2 else keep
        block = own[pl.ds(pl.multiple_of(info[3 + j] * rows, 16), rows), :]
        ref[j // 2 * rows : (j // 2 + 1) * rows, :] = block


def kernel_fold(rows, keep, came, left, give):
    for j in range(keep.shape[0] // rows):
        ref = give if j % 2 else left
        at = slice(j * rows, (j + 1) * rows)
        ref[j // 2 * rows : (j // 2 + 1) * rows, :] = total_of(keep[at, :], came[at, :])


def kernel_add_z(fs, *refs):
    parts, (out, *vectors) = refs[:fs], refs[fs:]
    rows = out.shape[0]
    out[...] = sum(part[:rows, :].astype(f32) for part in parts).astype(bf16)
    for ref in vectors:
        ref[...] = sum(part[rows:, :].astype(f32) for part in parts)


class Reduction:
    def __init__(self, order, info, fs, dp, rows, mine, theirs):
        self.order, self.info, self.fs, self.dp, self.rows = order, info, fs, dp, rows
        self.width = mine.shape[1]
        mine, theirs = self.beyond(mine), self.beyond(theirs)
        self.mine = [mine, send(theirs, "dp", dp, 1)]

    def beyond(self, value):
        bit = GROUP
        while bit < self.dp:
            value = total_of(value, send(value, "dp", self.dp, bit))
            bit *= 2
        return value

    def core(self):
        rows, self.rows = self.rows, self.width // self.fs
        to_x, to_y, *self.keep = self.order(
            functools.partial(kernel_add_core, self.fs, rows),
            [SMEM] + [VMEM] * 2,
            [shape((2, self.width // 2, PIECE), bf16)] * 4,
            (self.info, *self.mine),
        )
        self.came = send(to_x, "dp", self.dp, 2), send(to_y, "dp", self.dp, 4)

    def first(self):
        half = self.width // 2
        to_y, to_x, *self.keep = self.order(
            kernel_add_first,
            [SMEM] + [VMEM] * 4,
            [shape((half, PIECE), bf16)] * 4,
            (self.info, *self.keep, *self.came),
            moved=3e6,
        )
        self.came = send(to_y, "dp", self.dp, 4), send(to_x, "dp", self.dp, 2)

    def second(self):
        parts = self.order(
            functools.partial(kernel_add_second, self.fs, self.rows),
            [SMEM] + [VMEM] * 4,
            [shape((self.rows, PIECE), bf16)] * self.fs,
            (self.info, *self.keep, *self.came),
            scratch=[pltpu.VMEM((self.width, PIECE), bf16)],
            moved=2e6,
        )
        self.came = [parts[0]] + [send(parts[j], "fsdp", self.fs, j) for j in range(1, self.fs)]

    def second_half(self):
        self.bit, count = 1, self.fs // 2
        keep, give = self.order(
            functools.partial(kernel_add_second_half, self.fs, self.rows),
            [SMEM] + [VMEM] * 4,
            [shape((count * self.rows, PIECE), bf16)] * 2,
            (self.info, *self.keep, *self.came),
            scratch=[pltpu.VMEM((self.width, PIECE), bf16)],
        )
        self.came = [keep, send(give, "fsdp", self.fs, 1)]

    def fold(self):
        while 2 * self.bit < self.fs:
            self.bit *= 2
            count = self.fs // self.bit // 2
            keep, give = self.order(
                functools.partial(kernel_fold, self.rows),
                [VMEM] * 2,
                [shape((count * self.rows, PIECE), bf16)] * 2,
                self.came,
            )
            self.came = [keep, send(give, "fsdp", self.fs, self.bit)]

    def line(self, grad_rows):
        count = len(self.came)
        extra = [shape((self.rows - grad_rows, PIECE), f32)] if self.rows > grad_rows else []
        piece, *self.vectors = self.order(
            functools.partial(kernel_add_z, count), [VMEM] * count, [shape((grad_rows, PIECE), bf16)] + extra, self.came
        )
        self.rows, self.piece = grad_rows, piece

    def share_first(self):
        self.came = [self.piece, send(self.piece, "dp", self.dp, 2)]

    def share_second(self):
        (pair,) = self.order(kernel_join, [VMEM] * 2, [shape((2 * self.rows, PIECE), bf16)], self.came)
        self.came = [pair, send(pair, "dp", self.dp, 4)]

    def share_all(self):
        self.came = [self.piece] + [send(self.piece, "dp", self.dp, k) for k in (2, 4, 6)]

    def share(self):
        (side,) = self.order(kernel_join, [VMEM] * len(self.came), [shape((4 * self.rows, PIECE), bf16)], self.came)
        self.pieces = side, send(side, "dp", self.dp, 1)


def merge_stats(group):
    top = functools.reduce(jnp.maximum, [top for top, _ in group])
    return top, sum(mass * jnp.exp(old - top) for old, mass in group)


def exchange_stats(stats, fs, dp):
    def one_round(stats, hops):
        arrived = [stats] + [send(stats, axis, count, bit) for axis, count, bit in hops]
        top, mass = merge_stats([(a[0:1], a[1:2]) for a in arrived])
        return jnp.concatenate([top, mass], axis=0)

    stats = one_round(stats, [("dp", dp, 1)])
    stats = one_round(stats, [("fsdp", fs, j) for j in range(1, fs)])
    stats = one_round(stats, [("dp", dp, j) for j in range(2, dp, 2)])
    return stats


def body(
    fs,
    dp,
    hidden_in,
    lengths,
    images,
    labels,
    wide_master,
    down_master,
    vector_master,
    wide_momentum,
    down_momentum,
    vector_momentum,
    wide_average,
    down_average,
    vector_average,
):
    tokens, width = hidden_in.shape
    captions = lengths.shape[0]
    rows = wide_master.shape[0]
    hidden = wide_master.shape[1] - 4 * width
    rank, z = lax.axis_index("dp"), lax.axis_index("fsdp")
    core, x, y = rank % 2, rank // 2 % 2, rank // 4 % 2
    member = [rank ^ k for k in range(GROUP)]
    spots = [(m % 2) * 4 + (m // 4 % 2) * 2 + (m // 2 % 2) for m in member]
    info = jnp.stack([z, core, rank * fs + z] + [z ^ j for j in range(fs)] + spots + [rank, x, y]).astype(jnp.int32)

    place = jnp.arange(SEQ)
    keep = (place[None, :] < lengths[:, None]).astype(f32).reshape(tokens)
    valid, keep = keep[None, :], keep[:, None]
    lens = lengths.astype(f32)[:, None]

    order = Order(LIGHT)
    piece_shape = shape((rows, PIECE), bf16)
    near_shape = shape(((fs - 1) * rows, PIECE), bf16)

    def along_z(piece):
        return [send(piece, "fsdp", fs, j) for j in range(1, fs)]

    def pack(came, following):
        return order(
            functools.partial(kernel_pack, rows), [VMEM] * fs, [near_shape, piece_shape], (*came, following)
        )

    def hold(value):
        return order(kernel_copy, [VMEM], [shape(value.shape, bf16)], (value,))[0]

    def joined(parts):
        length = sum(part.shape[0] for part in parts)
        return order(kernel_join, [VMEM] * len(parts), [shape((length, PIECE), bf16)], parts)[0]

    def z_first(piece):
        bit = fs // 2
        return [piece, send(piece, "fsdp", fs, bit)], [[0], [bit]], bit

    def z_next(state):
        parts, places, bit = state
        while bit > 1:
            bit //= 2
            parts = parts + [send(joined(parts), "fsdp", fs, bit)]
            places = places + [[place ^ bit for of_part in places for place in of_part]]
        return parts, places

    def z_last(state):
        parts, places = state
        places = [[place - 1 for place in of_part] for of_part in places[1:]]
        return order(
            functools.partial(kernel_sorted, rows, places), [VMEM] * (len(parts) - 1), [near_shape], parts[1:]
        )[0]

    def over_plane(near):
        return near, send(near, "dp", dp, 2), send(near, "dp", dp, 4)

    def corner(near, over_x, over_y):
        cut = near.shape[0] // 32 * 16
        diag_a, diag_b = order(
            kernel_halves,
            [VMEM] * 2,
            [shape((cut, PIECE), bf16), shape((near.shape[0] - cut, PIECE), bf16)],
            (over_x, over_y),
        )
        return near, over_x, over_y, send(diag_a, "dp", dp, 4), send(diag_b, "dp", dp, 2)

    def join(parts):
        side = joined(parts)
        return side, send(side, "dp", dp, 1)

    spot = spots[0]

    def piece_of(values, column):
        return lax.dynamic_slice(values, (0, column + spot * PIECE), (rows, PIECE)).astype(bf16)

    total = captions * fs * dp
    tags = jnp.pad(jnp.stack([labels // 128, labels % 128]), ((0, PICTURE_TAGS - 2), (0, PIECE - captions)))
    picture = hold(jnp.concatenate([images[:, :PIECE], images[:, PIECE:], tags.astype(bf16)], axis=0))
    pictures = [picture, send(picture, "dp", dp, 2)]

    own_vec = jnp.pad(vector_master.astype(bf16), ((0, 4), (0, PIECE - vector_master.shape[1])))
    piece = hold(jnp.concatenate([piece_of(wide_master, 0), own_vec], axis=0))
    piece_b = piece_of(wide_master, 4 * width)
    piece_c = lax.dynamic_slice(down_master, ((spot % 4) * rows, (spot // 4) * PIECE), (rows, PIECE)).astype(bf16)
    came = along_z(piece)
    own_a, own_b, own_c = order(
        kernel_cast,
        [VMEM] * 2,
        [shape((rows, 4 * width), bf16), shape((rows, hidden), bf16), shape(down_master.shape, bf16)],
        (wide_master, down_master),
        limit=28,
    )
    bit = 4
    while bit < dp:
        picture = joined(pictures)
        pictures = [picture, send(picture, "dp", dp, bit)]
        bit *= 2
    near_a, vec, up_bias = order(
        functools.partial(kernel_pack_first, fs, rows),
        [SMEM] + [VMEM] * fs,
        [near_shape, shape((16, width), f32), shape((1, hidden), f32)],
        (info, piece, *came),
        scratch=[pltpu.VMEM((16, width), f32)],
    )
    plane_a = over_plane(near_a)
    came = along_z(hold(piece_b))
    corner_a = corner(*plane_a)
    near_b, piece_c = pack(came, piece_c)
    plane_b = over_plane(near_b)
    line_c = z_first(piece_c)
    parts_a = join(corner_a)
    gather_scratch = [pltpu.SemaphoreType.DMA((GROUP * fs * 2,))]

    qkv, w_att, w_out = order(
        functools.partial(kernel_qkv, fs, rows),
        [SMEM, VMEM, VMEM, VMEM] + [ANY] * 2,
        [shape((tokens, 3 * width), bf16), shape((width, 4 * width), bf16), shape((width, width), bf16)],
        (info, hidden_in, vec, own_a, *parts_a),
        scratch=gather_scratch,
        flops=6 * tokens * width * width,
        moved=10e6,
    )
    line_c = z_next(line_c)
    pictures = joined(pictures)
    pictures = [pictures] + along_z(pictures)
    corner_b = corner(*plane_b)
    ctx, h, second = order(
        kernel_attention,
        [VMEM] * 5,
        [shape((tokens, width), bf16), shape((tokens, width), f32), shape((tokens, width), bf16)],
        (hidden_in, valid, vec, qkv, w_out),
        flops=4 * tokens * width * width,
        moved=10e6,
    )
    near_c = z_last(line_c)
    plane_c = over_plane(near_c)
    parts_b = join(corner_b)
    u, g, w_up = order(
        functools.partial(kernel_up, fs, rows),
        [SMEM, VMEM, VMEM, VMEM] + [ANY] * 2,
        [shape((tokens, hidden), f32), shape((tokens, hidden), bf16), shape((width, hidden), bf16)],
        (info, second, up_bias, own_b, *parts_b),
        scratch=gather_scratch,
        flops=2 * tokens * width * hidden,
        moved=20e6,
    )
    corner_c = corner(*plane_c)
    pictures = join(pictures)
    parts_c = join(corner_c)
    block_out, pooled, inv, logits, stats, pictures, tags, w_down = order(
        functools.partial(kernel_down, fs, rows),
        [SMEM] + [VMEM] * 6 + [ANY] * 4,
        [
            shape((tokens, width), bf16),
            shape((captions, width), f32),
            shape((captions, 1), f32),
            shape((captions, total), f32),
            shape((2, total), f32),
            shape((total, width), bf16),
            shape((fs * dp * PICTURE_TAGS, 128), bf16),
            shape((hidden, width), bf16),
        ],
        (info, g, h, vec, lens, keep, own_c, *parts_c, *pictures),
        scratch=gather_scratch + [pltpu.SemaphoreType.DMA] * 2,
        limit=16 + (3 * total * width >> 20),
        flops=2 * tokens * width * hidden,
        moved=20e6,
    )

    tags = tags.reshape(fs * dp, PICTURE_TAGS, 128)[:, :2, :captions].astype(jnp.int32)
    all_labels = (tags[:, 0] * 128 + tags[:, 1]).reshape(1, total)
    stats = exchange_stats(stats, fs, dp)

    halves = [shape((4, width, PIECE), bf16)] * 2
    dpl, dy, down_bias_grad, mine, theirs = order(
        functools.partial(kernel_loss, rows),
        [SMEM] + [VMEM] * 9,
        [shape((captions, width), f32), shape((tokens, width), bf16), shape((1, width), f32)] + halves,
        (info, logits, stats, all_labels, pictures, pooled, inv, lens, keep, g),
        limit=16 + (3 * total * width >> 20),
        flops=2 * tokens * width * hidden,
        moved=10e6,
    )
    group_c = Reduction(order, info, fs, dp, rows, mine, theirs)
    du, up_bias_grad = order(
        kernel_gelu_back,
        [VMEM] * 3,
        [shape((tokens, hidden), bf16), shape((1, hidden), f32)],
        (dy, u, w_down),
        flops=2 * tokens * width * hidden,
        moved=20e6,
    )
    group_c.core()
    mine, theirs = order(
        kernel_up_grad,
        [SMEM] + [VMEM] * 2,
        halves,
        (info, du, second),
        flops=2 * tokens * width * hidden,
        moved=10e6,
    )
    group_b = Reduction(order, info, fs, dp, rows, mine, theirs)
    dh, da, dctx, mid_grads = order(
        kernel_mid_back,
        [VMEM] * 7,
        [
            shape((tokens, width), f32),
            shape((tokens, width), bf16),
            shape((tokens, width), bf16),
            shape((3, width), f32),
        ],
        (dpl, keep, du, h, vec, w_up, w_out),
        flops=10 * tokens * width * width,
        moved=20e6,
    )
    group_b.core()
    dqkv, bias_grads = order(
        kernel_attention_back,
        [VMEM] * 3,
        [shape((tokens, 3 * width), bf16), shape((2, width), f32)],
        (dctx, qkv, keep),
        flops=10 * tokens * width * width,
        moved=10e6,
    )
    input_grad, norm_grads = order(
        kernel_input_back,
        [VMEM] * 5,
        [shape((tokens, width), f32), shape((2, width), f32)],
        (dqkv, dh, hidden_in, vec, w_att),
        flops=6 * tokens * width * width,
        moved=10e6,
    )
    group_c.first()
    mine, theirs = order(
        functools.partial(kernel_attention_grad, fs),
        [SMEM] + [VMEM] * 10,
        [shape((4, width + 16 * fs, PIECE), bf16)] * 2,
        (info, hidden_in, vec, ctx, dqkv, da, norm_grads, bias_grads, mid_grads, down_bias_grad, up_bias_grad),
        scratch=[pltpu.VMEM((16, width), f32), pltpu.VMEM((16, PIECE), bf16)],
        flops=8 * tokens * width * width,
        moved=10e6,
    )
    group_a = Reduction(order, info, fs, dp, rows, mine, theirs)
    group_b.first()
    group_c.second_half()
    group_a.core()
    group_c.fold()
    group_b.second_half()
    group_c.line(rows)
    group_a.first()
    group_c.share_first()
    group_b.fold()
    group_c.share_second()
    group_b.line(rows)
    group_b.share_first()
    group_a.second()
    group_c.share()
    group_b.share_second()
    down_state = renew(order, info, fs, rows, group_c.pieces, down_master, down_momentum, down_average, None)
    group_b.share()
    group_a.line(rows)
    group_a.share_all()
    wide_state = renew(order, info, fs, rows, group_b.pieces, wide_master, wide_momentum, wide_average, GROUP)
    group_a.share()
    wide_state = renew(order, info, fs, rows, group_a.pieces, wide_master, wide_momentum, wide_average, 0, wide_state)

    vec_sum = group_a.vectors[0][:12, : width // fs]
    vector_state = renew_state(vector_master, vector_momentum, vector_average, vec_sum)
    return (
        block_out,
        input_grad,
        wide_state[0],
        down_state[0],
        vector_state[0],
        wide_state[1],
        down_state[1],
        vector_state[1],
        wide_state[2],
        down_state[2],
        vector_state[2],
        wide_state[3],
        down_state[3],
        vector_state[3],
    )


def solution(mesh):
    tokens = P(("dp", "fsdp"), None)
    each = P(("dp", "fsdp"))
    by_row = P("fsdp", None)
    by_col = P(None, "fsdp")
    states = (by_row, by_row, by_col)
    return jax.shard_map(
        functools.partial(body, mesh.shape["fsdp"], mesh.shape["dp"]),
        mesh=mesh,
        in_specs=(tokens, each, tokens, each) + states * 3,
        out_specs=(tokens, tokens) + states * 4,
        check_vma=False,
    )
```

```python
import functools

import jax
import jax.numpy as jnp
from jax import lax
from jax.experimental import pallas as pl
from jax.experimental.pallas import tpu as pltpu
from jax.sharding import PartitionSpec as P

HEADS = 12
SEQ = 16
PIECE = 384
GROUP = 8
PICTURE_TAGS = 16
LIGHT = (8, 36, 41, 42, 43, 46)

norm_epsilon = 1e-06
masked_score = -1e30
learn_rate = 0.02
momentum_decay = 0.5
average_decay = 0.5
gelu_scale = 0.7978845608028654
gelu_cube = 0.044715

f32 = jnp.float32
bf16 = jnp.bfloat16
VMEM = pl.BlockSpec(memory_space=pltpu.VMEM)
SMEM = pl.BlockSpec(memory_space=pltpu.SMEM)
ANY = pl.BlockSpec(memory_space=pl.ANY)
HBM = pl.BlockSpec(memory_space=pltpu.HBM)
PARAMS = pltpu.CompilerParams(vmem_limit_bytes=32 * 1024 * 1024)


def dot(left, right):
    return lax.dot_general(left, right, (((1,), (0,)), ((), ())), preferred_element_type=f32)


def dot_nt(left, right):
    return lax.dot_general(left, right, (((1,), (1,)), ((), ())), preferred_element_type=f32)


def dot_tn(left, right):
    return lax.dot_general(left, right, (((0,), (0,)), ((), ())), preferred_element_type=f32)


def shape(dims, kind):
    return jax.ShapeDtypeStruct(dims, kind)


class Order:
    def __init__(self, light):
        self.last, self.light, self.count = (), light, 0

    def weight(self):
        self.count += 1
        return cost(1 if self.count - 1 in self.light else 10**11, 1)

    def __call__(self, kernel, in_specs, out_shape, args, after=(), out_specs=None, scratch=(), flops=0, moved=0, limit=16):
        after = [*self.last, *after]
        count, skip = len(in_specs), len(after)

        def run(*refs):
            kernel(*refs[:count], *refs[count + skip :])

        outs = pl.pallas_call(
            run,
            in_specs=list(in_specs) + [ANY] * skip,
            out_specs=out_specs or [VMEM] * len(out_shape),
            out_shape=out_shape,
            scratch_shapes=scratch,
            compiler_params=pltpu.CompilerParams(vmem_limit_bytes=limit * 1024 * 1024),
            cost_estimate=self.weight(),
        )(*args, *after)
        self.last = (min(outs, key=lambda value: value.size),)
        return outs


def cost(flops, moved):
    return pl.CostEstimate(flops=int(flops), bytes_accessed=int(moved), transcendentals=0)


def norm_parts(values):
    centre = values - jnp.mean(values, axis=-1, keepdims=True)
    inv = lax.rsqrt(jnp.mean(centre * centre, axis=-1, keepdims=True) + norm_epsilon)
    return centre * inv, inv


def norm_back(grad, scaled, inv, gain):
    d_scaled = grad * gain
    first = jnp.mean(d_scaled, axis=-1, keepdims=True)
    second = jnp.mean(d_scaled * scaled, axis=-1, keepdims=True)
    return inv * (d_scaled - first - scaled * second)


def piece_copies(info, fs, rows, sides, target, sems, is_down):
    copies = []
    for k in range(GROUP):
        for j in range(1, fs):
            shard = info[3 + j]
            place = info[3 + fs + k]
            row = shard * rows
            if is_down:
                row = row * 4 + (place % 4) * rows
                col = (place // 4) * PIECE
            else:
                col = place * PIECE
            first = ((k // 2) * (fs - 1) + j - 1) * rows
            copies.append(
                pltpu.make_async_copy(
                    sides[k % 2].at[pl.ds(first, rows), :],
                    target.at[pl.ds(pl.multiple_of(row, 16), rows), pl.ds(pl.multiple_of(col, 128), PIECE)],
                    sems.at[len(copies)],
                )
            )
    return copies


def picture_copies(info, fs, captions, sides, images, tags, image_sem, tag_sem):
    block = PICTURE_TAGS
    members = sides[0].shape[0] // (block + 2 * captions) // fs
    rank, z = info[info.shape[0] - 3], info[0]
    for side in range(2):
        for j in range(fs):
            for m in range(members):
                device = (rank ^ (2 * m + side)) * fs + (z ^ j)
                first = (j * members + m) * (block + 2 * captions)
                to = pl.ds(pl.multiple_of(device * captions, 16), captions)
                for half in range(2):
                    pltpu.make_async_copy(
                        sides[side].at[pl.ds(first + half * captions, captions), :],
                        images.at[to, pl.ds(half * PIECE, PIECE)],
                        image_sem,
                    ).start()
                pltpu.make_async_copy(
                    sides[side].at[pl.ds(first + 2 * captions, block), pl.ds(0, 128)],
                    tags.at[pl.ds(pl.multiple_of(device * block, 16), block), :],
                    tag_sem,
                ).start()


def attend_forward(queries, keys, values, mask, half_low, half_high):
    both_q = jnp.concatenate([queries * half_low, queries * half_high], axis=0)
    scores = jnp.where(mask, dot_nt(both_q, keys) * 0.125, masked_score)
    top = jnp.max(scores, axis=-1, keepdims=True)
    raised = jnp.exp(scores - top)
    probs = raised / jnp.sum(raised, axis=-1, keepdims=True)
    return both_q, probs


def lane_halves():
    lane = lax.broadcasted_iota(jnp.int32, (1, 128), 1)
    low = (lane < 64).astype(f32)
    return low, low.astype(bf16), (1.0 - low).astype(bf16)


def caption_mask(valid_row):
    row = lax.broadcasted_iota(jnp.int32, (256, 128), 0)
    col = lax.broadcasted_iota(jnp.int32, (256, 128), 1)
    same = ((row & 127) // SEQ) == (col // SEQ)
    return same & (valid_row > 0.0)


def kernel_qkv(fs, rows, info, hid, vec, own, near, far, qkv_ref, w, w_out, sems):
    width = hid.shape[1]
    copies = piece_copies(info, fs, rows, (near, far), w, sems, False)
    for copy in copies:
        copy.start()
    vecs = vec[...]
    scaled, _ = norm_parts(hid[...].astype(f32))
    normed = (scaled * vecs[0:1] + vecs[1:2]).astype(bf16)
    w[pl.ds(pl.multiple_of(info[0] * rows, 16), rows), :] = own[...]
    for copy in copies:
        copy.wait()
    for part in range(3):
        cols = pl.ds(part * width, width)
        value = dot(normed, w[:, cols])
        if part == 0:
            value = value + vecs[2:3]
        if part == 2:
            value = value + vecs[3:4]
        qkv_ref[:, cols] = value.astype(bf16)
    w_out[...] = w[:, 3 * width :]


def kernel_attention(hid, valid, vec, qkv, w, ctx_ref, h_ref, second_ref):
    tokens, width = hid.shape
    low_f, low, high = lane_halves()

    def block(index, carry):
        at = pl.ds(pl.multiple_of(index * 128, 128), 128)
        mask = caption_mask(valid[:, at])
        for pair in range(width // 128):
            here = pair * 128
            queries = qkv[at, here : here + 128]
            keys = qkv[at, width + here : width + here + 128]
            values = qkv[at, 2 * width + here : 2 * width + here + 128]
            _, probs = attend_forward(queries, keys, values, mask, low, high)
            context = dot(probs.astype(bf16), values)
            ctx_ref[at, here : here + 128] = jnp.where(low_f > 0.0, context[:128], context[128:]).astype(bf16)
        return carry

    lax.fori_loop(0, tokens // 128, block, 0)
    residual = hid[...].astype(f32) + (dot(ctx_ref[...], w[...]) + vec[4:5, :])
    h_ref[...] = residual
    scaled, _ = norm_parts(residual)
    second_ref[...] = (scaled * vec[5:6, :] + vec[6:7, :]).astype(bf16)


def kernel_up(fs, rows, info, second, bias, own, near, far, slope_ref, g_ref, w, sems):
    width, hidden = w.shape
    copies = piece_copies(info, fs, rows, (near, far), w, sems, False)
    for copy in copies:
        copy.start()
    w[pl.ds(pl.multiple_of(info[0] * rows, 16), rows), :] = own[...]
    for copy in copies:
        copy.wait()

    def block(index, carry):
        cols = pl.ds(index * 512, 512)
        value = dot(second[...], w[:, cols]) + bias[:, cols]
        square = value * value
        inner = jnp.tanh(gelu_scale * (value + gelu_cube * value * square))
        slope = 0.5 * (1.0 + inner) + (0.5 * gelu_scale) * value * (1.0 - inner * inner) * (1.0 + (3.0 * gelu_cube) * square)
        slope_ref[:, cols] = slope.astype(bf16)
        g_ref[:, cols] = (0.5 * value * (1.0 + inner)).astype(bf16)
        return carry

    for index in range(hidden // 512):
        block(index, 0)


def kernel_down(fs, rows, info, g, h, vec, lens, keep, own, near, far, near_images, far_images, *rest):
    out_ref, pooled_ref, inv_ref, logit_ref, stat_ref, images, tags, w, sems, image_sem, tag_sem = rest
    tokens, width = h.shape
    captions = tokens // SEQ
    copies = piece_copies(info, fs, rows, (near, far), w, sems, True)
    picture_copies(info, fs, captions, (near_images, far_images), images, tags, image_sem, tag_sem)
    for copy in copies:
        copy.start()
    w[pl.ds(pl.multiple_of(info[0] * 4 * rows, 16), 4 * rows), :] = own[...]
    for copy in copies:
        copy.wait()
    block_rows = h[...] + (dot(g[...], w[...]) + vec[7:8, :])
    out_ref[...] = block_rows.astype(bf16)
    pooled = jnp.sum((block_rows * keep[...]).reshape(captions, SEQ, width), axis=1) / lens[...]
    inv = lax.rsqrt(jnp.sum(pooled * pooled, axis=-1, keepdims=True) + norm_epsilon)
    pooled_ref[...] = pooled
    inv_ref[...] = inv
    texts = (pooled * inv).astype(bf16)
    pltpu.make_async_copy(images, images, image_sem).wait()
    pltpu.make_async_copy(tags, tags, tag_sem).wait()
    logits = dot_nt(texts, images[...])
    logit_ref[...] = logits
    top = jnp.max(logits, axis=0, keepdims=True)
    stat_ref[0:1, :] = top
    stat_ref[1:2, :] = jnp.sum(jnp.exp(logits - top), axis=0, keepdims=True)


def put(info, half, place, value, mine, theirs):
    rows = value.shape[0]

    @pl.when(info[1] == half)
    def _():
        mine[place[0], pl.ds(place[1], rows), :] = value

    @pl.when(info[1] != half)
    def _():
        theirs[place[0], pl.ds(place[1], rows), :] = value


def kernel_loss(rows, info, logits, stats, labels, images, pooled, inv, lens, keep, g, dpl_ref, dy_ref, bias_ref, mine, theirs):
    captions, width = pooled.shape
    hidden, tokens = g.shape
    lse = stats[0:1, :] + jnp.log(stats[1:2, :])
    number = lax.broadcasted_iota(jnp.int32, logits.shape, 0) + info[2] * captions
    onehot = (labels[...] == number).astype(f32)
    slopes = (jnp.exp(logits[...] - lse) - onehot).astype(bf16)
    text_grad = dot(slopes, images[...])
    pool, inv_v = pooled[...], inv[...]
    d_pooled = inv_v * text_grad - inv_v**3 * pool * jnp.sum(pool * text_grad, axis=-1, keepdims=True)
    dpl = d_pooled / lens[...]
    dpl_ref[...] = dpl
    d_out = jnp.broadcast_to(dpl[:, None, :], (captions, SEQ, width)).reshape(tokens, width) * keep[...]
    dy = d_out.astype(bf16)
    dy_ref[...] = dy
    bias_ref[...] = jnp.sum(dy.astype(f32), axis=0, keepdims=True)
    for part in range(hidden // width):
        grad = dot(g[part * width : (part + 1) * width, :], dy).astype(bf16)
        for sub in range(width // rows):
            first = part * width + sub * rows
            shard, quarter = first // (4 * rows), (first % (4 * rows)) // rows
            for half in range(2):
                value = grad[sub * rows : (sub + 1) * rows, half * PIECE : (half + 1) * PIECE]
                put(info, half, (quarter, shard * rows), value, mine, theirs)


def kernel_gelu_back(dy, slope, w_down, du_ref, bias_ref):
    tokens, hidden = slope.shape
    for part in range(hidden // 768):
        cols = slice(part * 768, (part + 1) * 768)
        du = (dot_nt(dy[...], w_down[cols, :]) * slope[:, cols].astype(f32)).astype(bf16)
        du_ref[:, cols] = du
        bias_ref[:, cols] = jnp.sum(du.astype(f32), axis=0, keepdims=True)


def kernel_up_grad(info, du, second, mine, theirs):
    turned = second[...]
    for pair in range(du.shape[1] // PIECE // 2):
        grad = dot(turned, du[:, 2 * pair * PIECE : 2 * (pair + 1) * PIECE]).astype(bf16)
        for part in range(2):
            place = 2 * pair + part
            put(info, place // 4, (place % 4, 0), grad[:, part * PIECE : (part + 1) * PIECE], mine, theirs)


def kernel_mid_back(dpl, keep, du, h, vec, w_up, w_out, dh_ref, da_ref, dctx_ref, grads_ref):
    tokens, width = h.shape
    captions = tokens // SEQ
    d_second = dot_nt(du[...], w_up[...])
    scaled, inv = norm_parts(h[...])
    d_out = jnp.broadcast_to(dpl[...][:, None, :], (captions, SEQ, width)).reshape(tokens, width) * keep[...]
    dh = d_out + norm_back(d_second, scaled, inv, vec[5:6, :])
    dh_ref[...] = dh
    da = dh.astype(bf16)
    da_ref[...] = da
    grads_ref[0:1, :] = jnp.sum(da.astype(f32), axis=0, keepdims=True)
    grads_ref[1:2, :] = jnp.sum(d_second * scaled, axis=0, keepdims=True)
    grads_ref[2:3, :] = jnp.sum(d_second, axis=0, keepdims=True)
    dctx_ref[...] = dot_nt(da, w_out[...]).astype(bf16)


def kernel_attention_back(dctx, qkv, keep, dqkv_ref, grads_ref):
    tokens, width = dctx.shape
    low_f, low, high = lane_halves()
    row = lax.broadcasted_iota(jnp.int32, (128, 256), 0)
    col = lax.broadcasted_iota(jnp.int32, (128, 256), 1)
    same = (row // SEQ) == ((col & 127) // SEQ)

    def block(index, carry):
        at = pl.ds(pl.multiple_of(index * 128, 128), 128)
        mask = same & (keep[at, :] > 0.0)
        for pair in range(width // 128):
            here = pair * 128
            queries = qkv[at, here : here + 128]
            keys = qkv[at, width + here : width + here + 128]
            values = qkv[at, 2 * width + here : 2 * width + here + 128]
            d_context = dctx[at, here : here + 128]
            both_q = jnp.concatenate([queries * low, queries * high], axis=0)
            both_d = jnp.concatenate([d_context * low, d_context * high], axis=0)
            scores = jnp.where(mask, dot_nt(keys, both_q) * 0.125, masked_score)
            raised = jnp.exp(scores - jnp.max(scores, axis=0, keepdims=True))
            probs = raised / jnp.sum(raised, axis=0, keepdims=True)
            weighted = probs * dot_nt(values, both_d)
            d_scores = (weighted - probs * jnp.sum(weighted, axis=0, keepdims=True)).astype(bf16)
            d_both = dot_tn(d_scores, keys) * 0.125
            d_queries = jnp.where(low_f > 0.0, d_both[:128], d_both[128:])
            dqkv_ref[at, here : here + 128] = d_queries.astype(bf16)
            dqkv_ref[at, width + here : width + here + 128] = (dot(d_scores, both_q) * 0.125).astype(bf16)
            dqkv_ref[at, 2 * width + here : 2 * width + here + 128] = dot(probs.astype(bf16), both_d).astype(bf16)
        return carry

    lax.fori_loop(0, tokens // 128, block, 0)
    grads_ref[0:1, :] = jnp.sum(dqkv_ref[:, :width].astype(f32), axis=0, keepdims=True)
    grads_ref[1:2, :] = jnp.sum(dqkv_ref[:, 2 * width :].astype(f32), axis=0, keepdims=True)


def kernel_attention_grad(fs, info, hid, vec, ctx, dqkv, da, *refs):
    *vectors, up_bias, mine, theirs, held, block = refs
    width = hid.shape[1]
    scaled, _ = norm_parts(hid[...].astype(f32))
    turned = (scaled * vec[0:1, :] + vec[1:2, :]).astype(bf16).T
    for third in range(3):
        grad = dot(turned, dqkv[:, third * width : (third + 1) * width]).astype(bf16)
        for part in range(2):
            place = third * 2 + part
            put(info, place // 4, (place % 4, 0), grad[:, part * PIECE : (part + 1) * PIECE], mine, theirs)
    grad = dot(ctx[...], da[...]).astype(bf16)
    for part in range(2):
        put(info, 1, (2 + part, 0), grad[:, part * PIECE : (part + 1) * PIECE], mine, theirs)
    held[...] = jnp.zeros_like(held)
    row = 0
    for ref in vectors:
        held[row : row + ref.shape[0], :] = ref[...]
        row += ref.shape[0]
    for part in range(4):
        held[row + part : row + part + 1, :] = up_bias[:, part * width : (part + 1) * width]
    block[...] = jnp.zeros_like(block)
    step = width // fs
    for shard in range(fs):
        block[:, :step] = held[:, shard * step : (shard + 1) * step].astype(bf16)
        for spot in range(4):
            for ref in (mine, theirs):
                ref[spot, width + 16 * shard : width + 16 * (shard + 1), :] = block[...]


def kernel_input_back(dqkv, dh, hid, vec, w_att, out_ref, grads_ref):
    width = hid.shape[1]
    d_normed = dot_nt(dqkv[...], w_att[:, : 3 * width])
    scaled, inv = norm_parts(hid[...].astype(f32))
    out_ref[...] = dh[...] + norm_back(d_normed, scaled, inv, vec[0:1, :])
    grads_ref[0:1, :] = jnp.sum(d_normed * scaled, axis=0, keepdims=True)
    grads_ref[1:2, :] = jnp.sum(d_normed, axis=0, keepdims=True)


def renew_state(master, momentum, average, gradient):
    momentum_new = momentum_decay * momentum + gradient
    master_new = master - learn_rate * (gradient + momentum_decay * momentum_new)
    average_new = average_decay * average + (1.0 - average_decay) * master_new
    return (master_new, momentum_new, average_new, master_new.astype(bf16))


def kernel_renew(fs, column, skip, info, near, far, *refs):
    states, outs = refs[:3], refs[3 + skip : 7 + skip]
    *vectors, token, buf, new_f, new_h, in_sem, out_sem = refs[7 + skip :]
    rows = buf.shape[2]
    token[...] = jnp.zeros_like(token)
    if vectors:
        grad, *old = refs[3:7]
        new = renew_state(*(ref[...] for ref in old), grad[: old[0].shape[0], : old[0].shape[1]])
        for ref, value in zip(vectors, new):
            ref[...] = value

    def at(k):
        spot = info[3 + fs + k]
        if column is None:
            row, col = pl.multiple_of((spot % 4) * rows, 16), (spot // 4) * PIECE
        else:
            row, col = 0, (column + spot) * PIECE
        return pl.ds(row, rows), pl.ds(pl.multiple_of(col, 128), PIECE)

    def read(k, i):
        return pltpu.make_async_copy(states[i].at[at(k)], buf.at[k, i], in_sem.at[k, i])

    def write(k, i):
        source = new_h.at[k] if i == 3 else new_f.at[k, i]
        return pltpu.make_async_copy(source, outs[i].at[at(k)], out_sem.at[k, i])

    for k in range(GROUP):
        for i in range(3):
            read(k, i).start()
    for k in range(GROUP):
        for i in range(3):
            read(k, i).wait()
        source = far if k % 2 else near

        def step(index, carry):
            at = pl.ds(pl.multiple_of(index * 16, 16), 16)
            grad = source[pl.ds(pl.multiple_of(k // 2 * rows + index * 16, 16), 16), :].astype(f32)
            *new, half = renew_state(buf[k, 0, at], buf[k, 1, at], buf[k, 2, at], grad)
            for i in range(3):
                new_f[k, i, at] = new[i]
            new_h[k, at] = half
            return carry

        lax.fori_loop(0, rows // 16, step, 0, unroll=True)
        for i in range(4):
            write(k, i).start()
    for k in range(GROUP):
        for i in range(4):
            write(k, i).wait()


def renew(order, info, fs, rows, grads, master, momentum, average, column, earlier=(), vectors=()):
    skip = len(earlier) + len(order.last) + len(vectors)
    kinds = (f32, f32, f32, bf16)
    *outs, token = pl.pallas_call(
        functools.partial(kernel_renew, fs, column, skip),
        in_specs=[SMEM] + [VMEM] * 2 + [HBM] * 3 + [VMEM] * len(vectors) + [HBM] * len(earlier) + [ANY] * len(order.last),
        out_specs=[HBM] * 4 + [VMEM] * len(vectors) + [VMEM],
        out_shape=[shape(master.shape, kind) for kind in kinds]
        + [shape(vectors[1].shape, kind) for kind in kinds if vectors]
        + [shape((8, 128), f32)],
        scratch_shapes=[
            pltpu.VMEM((GROUP, 3, rows, PIECE), f32),
            pltpu.VMEM((GROUP, 3, rows, PIECE), f32),
            pltpu.VMEM((GROUP, rows, PIECE), bf16),
            pltpu.SemaphoreType.DMA((GROUP, 3)),
            pltpu.SemaphoreType.DMA((GROUP, 4)),
        ],
        input_output_aliases={6 + i: i for i in range(len(earlier))},
        compiler_params=pltpu.CompilerParams(vmem_limit_bytes=60 * 1024 * 1024),
        cost_estimate=order.weight(),
    )(info, *grads, master, momentum, average, *vectors, *earlier, *order.last)
    order.last = (token,)
    return outs


def flip(count, bit):
    return [(i, i ^ bit) for i in range(count)]


def send(value, axis, count, bit):
    return lax.ppermute(value, axis, flip(count, bit))


def kernel_pack(rows, *refs):
    *refs, own, near, piece = refs
    piece[...] = own[...]
    for j, ref in enumerate(refs):
        near[j * rows : (j + 1) * rows, :] = ref[:rows, :]


def kernel_cast(wide, down, out_a, out_b, out_c):
    cols = out_a.shape[1]
    out_a[...] = wide[:, :cols].astype(bf16)
    out_b[...] = wide[:, cols:].astype(bf16)
    out_c[...] = down[...].astype(bf16)


def kernel_join(*refs):
    *parts, out = refs
    row = 0
    for part in parts:
        out[row : row + part.shape[0], :] = part[...]
        row += part.shape[0]


def kernel_pack_first(fs, rows, info, own, *refs):
    *refs, near, vec, bias, wide = refs
    width = vec.shape[1]
    wide[...] = jnp.zeros_like(wide)
    total = jnp.zeros(vec.shape, f32)
    for j, ref in enumerate([own, *refs]):
        if j:
            near[(j - 1) * rows : j * rows, :] = ref[:rows, :]
        wide[:, :PIECE] = ref[rows:, :].astype(f32)
        total = total + pltpu.roll(wide[...], info[3 + j] * (width // fs), 1)
    vec[...] = total
    for row in range(4):
        bias[:, row * width : (row + 1) * width] = total[8 + row : 9 + row, :]


def kernel_sorted(rows, places, *refs):
    *parts, out = refs
    for part, of_part in zip(parts, places):
        for i, place in enumerate(of_part):
            out[place * rows : (place + 1) * rows, :] = part[i * rows : (i + 1) * rows, :]


def kernel_halves(over_x, over_y, first, second):
    cut = first.shape[0]
    first[...] = over_x[:cut, :]
    second[...] = over_y[cut:, :]


def kernel_copy(value, out):
    out[...] = value[...]


def total_of(left, right):
    return (left.astype(f32) + right.astype(f32)).astype(bf16)


def kernel_add_core(fs, rows, info, mine, came, *refs):
    to_x, to_y, keep_x, keep_y = refs
    step = to_x.shape[1] * 2 // fs
    x, y = info[info.shape[0] - 2], info[info.shape[0] - 1]
    for other in range(2):
        for ref, spot, first in (
            (to_x, other * 2 + (1 - x), 0),
            (to_y, (1 - y) * 2 + other, fs // 2),
            (keep_x, other * 2 + x, 0),
            (keep_y, y * 2 + other, fs // 2),
        ):
            for shard in range(fs // 2):
                at = pl.ds((first + shard) * rows, rows)
                ref[other, pl.ds(shard * step, rows), :] = total_of(mine[spot, at, :], came[spot, at, :])
                if step > rows:
                    at = pl.ds(fs * rows + (first + shard) * 16, 16)
                    ref[other, pl.ds(shard * step + rows, 16), :] = total_of(mine[spot, at, :], came[spot, at, :])


def kernel_add_first(info, keep_x, keep_y, came_x, came_y, to_y, to_x, left_x, left_y):
    x, y = info[info.shape[0] - 2], info[info.shape[0] - 1]
    to_y[...] = total_of(keep_x[1 - y], came_x[1 - y])
    to_x[...] = total_of(keep_y[1 - x], came_y[1 - x])
    left_x[...] = total_of(keep_x[y], came_x[y])
    left_y[...] = total_of(keep_y[x], came_y[x])


def kernel_add_second(fs, rows, info, left_x, left_y, came_y, came_x, *refs):
    *outs, own = refs
    half = left_x.shape[0]
    own[:half, :] = total_of(left_x[...], came_y[...])
    own[half:, :] = total_of(left_y[...], came_x[...])
    for j, ref in enumerate(outs):
        ref[...] = own[pl.ds(pl.multiple_of(info[3 + j] * rows, 16), rows), :]


def kernel_add_second_half(fs, rows, info, left_x, left_y, came_y, came_x, keep, give, own):
    half = left_x.shape[0]
    own[:half, :] = total_of(left_x[...], came_y[...])
    own[half:, :] = total_of(left_y[...], came_x[...])
    for j in range(fs):
        ref = give if j % 2 else keep
        block = own[pl.ds(pl.multiple_of(info[3 + j] * rows, 16), rows), :]
        ref[j // 2 * rows : (j // 2 + 1) * rows, :] = block


def kernel_fold(rows, keep, came, left, give):
    for j in range(keep.shape[0] // rows):
        ref = give if j % 2 else left
        at = slice(j * rows, (j + 1) * rows)
        ref[j // 2 * rows : (j // 2 + 1) * rows, :] = total_of(keep[at, :], came[at, :])


def kernel_add_z(fs, *refs):
    parts, (out, *vectors) = refs[:fs], refs[fs:]
    rows = out.shape[0]
    out[...] = sum(part[:rows, :].astype(f32) for part in parts).astype(bf16)
    for ref in vectors:
        ref[...] = sum(part[rows:, :].astype(f32) for part in parts)


class Reduction:
    def __init__(self, order, info, fs, dp, rows, mine, theirs):
        self.order, self.info, self.fs, self.dp, self.rows = order, info, fs, dp, rows
        self.width = mine.shape[1]
        mine, theirs = self.beyond(mine), self.beyond(theirs)
        self.mine = [mine, send(theirs, "dp", dp, 1)]

    def beyond(self, value):
        bit = GROUP
        while bit < self.dp:
            value = total_of(value, send(value, "dp", self.dp, bit))
            bit *= 2
        return value

    def core(self):
        rows, self.rows = self.rows, self.width // self.fs
        to_x, to_y, *self.keep = self.order(
            functools.partial(kernel_add_core, self.fs, rows),
            [SMEM] + [VMEM] * 2,
            [shape((2, self.width // 2, PIECE), bf16)] * 4,
            (self.info, *self.mine),
        )
        self.came = send(to_x, "dp", self.dp, 2), send(to_y, "dp", self.dp, 4)

    def first(self):
        half = self.width // 2
        to_y, to_x, *self.keep = self.order(
            kernel_add_first,
            [SMEM] + [VMEM] * 4,
            [shape((half, PIECE), bf16)] * 4,
            (self.info, *self.keep, *self.came),
            moved=3e6,
        )
        self.came = send(to_y, "dp", self.dp, 4), send(to_x, "dp", self.dp, 2)

    def second(self):
        parts = self.order(
            functools.partial(kernel_add_second, self.fs, self.rows),
            [SMEM] + [VMEM] * 4,
            [shape((self.rows, PIECE), bf16)] * self.fs,
            (self.info, *self.keep, *self.came),
            scratch=[pltpu.VMEM((self.width, PIECE), bf16)],
            moved=2e6,
        )
        self.came = [parts[0]] + [send(parts[j], "fsdp", self.fs, j) for j in range(1, self.fs)]

    def second_half(self):
        self.bit, count = 1, self.fs // 2
        keep, give = self.order(
            functools.partial(kernel_add_second_half, self.fs, self.rows),
            [SMEM] + [VMEM] * 4,
            [shape((count * self.rows, PIECE), bf16)] * 2,
            (self.info, *self.keep, *self.came),
            scratch=[pltpu.VMEM((self.width, PIECE), bf16)],
        )
        self.came = [keep, send(give, "fsdp", self.fs, 1)]

    def fold(self):
        while 2 * self.bit < self.fs:
            self.bit *= 2
            count = self.fs // self.bit // 2
            keep, give = self.order(
                functools.partial(kernel_fold, self.rows),
                [VMEM] * 2,
                [shape((count * self.rows, PIECE), bf16)] * 2,
                self.came,
            )
            self.came = [keep, send(give, "fsdp", self.fs, self.bit)]

    def line(self, grad_rows):
        count = len(self.came)
        extra = [shape((self.rows - grad_rows, PIECE), f32)] if self.rows > grad_rows else []
        piece, *self.vectors = self.order(
            functools.partial(kernel_add_z, count), [VMEM] * count, [shape((grad_rows, PIECE), bf16)] + extra, self.came
        )
        self.rows, self.piece = grad_rows, piece

    def share_first(self):
        self.came = [self.piece, send(self.piece, "dp", self.dp, 2)]

    def share_second(self):
        (pair,) = self.order(kernel_join, [VMEM] * 2, [shape((2 * self.rows, PIECE), bf16)], self.came)
        self.came = [pair, send(pair, "dp", self.dp, 4)]

    def share_all(self):
        self.came = [self.piece] + [send(self.piece, "dp", self.dp, k) for k in (2, 4, 6)]

    def share(self):
        (side,) = self.order(kernel_join, [VMEM] * len(self.came), [shape((4 * self.rows, PIECE), bf16)], self.came)
        self.pieces = side, send(side, "dp", self.dp, 1)


def merge_stats(group):
    top = functools.reduce(jnp.maximum, [top for top, _ in group])
    return top, sum(mass * jnp.exp(old - top) for old, mass in group)


def kernel_merge(*refs):
    *parts, out = refs
    top, mass = merge_stats([(part[0:1, :], part[1:2, :]) for part in parts])
    out[0:1, :] = top
    out[1:2, :] = mass


def kernel_turn(*refs):
    half = len(refs) // 2
    for value, out in zip(refs[:half], refs[half:]):
        out[...] = value[...].T


def body(
    fs,
    dp,
    hidden_in,
    lengths,
    images,
    labels,
    wide_master,
    down_master,
    vector_master,
    wide_momentum,
    down_momentum,
    vector_momentum,
    wide_average,
    down_average,
    vector_average,
):
    tokens, width = hidden_in.shape
    captions = lengths.shape[0]
    rows = wide_master.shape[0]
    hidden = wide_master.shape[1] - 4 * width
    rank, z = lax.axis_index("dp"), lax.axis_index("fsdp")
    core, x, y = rank % 2, rank // 2 % 2, rank // 4 % 2
    member = [rank ^ k for k in range(GROUP)]
    spots = [(m % 2) * 4 + (m // 4 % 2) * 2 + (m // 2 % 2) for m in member]
    info = jnp.stack([z, core, rank * fs + z] + [z ^ j for j in range(fs)] + spots + [rank, x, y]).astype(jnp.int32)

    place = jnp.arange(SEQ)
    keep = (place[None, :] < lengths[:, None]).astype(f32).reshape(tokens)
    valid, keep = keep[None, :], keep[:, None]
    lens = lengths.astype(f32)[:, None]

    order = Order(LIGHT)
    piece_shape = shape((rows, PIECE), bf16)
    near_shape = shape(((fs - 1) * rows, PIECE), bf16)

    def along_z(piece):
        return [send(piece, "fsdp", fs, j) for j in range(1, fs)]

    def pack(came, following):
        return order(
            functools.partial(kernel_pack, rows), [VMEM] * fs, [near_shape, piece_shape], (*came, following)
        )

    def hold(value):
        return order(kernel_copy, [VMEM], [shape(value.shape, bf16)], (value,))[0]

    def joined(parts):
        length = sum(part.shape[0] for part in parts)
        return order(kernel_join, [VMEM] * len(parts), [shape((length, PIECE), bf16)], parts)[0]

    def z_first(piece):
        bit = fs // 2
        return [piece, send(piece, "fsdp", fs, bit)], [[0], [bit]], bit

    def z_next(state):
        parts, places, bit = state
        while bit > 1:
            bit //= 2
            parts = parts + [send(joined(parts), "fsdp", fs, bit)]
            places = places + [[place ^ bit for of_part in places for place in of_part]]
        return parts, places

    def z_last(state):
        parts, places = state
        places = [[place - 1 for place in of_part] for of_part in places[1:]]
        return order(
            functools.partial(kernel_sorted, rows, places), [VMEM] * (len(parts) - 1), [near_shape], parts[1:]
        )[0]

    def over_plane(near):
        return near, send(near, "dp", dp, 2), send(near, "dp", dp, 4)

    def corner(near, over_x, over_y):
        cut = near.shape[0] // 32 * 16
        diag_a, diag_b = order(
            kernel_halves,
            [VMEM] * 2,
            [shape((cut, PIECE), bf16), shape((near.shape[0] - cut, PIECE), bf16)],
            (over_x, over_y),
        )
        return near, over_x, over_y, send(diag_a, "dp", dp, 4), send(diag_b, "dp", dp, 2)

    def join(parts):
        side = joined(parts)
        return side, send(side, "dp", dp, 1)

    spot = spots[0]

    def piece_of(values, column):
        return lax.dynamic_slice(values, (0, column + spot * PIECE), (rows, PIECE)).astype(bf16)

    total = captions * fs * dp
    tags = jnp.pad(jnp.stack([labels // 128, labels % 128]), ((0, PICTURE_TAGS - 2), (0, PIECE - captions)))
    picture = hold(jnp.concatenate([images[:, :PIECE], images[:, PIECE:], tags.astype(bf16)], axis=0))
    pictures = [picture, send(picture, "dp", dp, 2)]

    own_vec = jnp.pad(vector_master.astype(bf16), ((0, 4), (0, PIECE - vector_master.shape[1])))
    piece = hold(jnp.concatenate([piece_of(wide_master, 0), own_vec], axis=0))
    piece_b = piece_of(wide_master, 4 * width)
    piece_c = lax.dynamic_slice(down_master, ((spot % 4) * rows, (spot // 4) * PIECE), (rows, PIECE)).astype(bf16)
    came = along_z(piece)
    own_a, own_b, own_c = order(
        kernel_cast,
        [VMEM] * 2,
        [shape((rows, 4 * width), bf16), shape((rows, hidden), bf16), shape(down_master.shape, bf16)],
        (wide_master, down_master),
        limit=28,
    )
    bit = 4
    while bit < dp:
        picture = joined(pictures)
        pictures = [picture, send(picture, "dp", dp, bit)]
        bit *= 2
    near_a, vec, up_bias = order(
        functools.partial(kernel_pack_first, fs, rows),
        [SMEM] + [VMEM] * fs,
        [near_shape, shape((16, width), f32), shape((1, hidden), f32)],
        (info, piece, *came),
        scratch=[pltpu.VMEM((16, width), f32)],
    )
    plane_a = over_plane(near_a)
    came = along_z(hold(piece_b))
    corner_a = corner(*plane_a)
    near_b, piece_c = pack(came, piece_c)
    plane_b = over_plane(near_b)
    line_c = z_first(piece_c)
    parts_a = join(corner_a)
    gather_scratch = [pltpu.SemaphoreType.DMA((GROUP * fs * 2,))]

    qkv, w_att, w_out = order(
        functools.partial(kernel_qkv, fs, rows),
        [SMEM, VMEM, VMEM, VMEM] + [ANY] * 2,
        [shape((tokens, 3 * width), bf16), shape((width, 4 * width), bf16), shape((width, width), bf16)],
        (info, hidden_in, vec, own_a, *parts_a),
        scratch=gather_scratch,
        flops=6 * tokens * width * width,
        moved=10e6,
    )
    line_c = z_next(line_c)
    pictures = joined(pictures)
    pictures = [pictures] + along_z(pictures)
    corner_b = corner(*plane_b)
    ctx, h, second = order(
        kernel_attention,
        [VMEM] * 5,
        [shape((tokens, width), bf16), shape((tokens, width), f32), shape((tokens, width), bf16)],
        (hidden_in, valid, vec, qkv, w_out),
        flops=4 * tokens * width * width,
        moved=10e6,
    )
    near_c = z_last(line_c)
    plane_c = over_plane(near_c)
    parts_b = join(corner_b)
    slope, g, w_up = order(
        functools.partial(kernel_up, fs, rows),
        [SMEM, VMEM, VMEM, VMEM] + [ANY] * 2,
        [shape((tokens, hidden), bf16)] * 2 + [shape((width, hidden), bf16)],
        (info, second, up_bias, own_b, *parts_b),
        scratch=gather_scratch,
        flops=2 * tokens * width * hidden,
        moved=20e6,
    )
    corner_c = corner(*plane_c)
    pictures = join(pictures)
    parts_c = join(corner_c)
    block_out, pooled, inv, logits, stats, pictures, tags, w_down = order(
        functools.partial(kernel_down, fs, rows),
        [SMEM] + [VMEM] * 6 + [ANY] * 4,
        [
            shape((tokens, width), bf16),
            shape((captions, width), f32),
            shape((captions, 1), f32),
            shape((captions, total), f32),
            shape((2, total), f32),
            shape((total, width), bf16),
            shape((fs * dp * PICTURE_TAGS, 128), bf16),
            shape((hidden, width), bf16),
        ],
        (info, g, h, vec, lens, keep, own_c, *parts_c, *pictures),
        scratch=gather_scratch + [pltpu.SemaphoreType.DMA] * 2,
        limit=16 + (3 * total * width >> 20),
        flops=2 * tokens * width * hidden,
        moved=20e6,
    )

    tags = tags.reshape(fs * dp, PICTURE_TAGS, 128)[:, :2, :captions].astype(jnp.int32)
    all_labels = (tags[:, 0] * 128 + tags[:, 1]).reshape(1, total)

    def merged(came):
        return order(kernel_merge, [VMEM] * len(came), [shape((2, total), f32)], came, limit=16 + (total >> 9))[0]

    def turned(values):
        return order(kernel_turn, [VMEM] * len(values), [shape(value.shape[::-1], bf16) for value in values], values)

    came = [stats, send(stats, "dp", dp, 1)]
    g_turned = turned([g])[0]
    stats = merged(came)
    came = [stats] + [send(stats, "fsdp", fs, j) for j in range(1, fs)]
    (second_turned,) = turned([second])
    stats = merged(came)
    came = [stats] + [send(stats, "dp", dp, j) for j in range(2, dp, 2)]
    (ctx_turned,) = turned([ctx])
    stats = merged(came)

    halves = [shape((4, width, PIECE), bf16)] * 2
    dpl, dy, down_bias_grad, mine, theirs = order(
        functools.partial(kernel_loss, rows),
        [SMEM] + [VMEM] * 9,
        [shape((captions, width), f32), shape((tokens, width), bf16), shape((1, width), f32)] + halves,
        (info, logits, stats, all_labels, pictures, pooled, inv, lens, keep, g_turned),
        limit=16 + (3 * total * width >> 20),
        flops=2 * tokens * width * hidden,
        moved=10e6,
    )
    group_c = Reduction(order, info, fs, dp, rows, mine, theirs)
    du, up_bias_grad = order(
        kernel_gelu_back,
        [VMEM] * 3,
        [shape((tokens, hidden), bf16), shape((1, hidden), f32)],
        (dy, slope, w_down),
        flops=2 * tokens * width * hidden,
        moved=20e6,
    )
    group_c.core()
    mine, theirs = order(
        kernel_up_grad,
        [SMEM] + [VMEM] * 2,
        halves,
        (info, du, second_turned),
        flops=2 * tokens * width * hidden,
        moved=10e6,
    )
    group_b = Reduction(order, info, fs, dp, rows, mine, theirs)
    dh, da, dctx, mid_grads = order(
        kernel_mid_back,
        [VMEM] * 7,
        [
            shape((tokens, width), f32),
            shape((tokens, width), bf16),
            shape((tokens, width), bf16),
            shape((3, width), f32),
        ],
        (dpl, keep, du, h, vec, w_up, w_out),
        flops=10 * tokens * width * width,
        moved=20e6,
    )
    group_b.core()
    dqkv, bias_grads = order(
        kernel_attention_back,
        [VMEM] * 3,
        [shape((tokens, 3 * width), bf16), shape((2, width), f32)],
        (dctx, qkv, keep),
        flops=10 * tokens * width * width,
        moved=10e6,
    )
    input_grad, norm_grads = order(
        kernel_input_back,
        [VMEM] * 5,
        [shape((tokens, width), f32), shape((2, width), f32)],
        (dqkv, dh, hidden_in, vec, w_att),
        flops=6 * tokens * width * width,
        moved=10e6,
    )
    group_c.first()
    mine, theirs = order(
        functools.partial(kernel_attention_grad, fs),
        [SMEM] + [VMEM] * 10,
        [shape((4, width + 16 * fs, PIECE), bf16)] * 2,
        (info, hidden_in, vec, ctx_turned, dqkv, da, norm_grads, bias_grads, mid_grads, down_bias_grad, up_bias_grad),
        scratch=[pltpu.VMEM((16, width), f32), pltpu.VMEM((16, PIECE), bf16)],
        flops=8 * tokens * width * width,
        moved=10e6,
    )
    group_a = Reduction(order, info, fs, dp, rows, mine, theirs)
    group_b.first()
    group_c.second_half()
    group_a.core()
    group_c.fold()
    group_b.second_half()
    group_c.line(rows)
    group_a.first()
    group_c.share_first()
    group_b.fold()
    group_c.share_second()
    group_b.line(rows)
    group_b.share_first()
    group_a.second()
    group_c.share()
    group_b.share_second()
    down_state = renew(order, info, fs, rows, group_c.pieces, down_master, down_momentum, down_average, None)
    group_b.share()
    group_a.line(rows)
    group_a.share_all()
    vectors = (*group_a.vectors, vector_master, vector_momentum, vector_average)
    wide_state = renew(
        order, info, fs, rows, group_b.pieces, wide_master, wide_momentum, wide_average, GROUP, vectors=vectors
    )
    wide_state, vector_state = wide_state[:4], wide_state[4:]
    group_a.share()
    wide_state = renew(order, info, fs, rows, group_a.pieces, wide_master, wide_momentum, wide_average, 0, wide_state)

    return (
        block_out,
        input_grad,
        wide_state[0],
        down_state[0],
        vector_state[0],
        wide_state[1],
        down_state[1],
        vector_state[1],
        wide_state[2],
        down_state[2],
        vector_state[2],
        wide_state[3],
        down_state[3],
        vector_state[3],
    )


def solution(mesh):
    tokens = P(("dp", "fsdp"), None)
    each = P(("dp", "fsdp"))
    by_row = P("fsdp", None)
    by_col = P(None, "fsdp")
    states = (by_row, by_row, by_col)
    return jax.shard_map(
        functools.partial(body, mesh.shape["fsdp"], mesh.shape["dp"]),
        mesh=mesh,
        in_specs=(tokens, each, tokens, each) + states * 3,
        out_specs=(tokens, tokens) + states * 4,
        check_vma=False,
    )
```

```python
import functools

import jax
import jax.numpy as jnp
from jax import lax
from jax.experimental import pallas as pl
from jax.experimental.pallas import tpu as pltpu
from jax.sharding import PartitionSpec as P

HEADS = 12
SEQ = 16
PIECE = 384
GROUP = 8
PICTURE_TAGS = 16
LIGHT = (8, 22, 36, 41, 42, 43, 46)

norm_epsilon = 1e-06
masked_score = -1e30
learn_rate = 0.02
momentum_decay = 0.5
average_decay = 0.5
gelu_scale = 0.7978845608028654
gelu_cube = 0.044715

f32 = jnp.float32
bf16 = jnp.bfloat16
VMEM = pl.BlockSpec(memory_space=pltpu.VMEM)
SMEM = pl.BlockSpec(memory_space=pltpu.SMEM)
ANY = pl.BlockSpec(memory_space=pl.ANY)
HBM = pl.BlockSpec(memory_space=pltpu.HBM)
PARAMS = pltpu.CompilerParams(vmem_limit_bytes=32 * 1024 * 1024)


def dot(left, right):
    return lax.dot_general(left, right, (((1,), (0,)), ((), ())), preferred_element_type=f32)


def dot_nt(left, right):
    return lax.dot_general(left, right, (((1,), (1,)), ((), ())), preferred_element_type=f32)


def dot_tn(left, right):
    return lax.dot_general(left, right, (((0,), (0,)), ((), ())), preferred_element_type=f32)


def shape(dims, kind):
    return jax.ShapeDtypeStruct(dims, kind)


class Order:
    def __init__(self, light):
        self.last, self.light, self.count = (), light, 0

    def weight(self):
        self.count += 1
        return cost(1 if self.count - 1 in self.light else 10**11, 1)

    def __call__(self, kernel, in_specs, out_shape, args, after=(), out_specs=None, scratch=(), flops=0, moved=0, limit=16):
        after = [*self.last, *after]
        count, skip = len(in_specs), len(after)

        def run(*refs):
            kernel(*refs[:count], *refs[count + skip :])

        outs = pl.pallas_call(
            run,
            in_specs=list(in_specs) + [ANY] * skip,
            out_specs=out_specs or [VMEM] * len(out_shape),
            out_shape=out_shape,
            scratch_shapes=scratch,
            compiler_params=pltpu.CompilerParams(vmem_limit_bytes=limit * 1024 * 1024),
            cost_estimate=self.weight(),
        )(*args, *after)
        self.last = (min(outs, key=lambda value: value.size),)
        return outs


def cost(flops, moved):
    return pl.CostEstimate(flops=int(flops), bytes_accessed=int(moved), transcendentals=0)


def norm_parts(values):
    centre = values - jnp.mean(values, axis=-1, keepdims=True)
    inv = lax.rsqrt(jnp.mean(centre * centre, axis=-1, keepdims=True) + norm_epsilon)
    return centre * inv, inv


def norm_back(grad, scaled, inv, gain):
    d_scaled = grad * gain
    first = jnp.mean(d_scaled, axis=-1, keepdims=True)
    second = jnp.mean(d_scaled * scaled, axis=-1, keepdims=True)
    return inv * (d_scaled - first - scaled * second)


def piece_copies(info, fs, rows, sides, target, sems, is_down):
    copies = []
    for k in range(GROUP):
        for j in range(1, fs):
            shard = info[3 + j]
            place = info[3 + fs + k]
            row = shard * rows
            if is_down:
                row = row * 4 + (place % 4) * rows
                col = (place // 4) * PIECE
            else:
                col = place * PIECE
            first = ((k // 2) * (fs - 1) + j - 1) * rows
            copies.append(
                pltpu.make_async_copy(
                    sides[k % 2].at[pl.ds(first, rows), :],
                    target.at[pl.ds(pl.multiple_of(row, 16), rows), pl.ds(pl.multiple_of(col, 128), PIECE)],
                    sems.at[len(copies)],
                )
            )
    return copies


def picture_copies(info, fs, captions, sides, images, tags, image_sem, tag_sem):
    block = PICTURE_TAGS
    members = sides[0].shape[0] // (block + 2 * captions) // fs
    rank, z = info[info.shape[0] - 3], info[0]
    for side in range(2):
        for j in range(fs):
            for m in range(members):
                device = (rank ^ (2 * m + side)) * fs + (z ^ j)
                first = (j * members + m) * (block + 2 * captions)
                to = pl.ds(pl.multiple_of(device * captions, 16), captions)
                for half in range(2):
                    pltpu.make_async_copy(
                        sides[side].at[pl.ds(first + half * captions, captions), :],
                        images.at[to, pl.ds(half * PIECE, PIECE)],
                        image_sem,
                    ).start()
                pltpu.make_async_copy(
                    sides[side].at[pl.ds(first + 2 * captions, block), pl.ds(0, 128)],
                    tags.at[pl.ds(pl.multiple_of(device * block, 16), block), :],
                    tag_sem,
                ).start()


def attend_forward(queries, keys, values, mask, half_low, half_high):
    both_q = jnp.concatenate([queries * half_low, queries * half_high], axis=0)
    scores = jnp.where(mask, dot_nt(both_q, keys) * 0.125, masked_score)
    top = jnp.max(scores, axis=-1, keepdims=True)
    raised = jnp.exp(scores - top)
    probs = raised / jnp.sum(raised, axis=-1, keepdims=True)
    return both_q, probs


def lane_halves():
    lane = lax.broadcasted_iota(jnp.int32, (1, 128), 1)
    low = (lane < 64).astype(f32)
    return low, low.astype(bf16), (1.0 - low).astype(bf16)


def caption_mask(valid_row):
    row = lax.broadcasted_iota(jnp.int32, (256, 128), 0)
    col = lax.broadcasted_iota(jnp.int32, (256, 128), 1)
    same = ((row & 127) // SEQ) == (col // SEQ)
    return same & (valid_row > 0.0)


def kernel_qkv(fs, rows, info, hid, vec, own, near, far, qkv_ref, w, w_out, sems):
    width = hid.shape[1]
    copies = piece_copies(info, fs, rows, (near, far), w, sems, False)
    for copy in copies:
        copy.start()
    vecs = vec[...]
    scaled, _ = norm_parts(hid[...].astype(f32))
    normed = (scaled * vecs[0:1] + vecs[1:2]).astype(bf16)
    w[pl.ds(pl.multiple_of(info[0] * rows, 16), rows), :] = own[...]
    for copy in copies:
        copy.wait()
    for part in range(3):
        cols = pl.ds(part * width, width)
        value = dot(normed, w[:, cols])
        if part == 0:
            value = value + vecs[2:3]
        if part == 2:
            value = value + vecs[3:4]
        qkv_ref[:, cols] = value.astype(bf16)
    w_out[...] = w[:, 3 * width :]


def kernel_attention(hid, valid, vec, qkv, w, ctx_ref, h_ref, second_ref):
    tokens, width = hid.shape
    low_f, low, high = lane_halves()

    def block(index, carry):
        at = pl.ds(pl.multiple_of(index * 128, 128), 128)
        mask = caption_mask(valid[:, at])
        for pair in range(width // 128):
            here = pair * 128
            queries = qkv[at, here : here + 128]
            keys = qkv[at, width + here : width + here + 128]
            values = qkv[at, 2 * width + here : 2 * width + here + 128]
            _, probs = attend_forward(queries, keys, values, mask, low, high)
            context = dot(probs.astype(bf16), values)
            ctx_ref[at, here : here + 128] = jnp.where(low_f > 0.0, context[:128], context[128:]).astype(bf16)
        return carry

    lax.fori_loop(0, tokens // 128, block, 0)
    residual = hid[...].astype(f32) + (dot(ctx_ref[...], w[...]) + vec[4:5, :])
    h_ref[...] = residual
    scaled, _ = norm_parts(residual)
    second_ref[...] = (scaled * vec[5:6, :] + vec[6:7, :]).astype(bf16)


def kernel_up(fs, rows, info, second, bias, own, near, far, slope_ref, g_ref, w, sems):
    width, hidden = w.shape
    copies = piece_copies(info, fs, rows, (near, far), w, sems, False)
    for copy in copies:
        copy.start()
    w[pl.ds(pl.multiple_of(info[0] * rows, 16), rows), :] = own[...]
    for copy in copies:
        copy.wait()

    def block(index, carry):
        cols = pl.ds(index * 512, 512)
        value = dot(second[...], w[:, cols]) + bias[:, cols]
        square = value * value
        inner = jnp.tanh(gelu_scale * (value + gelu_cube * value * square))
        slope = 0.5 * (1.0 + inner) + (0.5 * gelu_scale) * value * (1.0 - inner * inner) * (1.0 + (3.0 * gelu_cube) * square)
        slope_ref[:, cols] = slope.astype(bf16)
        g_ref[:, cols] = (0.5 * value * (1.0 + inner)).astype(bf16)
        return carry

    for index in range(hidden // 512):
        block(index, 0)


def kernel_down(fs, rows, info, g, h, vec, lens, keep, own, near, far, near_images, far_images, *rest):
    out_ref, pooled_ref, inv_ref, logit_ref, stat_ref, images, tags, w, sems, image_sem, tag_sem = rest
    tokens, width = h.shape
    captions = tokens // SEQ
    copies = piece_copies(info, fs, rows, (near, far), w, sems, True)
    picture_copies(info, fs, captions, (near_images, far_images), images, tags, image_sem, tag_sem)
    for copy in copies:
        copy.start()
    w[pl.ds(pl.multiple_of(info[0] * 4 * rows, 16), 4 * rows), :] = own[...]
    for copy in copies:
        copy.wait()
    block_rows = h[...] + (dot(g[...], w[...]) + vec[7:8, :])
    out_ref[...] = block_rows.astype(bf16)
    pooled = jnp.sum((block_rows * keep[...]).reshape(captions, SEQ, width), axis=1) / lens[...]
    inv = lax.rsqrt(jnp.sum(pooled * pooled, axis=-1, keepdims=True) + norm_epsilon)
    pooled_ref[...] = pooled
    inv_ref[...] = inv
    texts = (pooled * inv).astype(bf16)
    pltpu.make_async_copy(images, images, image_sem).wait()
    pltpu.make_async_copy(tags, tags, tag_sem).wait()
    logits = dot_nt(texts, images[...])
    logit_ref[...] = logits
    top = jnp.max(logits, axis=0, keepdims=True)
    stat_ref[0:1, :] = top
    stat_ref[1:2, :] = jnp.sum(jnp.exp(logits - top), axis=0, keepdims=True)


def put(info, half, place, value, mine, theirs):
    rows = value.shape[0]

    @pl.when(info[1] == half)
    def _():
        mine[place[0], pl.ds(place[1], rows), :] = value

    @pl.when(info[1] != half)
    def _():
        theirs[place[0], pl.ds(place[1], rows), :] = value


def kernel_loss(rows, info, logits, stats, labels, images, pooled, inv, lens, keep, g, dpl_ref, dy_ref, bias_ref, mine, theirs):
    captions, width = pooled.shape
    hidden, tokens = g.shape
    lse = stats[0:1, :] + jnp.log(stats[1:2, :])
    number = lax.broadcasted_iota(jnp.int32, logits.shape, 0) + info[2] * captions
    onehot = (labels[...] == number).astype(f32)
    slopes = (jnp.exp(logits[...] - lse) - onehot).astype(bf16)
    text_grad = dot(slopes, images[...])
    pool, inv_v = pooled[...], inv[...]
    d_pooled = inv_v * text_grad - inv_v**3 * pool * jnp.sum(pool * text_grad, axis=-1, keepdims=True)
    dpl = d_pooled / lens[...]
    dpl_ref[...] = dpl
    d_out = jnp.broadcast_to(dpl[:, None, :], (captions, SEQ, width)).reshape(tokens, width) * keep[...]
    dy = d_out.astype(bf16)
    dy_ref[...] = dy
    bias_ref[...] = jnp.sum(dy.astype(f32), axis=0, keepdims=True)
    for part in range(hidden // width):
        grad = dot(g[part * width : (part + 1) * width, :], dy).astype(bf16)
        for sub in range(width // rows):
            first = part * width + sub * rows
            shard, quarter = first // (4 * rows), (first % (4 * rows)) // rows
            for half in range(2):
                value = grad[sub * rows : (sub + 1) * rows, half * PIECE : (half + 1) * PIECE]
                put(info, half, (quarter, shard * rows), value, mine, theirs)


def kernel_gelu_back(dy, slope, w_down, du_ref, bias_ref):
    tokens, hidden = slope.shape
    for part in range(hidden // 768):
        cols = slice(part * 768, (part + 1) * 768)
        du = (dot_nt(dy[...], w_down[cols, :]) * slope[:, cols].astype(f32)).astype(bf16)
        du_ref[:, cols] = du
        bias_ref[:, cols] = jnp.sum(du.astype(f32), axis=0, keepdims=True)


def kernel_up_grad(info, du, second, mine, theirs):
    turned = second[...]
    for pair in range(du.shape[1] // PIECE // 2):
        grad = dot(turned, du[:, 2 * pair * PIECE : 2 * (pair + 1) * PIECE]).astype(bf16)
        for part in range(2):
            place = 2 * pair + part
            put(info, place // 4, (place % 4, 0), grad[:, part * PIECE : (part + 1) * PIECE], mine, theirs)


def kernel_mid_back(dpl, keep, du, h, vec, w_up, w_out, dh_ref, da_ref, dctx_ref, grads_ref):
    tokens, width = h.shape
    captions = tokens // SEQ
    d_second = dot_nt(du[...], w_up[...])
    scaled, inv = norm_parts(h[...])
    d_out = jnp.broadcast_to(dpl[...][:, None, :], (captions, SEQ, width)).reshape(tokens, width) * keep[...]
    dh = d_out + norm_back(d_second, scaled, inv, vec[5:6, :])
    dh_ref[...] = dh
    da = dh.astype(bf16)
    da_ref[...] = da
    grads_ref[0:1, :] = jnp.sum(da.astype(f32), axis=0, keepdims=True)
    grads_ref[1:2, :] = jnp.sum(d_second * scaled, axis=0, keepdims=True)
    grads_ref[2:3, :] = jnp.sum(d_second, axis=0, keepdims=True)
    dctx_ref[...] = dot_nt(da, w_out[...]).astype(bf16)


def kernel_attention_back(dctx, qkv, keep, dqkv_ref, grads_ref):
    tokens, width = dctx.shape
    low_f, low, high = lane_halves()
    row = lax.broadcasted_iota(jnp.int32, (128, 256), 0)
    col = lax.broadcasted_iota(jnp.int32, (128, 256), 1)
    same = (row // SEQ) == ((col & 127) // SEQ)

    def block(index, carry):
        at = pl.ds(pl.multiple_of(index * 128, 128), 128)
        mask = same & (keep[at, :] > 0.0)
        for pair in range(width // 128):
            here = pair * 128
            queries = qkv[at, here : here + 128]
            keys = qkv[at, width + here : width + here + 128]
            values = qkv[at, 2 * width + here : 2 * width + here + 128]
            d_context = dctx[at, here : here + 128]
            both_q = jnp.concatenate([queries * low, queries * high], axis=0)
            both_d = jnp.concatenate([d_context * low, d_context * high], axis=0)
            scores = jnp.where(mask, dot_nt(keys, both_q) * 0.125, masked_score)
            raised = jnp.exp(scores - jnp.max(scores, axis=0, keepdims=True))
            probs = raised / jnp.sum(raised, axis=0, keepdims=True)
            weighted = probs * dot_nt(values, both_d)
            d_scores = (weighted - probs * jnp.sum(weighted, axis=0, keepdims=True)).astype(bf16)
            d_both = dot_tn(d_scores, keys) * 0.125
            d_queries = jnp.where(low_f > 0.0, d_both[:128], d_both[128:])
            dqkv_ref[at, here : here + 128] = d_queries.astype(bf16)
            dqkv_ref[at, width + here : width + here + 128] = (dot(d_scores, both_q) * 0.125).astype(bf16)
            dqkv_ref[at, 2 * width + here : 2 * width + here + 128] = dot(probs.astype(bf16), both_d).astype(bf16)
        return carry

    lax.fori_loop(0, tokens // 128, block, 0)
    grads_ref[0:1, :] = jnp.sum(dqkv_ref[:, :width].astype(f32), axis=0, keepdims=True)
    grads_ref[1:2, :] = jnp.sum(dqkv_ref[:, 2 * width :].astype(f32), axis=0, keepdims=True)


def kernel_attention_grad(fs, info, hid, vec, ctx, dqkv, da, *refs):
    *vectors, up_bias, mine, theirs, held, block = refs
    width = hid.shape[1]
    scaled, _ = norm_parts(hid[...].astype(f32))
    turned = (scaled * vec[0:1, :] + vec[1:2, :]).astype(bf16).T
    for third in range(3):
        grad = dot(turned, dqkv[:, third * width : (third + 1) * width]).astype(bf16)
        for part in range(2):
            place = third * 2 + part
            put(info, place // 4, (place % 4, 0), grad[:, part * PIECE : (part + 1) * PIECE], mine, theirs)
    grad = dot(ctx[...], da[...]).astype(bf16)
    for part in range(2):
        put(info, 1, (2 + part, 0), grad[:, part * PIECE : (part + 1) * PIECE], mine, theirs)
    held[...] = jnp.zeros_like(held)
    row = 0
    for ref in vectors:
        held[row : row + ref.shape[0], :] = ref[...]
        row += ref.shape[0]
    for part in range(4):
        held[row + part : row + part + 1, :] = up_bias[:, part * width : (part + 1) * width]
    block[...] = jnp.zeros_like(block)
    step = width // fs
    for shard in range(fs):
        block[:, :step] = held[:, shard * step : (shard + 1) * step].astype(bf16)
        for spot in range(4):
            for ref in (mine, theirs):
                ref[spot, width + 16 * shard : width + 16 * (shard + 1), :] = block[...]


def kernel_input_back(dqkv, dh, hid, vec, w_att, out_ref, grads_ref):
    width = hid.shape[1]
    d_normed = dot_nt(dqkv[...], w_att[:, : 3 * width])
    scaled, inv = norm_parts(hid[...].astype(f32))
    out_ref[...] = dh[...] + norm_back(d_normed, scaled, inv, vec[0:1, :])
    grads_ref[0:1, :] = jnp.sum(d_normed * scaled, axis=0, keepdims=True)
    grads_ref[1:2, :] = jnp.sum(d_normed, axis=0, keepdims=True)


def renew_state(master, momentum, average, gradient):
    momentum_new = momentum_decay * momentum + gradient
    master_new = master - learn_rate * (gradient + momentum_decay * momentum_new)
    average_new = average_decay * average + (1.0 - average_decay) * master_new
    return (master_new, momentum_new, average_new, master_new.astype(bf16))


def kernel_renew(fs, column, skip, info, near, far, *refs):
    states, outs = refs[:3], refs[3 + skip : 7 + skip]
    *vectors, token, buf, new_f, new_h, in_sem, out_sem = refs[7 + skip :]
    rows = buf.shape[2]
    token[...] = jnp.zeros_like(token)
    if vectors:
        grad, *old = refs[3:7]
        new = renew_state(*(ref[...] for ref in old), grad[: old[0].shape[0], : old[0].shape[1]])
        for ref, value in zip(vectors, new):
            ref[...] = value

    def at(k):
        spot = info[3 + fs + k]
        if column is None:
            row, col = pl.multiple_of((spot % 4) * rows, 16), (spot // 4) * PIECE
        else:
            row, col = 0, (column + spot) * PIECE
        return pl.ds(row, rows), pl.ds(pl.multiple_of(col, 128), PIECE)

    def read(k, i):
        return pltpu.make_async_copy(states[i].at[at(k)], buf.at[k, i], in_sem.at[k, i])

    def write(k, i):
        source = new_h.at[k] if i == 3 else new_f.at[k, i]
        return pltpu.make_async_copy(source, outs[i].at[at(k)], out_sem.at[k, i])

    for k in range(GROUP):
        for i in range(3):
            read(k, i).start()
    for k in range(GROUP):
        for i in range(3):
            read(k, i).wait()
        source = far if k % 2 else near

        def step(index, carry):
            at = pl.ds(pl.multiple_of(index * 16, 16), 16)
            grad = source[pl.ds(pl.multiple_of(k // 2 * rows + index * 16, 16), 16), :].astype(f32)
            *new, half = renew_state(buf[k, 0, at], buf[k, 1, at], buf[k, 2, at], grad)
            for i in range(3):
                new_f[k, i, at] = new[i]
            new_h[k, at] = half
            return carry

        lax.fori_loop(0, rows // 16, step, 0, unroll=True)
        for i in range(4):
            write(k, i).start()
    for k in range(GROUP):
        for i in range(4):
            write(k, i).wait()


def renew(order, info, fs, rows, grads, master, momentum, average, column, earlier=(), vectors=()):
    skip = len(earlier) + len(order.last) + len(vectors)
    kinds = (f32, f32, f32, bf16)
    *outs, token = pl.pallas_call(
        functools.partial(kernel_renew, fs, column, skip),
        in_specs=[SMEM] + [VMEM] * 2 + [HBM] * 3 + [VMEM] * len(vectors) + [HBM] * len(earlier) + [ANY] * len(order.last),
        out_specs=[HBM] * 4 + [VMEM] * len(vectors) + [VMEM],
        out_shape=[shape(master.shape, kind) for kind in kinds]
        + [shape(vectors[1].shape, kind) for kind in kinds if vectors]
        + [shape((8, 128), f32)],
        scratch_shapes=[
            pltpu.VMEM((GROUP, 3, rows, PIECE), f32),
            pltpu.VMEM((GROUP, 3, rows, PIECE), f32),
            pltpu.VMEM((GROUP, rows, PIECE), bf16),
            pltpu.SemaphoreType.DMA((GROUP, 3)),
            pltpu.SemaphoreType.DMA((GROUP, 4)),
        ],
        input_output_aliases={6 + i: i for i in range(len(earlier))},
        compiler_params=pltpu.CompilerParams(vmem_limit_bytes=60 * 1024 * 1024),
        cost_estimate=order.weight(),
    )(info, *grads, master, momentum, average, *vectors, *earlier, *order.last)
    order.last = (token,)
    return outs


def flip(count, bit):
    return [(i, i ^ bit) for i in range(count)]


def send(value, axis, count, bit):
    return lax.ppermute(value, axis, flip(count, bit))


def kernel_pack(rows, *refs):
    *refs, own, near, piece = refs
    piece[...] = own[...]
    for j, ref in enumerate(refs):
        near[j * rows : (j + 1) * rows, :] = ref[:rows, :]


def kernel_cast(wide, down, out_a, out_b, out_c):
    cols = out_a.shape[1]
    out_a[...] = wide[:, :cols].astype(bf16)
    out_b[...] = wide[:, cols:].astype(bf16)
    out_c[...] = down[...].astype(bf16)


def kernel_join(*refs):
    *parts, out = refs
    row = 0
    for part in parts:
        out[row : row + part.shape[0], :] = part[...]
        row += part.shape[0]


def kernel_pack_first(fs, rows, info, own, *refs):
    *refs, near, vec, bias, wide = refs
    width = vec.shape[1]
    wide[...] = jnp.zeros_like(wide)
    total = jnp.zeros(vec.shape, f32)
    for j, ref in enumerate([own, *refs]):
        if j:
            near[(j - 1) * rows : j * rows, :] = ref[:rows, :]
        wide[:, :PIECE] = ref[rows:, :].astype(f32)
        total = total + pltpu.roll(wide[...], info[3 + j] * (width // fs), 1)
    vec[...] = total
    for row in range(4):
        bias[:, row * width : (row + 1) * width] = total[8 + row : 9 + row, :]


def kernel_sorted(rows, places, *refs):
    *parts, out = refs
    for part, of_part in zip(parts, places):
        for i, place in enumerate(of_part):
            out[place * rows : (place + 1) * rows, :] = part[i * rows : (i + 1) * rows, :]


def kernel_halves(over_x, over_y, first, second):
    cut = first.shape[0]
    first[...] = over_x[:cut, :]
    second[...] = over_y[cut:, :]


def kernel_copy(value, out):
    out[...] = value[...]


def total_of(left, right):
    return (left.astype(f32) + right.astype(f32)).astype(bf16)


def kernel_add_core(fs, rows, info, mine, came, *refs):
    to_x, to_y, keep_x, keep_y = refs
    step = to_x.shape[1] * 2 // fs
    x, y = info[info.shape[0] - 2], info[info.shape[0] - 1]
    for other in range(2):
        for ref, spot, first in (
            (to_x, other * 2 + (1 - x), 0),
            (to_y, (1 - y) * 2 + other, fs // 2),
            (keep_x, other * 2 + x, 0),
            (keep_y, y * 2 + other, fs // 2),
        ):
            for shard in range(fs // 2):
                at = pl.ds((first + shard) * rows, rows)
                ref[other, pl.ds(shard * step, rows), :] = total_of(mine[spot, at, :], came[spot, at, :])
                if step > rows:
                    at = pl.ds(fs * rows + (first + shard) * 16, 16)
                    ref[other, pl.ds(shard * step + rows, 16), :] = total_of(mine[spot, at, :], came[spot, at, :])


def kernel_add_first(info, keep_x, keep_y, came_x, came_y, to_y, to_x, left_x, left_y):
    x, y = info[info.shape[0] - 2], info[info.shape[0] - 1]
    to_y[...] = total_of(keep_x[1 - y], came_x[1 - y])
    to_x[...] = total_of(keep_y[1 - x], came_y[1 - x])
    left_x[...] = total_of(keep_x[y], came_x[y])
    left_y[...] = total_of(keep_y[x], came_y[x])


def kernel_add_second(fs, rows, info, left_x, left_y, came_y, came_x, *refs):
    *outs, own = refs
    half = left_x.shape[0]
    own[:half, :] = total_of(left_x[...], came_y[...])
    own[half:, :] = total_of(left_y[...], came_x[...])
    for j, ref in enumerate(outs):
        ref[...] = own[pl.ds(pl.multiple_of(info[3 + j] * rows, 16), rows), :]


def kernel_add_second_half(fs, rows, info, left_x, left_y, came_y, came_x, keep, give, own):
    half = left_x.shape[0]
    own[:half, :] = total_of(left_x[...], came_y[...])
    own[half:, :] = total_of(left_y[...], came_x[...])
    for j in range(fs):
        ref = give if j % 2 else keep
        block = own[pl.ds(pl.multiple_of(info[3 + j] * rows, 16), rows), :]
        ref[j // 2 * rows : (j // 2 + 1) * rows, :] = block


def kernel_fold(rows, keep, came, left, give):
    for j in range(keep.shape[0] // rows):
        ref = give if j % 2 else left
        at = slice(j * rows, (j + 1) * rows)
        ref[j // 2 * rows : (j // 2 + 1) * rows, :] = total_of(keep[at, :], came[at, :])


def kernel_add_z(fs, *refs):
    parts, (out, *vectors) = refs[:fs], refs[fs:]
    rows = out.shape[0]
    out[...] = sum(part[:rows, :].astype(f32) for part in parts).astype(bf16)
    for ref in vectors:
        ref[...] = sum(part[rows:, :].astype(f32) for part in parts)


class Reduction:
    def __init__(self, order, info, fs, dp, rows, mine, theirs):
        self.order, self.info, self.fs, self.dp, self.rows = order, info, fs, dp, rows
        self.width = mine.shape[1]
        mine, theirs = self.beyond(mine), self.beyond(theirs)
        self.mine = [mine, send(theirs, "dp", dp, 1)]

    def beyond(self, value):
        bit = GROUP
        while bit < self.dp:
            value = total_of(value, send(value, "dp", self.dp, bit))
            bit *= 2
        return value

    def core(self):
        rows, self.rows = self.rows, self.width // self.fs
        to_x, to_y, *self.keep = self.order(
            functools.partial(kernel_add_core, self.fs, rows),
            [SMEM] + [VMEM] * 2,
            [shape((2, self.width // 2, PIECE), bf16)] * 4,
            (self.info, *self.mine),
        )
        self.came = send(to_x, "dp", self.dp, 2), send(to_y, "dp", self.dp, 4)

    def first(self):
        half = self.width // 2
        to_y, to_x, *self.keep = self.order(
            kernel_add_first,
            [SMEM] + [VMEM] * 4,
            [shape((half, PIECE), bf16)] * 4,
            (self.info, *self.keep, *self.came),
            moved=3e6,
        )
        self.came = send(to_y, "dp", self.dp, 4), send(to_x, "dp", self.dp, 2)

    def second(self):
        parts = self.order(
            functools.partial(kernel_add_second, self.fs, self.rows),
            [SMEM] + [VMEM] * 4,
            [shape((self.rows, PIECE), bf16)] * self.fs,
            (self.info, *self.keep, *self.came),
            scratch=[pltpu.VMEM((self.width, PIECE), bf16)],
            moved=2e6,
        )
        self.came = [parts[0]] + [send(parts[j], "fsdp", self.fs, j) for j in range(1, self.fs)]

    def second_half(self):
        self.bit, count = 1, self.fs // 2
        keep, give = self.order(
            functools.partial(kernel_add_second_half, self.fs, self.rows),
            [SMEM] + [VMEM] * 4,
            [shape((count * self.rows, PIECE), bf16)] * 2,
            (self.info, *self.keep, *self.came),
            scratch=[pltpu.VMEM((self.width, PIECE), bf16)],
        )
        self.came = [keep, send(give, "fsdp", self.fs, 1)]

    def fold(self):
        while 2 * self.bit < self.fs:
            self.bit *= 2
            count = self.fs // self.bit // 2
            keep, give = self.order(
                functools.partial(kernel_fold, self.rows),
                [VMEM] * 2,
                [shape((count * self.rows, PIECE), bf16)] * 2,
                self.came,
            )
            self.came = [keep, send(give, "fsdp", self.fs, self.bit)]

    def line(self, grad_rows):
        count = len(self.came)
        extra = [shape((self.rows - grad_rows, PIECE), f32)] if self.rows > grad_rows else []
        piece, *self.vectors = self.order(
            functools.partial(kernel_add_z, count), [VMEM] * count, [shape((grad_rows, PIECE), bf16)] + extra, self.came
        )
        self.rows, self.piece = grad_rows, piece

    def share_first(self):
        self.came = [self.piece, send(self.piece, "dp", self.dp, 2)]

    def share_second(self):
        (pair,) = self.order(kernel_join, [VMEM] * 2, [shape((2 * self.rows, PIECE), bf16)], self.came)
        self.came = [pair, send(pair, "dp", self.dp, 4)]

    def share_all(self):
        self.came = [self.piece] + [send(self.piece, "dp", self.dp, k) for k in (2, 4, 6)]

    def share(self):
        (side,) = self.order(kernel_join, [VMEM] * len(self.came), [shape((4 * self.rows, PIECE), bf16)], self.came)
        self.pieces = side, send(side, "dp", self.dp, 1)


def merge_stats(group):
    top = functools.reduce(jnp.maximum, [top for top, _ in group])
    return top, sum(mass * jnp.exp(old - top) for old, mass in group)


def kernel_merge(*refs):
    *parts, out = refs
    top, mass = merge_stats([(part[0:1, :], part[1:2, :]) for part in parts])
    out[0:1, :] = top
    out[1:2, :] = mass


def kernel_turn(*refs):
    half = len(refs) // 2
    for value, out in zip(refs[:half], refs[half:]):
        out[...] = value[...].T


def body(
    fs,
    dp,
    hidden_in,
    lengths,
    images,
    labels,
    wide_master,
    down_master,
    vector_master,
    wide_momentum,
    down_momentum,
    vector_momentum,
    wide_average,
    down_average,
    vector_average,
):
    tokens, width = hidden_in.shape
    captions = lengths.shape[0]
    rows = wide_master.shape[0]
    hidden = wide_master.shape[1] - 4 * width
    rank, z = lax.axis_index("dp"), lax.axis_index("fsdp")
    core, x, y = rank % 2, rank // 2 % 2, rank // 4 % 2
    member = [rank ^ k for k in range(GROUP)]
    spots = [(m % 2) * 4 + (m // 4 % 2) * 2 + (m // 2 % 2) for m in member]
    info = jnp.stack([z, core, rank * fs + z] + [z ^ j for j in range(fs)] + spots + [rank, x, y]).astype(jnp.int32)

    place = jnp.arange(SEQ)
    keep = (place[None, :] < lengths[:, None]).astype(f32).reshape(tokens)
    valid, keep = keep[None, :], keep[:, None]
    lens = lengths.astype(f32)[:, None]

    order = Order(LIGHT)
    piece_shape = shape((rows, PIECE), bf16)
    near_shape = shape(((fs - 1) * rows, PIECE), bf16)

    def along_z(piece):
        return [send(piece, "fsdp", fs, j) for j in range(1, fs)]

    def pack(came, following):
        return order(
            functools.partial(kernel_pack, rows), [VMEM] * fs, [near_shape, piece_shape], (*came, following)
        )

    def hold(value):
        return order(kernel_copy, [VMEM], [shape(value.shape, bf16)], (value,))[0]

    def joined(parts):
        length = sum(part.shape[0] for part in parts)
        return order(kernel_join, [VMEM] * len(parts), [shape((length, PIECE), bf16)], parts)[0]

    def z_first(piece):
        bit = fs // 2
        return [piece, send(piece, "fsdp", fs, bit)], [[0], [bit]], bit

    def z_next(state):
        parts, places, bit = state
        while bit > 1:
            bit //= 2
            parts = parts + [send(joined(parts), "fsdp", fs, bit)]
            places = places + [[place ^ bit for of_part in places for place in of_part]]
        return parts, places

    def z_last(state):
        parts, places = state
        places = [[place - 1 for place in of_part] for of_part in places[1:]]
        return order(
            functools.partial(kernel_sorted, rows, places), [VMEM] * (len(parts) - 1), [near_shape], parts[1:]
        )[0]

    def over_plane(near):
        return near, send(near, "dp", dp, 2), send(near, "dp", dp, 4)

    def corner(near, over_x, over_y):
        cut = near.shape[0] // 32 * 16
        diag_a, diag_b = order(
            kernel_halves,
            [VMEM] * 2,
            [shape((cut, PIECE), bf16), shape((near.shape[0] - cut, PIECE), bf16)],
            (over_x, over_y),
        )
        return near, over_x, over_y, send(diag_a, "dp", dp, 4), send(diag_b, "dp", dp, 2)

    def join(parts):
        side = joined(parts)
        return side, send(side, "dp", dp, 1)

    spot = spots[0]

    def piece_of(values, column):
        return lax.dynamic_slice(values, (0, column + spot * PIECE), (rows, PIECE)).astype(bf16)

    total = captions * fs * dp
    tags = jnp.pad(jnp.stack([labels // 128, labels % 128]), ((0, PICTURE_TAGS - 2), (0, PIECE - captions)))
    picture = hold(jnp.concatenate([images[:, :PIECE], images[:, PIECE:], tags.astype(bf16)], axis=0))
    pictures = [picture, send(picture, "dp", dp, 2)]

    own_vec = jnp.pad(vector_master.astype(bf16), ((0, 4), (0, PIECE - vector_master.shape[1])))
    piece = hold(jnp.concatenate([piece_of(wide_master, 0), own_vec], axis=0))
    piece_b = piece_of(wide_master, 4 * width)
    piece_c = lax.dynamic_slice(down_master, ((spot % 4) * rows, (spot // 4) * PIECE), (rows, PIECE)).astype(bf16)
    came = along_z(piece)
    own_a, own_b, own_c = order(
        kernel_cast,
        [VMEM] * 2,
        [shape((rows, 4 * width), bf16), shape((rows, hidden), bf16), shape(down_master.shape, bf16)],
        (wide_master, down_master),
        limit=28,
    )
    bit = 4
    while bit < dp:
        picture = joined(pictures)
        pictures = [picture, send(picture, "dp", dp, bit)]
        bit *= 2
    near_a, vec, up_bias = order(
        functools.partial(kernel_pack_first, fs, rows),
        [SMEM] + [VMEM] * fs,
        [near_shape, shape((16, width), f32), shape((1, hidden), f32)],
        (info, piece, *came),
        scratch=[pltpu.VMEM((16, width), f32)],
    )
    plane_a = over_plane(near_a)
    came = along_z(hold(piece_b))
    corner_a = corner(*plane_a)
    near_b, piece_c = pack(came, piece_c)
    plane_b = over_plane(near_b)
    line_c = z_first(piece_c)
    parts_a = join(corner_a)
    gather_scratch = [pltpu.SemaphoreType.DMA((GROUP * fs * 2,))]

    qkv, w_att, w_out = order(
        functools.partial(kernel_qkv, fs, rows),
        [SMEM, VMEM, VMEM, VMEM] + [ANY] * 2,
        [shape((tokens, 3 * width), bf16), shape((width, 4 * width), bf16), shape((width, width), bf16)],
        (info, hidden_in, vec, own_a, *parts_a),
        scratch=gather_scratch,
        flops=6 * tokens * width * width,
        moved=10e6,
    )
    line_c = z_next(line_c)
    pictures = joined(pictures)
    pictures = [pictures] + along_z(pictures)
    corner_b = corner(*plane_b)
    ctx, h, second = order(
        kernel_attention,
        [VMEM] * 5,
        [shape((tokens, width), bf16), shape((tokens, width), f32), shape((tokens, width), bf16)],
        (hidden_in, valid, vec, qkv, w_out),
        flops=4 * tokens * width * width,
        moved=10e6,
    )
    near_c = z_last(line_c)
    plane_c = over_plane(near_c)
    parts_b = join(corner_b)
    slope, g, w_up = order(
        functools.partial(kernel_up, fs, rows),
        [SMEM, VMEM, VMEM, VMEM] + [ANY] * 2,
        [shape((tokens, hidden), bf16)] * 2 + [shape((width, hidden), bf16)],
        (info, second, up_bias, own_b, *parts_b),
        scratch=gather_scratch,
        flops=2 * tokens * width * hidden,
        moved=20e6,
    )
    corner_c = corner(*plane_c)
    pictures = join(pictures)
    parts_c = join(corner_c)
    block_out, pooled, inv, logits, stats, pictures, tags, w_down = order(
        functools.partial(kernel_down, fs, rows),
        [SMEM] + [VMEM] * 6 + [ANY] * 4,
        [
            shape((tokens, width), bf16),
            shape((captions, width), f32),
            shape((captions, 1), f32),
            shape((captions, total), f32),
            shape((2, total), f32),
            shape((total, width), bf16),
            shape((fs * dp * PICTURE_TAGS, 128), bf16),
            shape((hidden, width), bf16),
        ],
        (info, g, h, vec, lens, keep, own_c, *parts_c, *pictures),
        scratch=gather_scratch + [pltpu.SemaphoreType.DMA] * 2,
        limit=16 + (3 * total * width >> 20),
        flops=2 * tokens * width * hidden,
        moved=20e6,
    )

    tags = tags.reshape(fs * dp, PICTURE_TAGS, 128)[:, :2, :captions].astype(jnp.int32)
    all_labels = (tags[:, 0] * 128 + tags[:, 1]).reshape(1, total)

    def merged(came):
        return order(kernel_merge, [VMEM] * len(came), [shape((2, total), f32)], came, limit=16 + (total >> 9))[0]

    def turned(values):
        return order(kernel_turn, [VMEM] * len(values), [shape(value.shape[::-1], bf16) for value in values], values)

    came = [stats, send(stats, "dp", dp, 1)]
    g_turned = turned([g])[0]
    stats = merged(came)
    came = [stats] + [send(stats, "fsdp", fs, j) for j in range(1, fs)]
    (second_turned,) = turned([second])
    stats = merged(came)
    came = [stats] + [send(stats, "dp", dp, j) for j in range(2, dp, 2)]
    (ctx_turned,) = turned([ctx])
    stats = merged(came)

    halves = [shape((4, width, PIECE), bf16)] * 2
    dpl, dy, down_bias_grad, mine, theirs = order(
        functools.partial(kernel_loss, rows),
        [SMEM] + [VMEM] * 9,
        [shape((captions, width), f32), shape((tokens, width), bf16), shape((1, width), f32)] + halves,
        (info, logits, stats, all_labels, pictures, pooled, inv, lens, keep, g_turned),
        limit=16 + (3 * total * width >> 20),
        flops=2 * tokens * width * hidden,
        moved=10e6,
    )
    group_c = Reduction(order, info, fs, dp, rows, mine, theirs)
    du, up_bias_grad = order(
        kernel_gelu_back,
        [VMEM] * 3,
        [shape((tokens, hidden), bf16), shape((1, hidden), f32)],
        (dy, slope, w_down),
        flops=2 * tokens * width * hidden,
        moved=20e6,
    )
    group_c.core()
    mine, theirs = order(
        kernel_up_grad,
        [SMEM] + [VMEM] * 2,
        halves,
        (info, du, second_turned),
        flops=2 * tokens * width * hidden,
        moved=10e6,
    )
    group_b = Reduction(order, info, fs, dp, rows, mine, theirs)
    dh, da, dctx, mid_grads = order(
        kernel_mid_back,
        [VMEM] * 7,
        [
            shape((tokens, width), f32),
            shape((tokens, width), bf16),
            shape((tokens, width), bf16),
            shape((3, width), f32),
        ],
        (dpl, keep, du, h, vec, w_up, w_out),
        flops=10 * tokens * width * width,
        moved=20e6,
    )
    group_b.core()
    dqkv, bias_grads = order(
        kernel_attention_back,
        [VMEM] * 3,
        [shape((tokens, 3 * width), bf16), shape((2, width), f32)],
        (dctx, qkv, keep),
        flops=10 * tokens * width * width,
        moved=10e6,
    )
    input_grad, norm_grads = order(
        kernel_input_back,
        [VMEM] * 5,
        [shape((tokens, width), f32), shape((2, width), f32)],
        (dqkv, dh, hidden_in, vec, w_att),
        flops=6 * tokens * width * width,
        moved=10e6,
    )
    group_c.first()
    mine, theirs = order(
        functools.partial(kernel_attention_grad, fs),
        [SMEM] + [VMEM] * 10,
        [shape((4, width + 16 * fs, PIECE), bf16)] * 2,
        (info, hidden_in, vec, ctx_turned, dqkv, da, norm_grads, bias_grads, mid_grads, down_bias_grad, up_bias_grad),
        scratch=[pltpu.VMEM((16, width), f32), pltpu.VMEM((16, PIECE), bf16)],
        flops=8 * tokens * width * width,
        moved=10e6,
    )
    group_a = Reduction(order, info, fs, dp, rows, mine, theirs)
    group_b.first()
    group_c.second_half()
    group_a.core()
    group_c.fold()
    group_b.second_half()
    group_c.line(rows)
    group_a.first()
    group_c.share_first()
    group_b.fold()
    group_c.share_second()
    group_b.line(rows)
    group_b.share_first()
    group_a.second()
    group_c.share()
    group_b.share_second()
    down_state = renew(order, info, fs, rows, group_c.pieces, down_master, down_momentum, down_average, None)
    group_b.share()
    group_a.line(rows)
    group_a.share_all()
    vectors = (*group_a.vectors, vector_master, vector_momentum, vector_average)
    wide_state = renew(
        order, info, fs, rows, group_b.pieces, wide_master, wide_momentum, wide_average, GROUP, vectors=vectors
    )
    wide_state, vector_state = wide_state[:4], wide_state[4:]
    group_a.share()
    wide_state = renew(order, info, fs, rows, group_a.pieces, wide_master, wide_momentum, wide_average, 0, wide_state)

    return (
        block_out,
        input_grad,
        wide_state[0],
        down_state[0],
        vector_state[0],
        wide_state[1],
        down_state[1],
        vector_state[1],
        wide_state[2],
        down_state[2],
        vector_state[2],
        wide_state[3],
        down_state[3],
        vector_state[3],
    )


def solution(mesh):
    tokens = P(("dp", "fsdp"), None)
    each = P(("dp", "fsdp"))
    by_row = P("fsdp", None)
    by_col = P(None, "fsdp")
    states = (by_row, by_row, by_col)
    return jax.shard_map(
        functools.partial(body, mesh.shape["fsdp"], mesh.shape["dp"]),
        mesh=mesh,
        in_specs=(tokens, each, tokens, each) + states * 3,
        out_specs=(tokens, tokens) + states * 4,
        check_vma=False,
    )
```

```python
import functools

import jax
import jax.numpy as jnp
from jax import lax
from jax.experimental import pallas as pl
from jax.experimental.pallas import tpu as pltpu
from jax.sharding import PartitionSpec as P

HEADS = 12
SEQ = 16
PIECE = 384
GROUP = 8
PICTURE_TAGS = 16
LIGHT = (8, 22, 24, 36, 41, 42, 43, 46)

norm_epsilon = 1e-06
masked_score = -1e30
learn_rate = 0.02
momentum_decay = 0.5
average_decay = 0.5
gelu_scale = 0.7978845608028654
gelu_cube = 0.044715

f32 = jnp.float32
bf16 = jnp.bfloat16
VMEM = pl.BlockSpec(memory_space=pltpu.VMEM)
SMEM = pl.BlockSpec(memory_space=pltpu.SMEM)
ANY = pl.BlockSpec(memory_space=pl.ANY)
HBM = pl.BlockSpec(memory_space=pltpu.HBM)
PARAMS = pltpu.CompilerParams(vmem_limit_bytes=32 * 1024 * 1024)


def dot(left, right):
    return lax.dot_general(left, right, (((1,), (0,)), ((), ())), preferred_element_type=f32)


def dot_nt(left, right):
    return lax.dot_general(left, right, (((1,), (1,)), ((), ())), preferred_element_type=f32)


def dot_tn(left, right):
    return lax.dot_general(left, right, (((0,), (0,)), ((), ())), preferred_element_type=f32)


def shape(dims, kind):
    return jax.ShapeDtypeStruct(dims, kind)


class Order:
    def __init__(self, light):
        self.last, self.light, self.count = (), light, 0

    def weight(self):
        self.count += 1
        return cost(1 if self.count - 1 in self.light else 10**11, 1)

    def __call__(self, kernel, in_specs, out_shape, args, after=(), out_specs=None, scratch=(), flops=0, moved=0, limit=16):
        after = [*self.last, *after]
        count, skip = len(in_specs), len(after)

        def run(*refs):
            kernel(*refs[:count], *refs[count + skip :])

        outs = pl.pallas_call(
            run,
            in_specs=list(in_specs) + [ANY] * skip,
            out_specs=out_specs or [VMEM] * len(out_shape),
            out_shape=out_shape,
            scratch_shapes=scratch,
            compiler_params=pltpu.CompilerParams(vmem_limit_bytes=limit * 1024 * 1024),
            cost_estimate=self.weight(),
        )(*args, *after)
        self.last = (min(outs, key=lambda value: value.size),)
        return outs


def cost(flops, moved):
    return pl.CostEstimate(flops=int(flops), bytes_accessed=int(moved), transcendentals=0)


def norm_parts(values):
    centre = values - jnp.mean(values, axis=-1, keepdims=True)
    inv = lax.rsqrt(jnp.mean(centre * centre, axis=-1, keepdims=True) + norm_epsilon)
    return centre * inv, inv


def norm_back(grad, scaled, inv, gain):
    d_scaled = grad * gain
    first = jnp.mean(d_scaled, axis=-1, keepdims=True)
    second = jnp.mean(d_scaled * scaled, axis=-1, keepdims=True)
    return inv * (d_scaled - first - scaled * second)


def piece_copies(info, fs, rows, sides, target, sems, is_down):
    copies = []
    for k in range(GROUP):
        for j in range(1, fs):
            shard = info[3 + j]
            place = info[3 + fs + k]
            row = shard * rows
            if is_down:
                row = row * 4 + (place % 4) * rows
                col = (place // 4) * PIECE
            else:
                col = place * PIECE
            first = ((k // 2) * (fs - 1) + j - 1) * rows
            copies.append(
                pltpu.make_async_copy(
                    sides[k % 2].at[pl.ds(first, rows), :],
                    target.at[pl.ds(pl.multiple_of(row, 16), rows), pl.ds(pl.multiple_of(col, 128), PIECE)],
                    sems.at[len(copies)],
                )
            )
    return copies


def picture_copies(info, fs, captions, sides, images, tags, image_sem, tag_sem):
    block = PICTURE_TAGS
    members = sides[0].shape[0] // (block + 2 * captions) // fs
    rank, z = info[info.shape[0] - 3], info[0]
    for side in range(2):
        for j in range(fs):
            for m in range(members):
                device = (rank ^ (2 * m + side)) * fs + (z ^ j)
                first = (j * members + m) * (block + 2 * captions)
                to = pl.ds(pl.multiple_of(device * captions, 16), captions)
                for half in range(2):
                    pltpu.make_async_copy(
                        sides[side].at[pl.ds(first + half * captions, captions), :],
                        images.at[to, pl.ds(half * PIECE, PIECE)],
                        image_sem,
                    ).start()
                pltpu.make_async_copy(
                    sides[side].at[pl.ds(first + 2 * captions, block), pl.ds(0, 128)],
                    tags.at[pl.ds(pl.multiple_of(device * block, 16), block), :],
                    tag_sem,
                ).start()


def attend_forward(queries, keys, values, mask, half_low, half_high):
    both_q = jnp.concatenate([queries * half_low, queries * half_high], axis=0)
    scores = jnp.where(mask, dot_nt(both_q, keys) * 0.125, masked_score)
    top = jnp.max(scores, axis=-1, keepdims=True)
    raised = jnp.exp(scores - top)
    probs = raised / jnp.sum(raised, axis=-1, keepdims=True)
    return both_q, probs


def lane_halves():
    lane = lax.broadcasted_iota(jnp.int32, (1, 128), 1)
    low = (lane < 64).astype(f32)
    return low, low.astype(bf16), (1.0 - low).astype(bf16)


def caption_mask(valid_row):
    row = lax.broadcasted_iota(jnp.int32, (256, 128), 0)
    col = lax.broadcasted_iota(jnp.int32, (256, 128), 1)
    same = ((row & 127) // SEQ) == (col // SEQ)
    return same & (valid_row > 0.0)


def kernel_qkv(fs, rows, info, hid, vec, own, near, far, qkv_ref, w, w_out, sems):
    width = hid.shape[1]
    copies = piece_copies(info, fs, rows, (near, far), w, sems, False)
    for copy in copies:
        copy.start()
    vecs = vec[...]
    scaled, _ = norm_parts(hid[...].astype(f32))
    normed = (scaled * vecs[0:1] + vecs[1:2]).astype(bf16)
    w[pl.ds(pl.multiple_of(info[0] * rows, 16), rows), :] = own[...]
    for copy in copies:
        copy.wait()
    for part in range(3):
        cols = pl.ds(part * width, width)
        value = dot(normed, w[:, cols])
        if part == 0:
            value = value + vecs[2:3]
        if part == 2:
            value = value + vecs[3:4]
        qkv_ref[:, cols] = value.astype(bf16)
    w_out[...] = w[:, 3 * width :]


def kernel_attention(hid, valid, vec, qkv, w, ctx_ref, h_ref, second_ref):
    tokens, width = hid.shape
    low_f, low, high = lane_halves()

    def block(index, carry):
        at = pl.ds(pl.multiple_of(index * 128, 128), 128)
        mask = caption_mask(valid[:, at])
        for pair in range(width // 128):
            here = pair * 128
            queries = qkv[at, here : here + 128]
            keys = qkv[at, width + here : width + here + 128]
            values = qkv[at, 2 * width + here : 2 * width + here + 128]
            _, probs = attend_forward(queries, keys, values, mask, low, high)
            context = dot(probs.astype(bf16), values)
            ctx_ref[at, here : here + 128] = jnp.where(low_f > 0.0, context[:128], context[128:]).astype(bf16)
        return carry

    lax.fori_loop(0, tokens // 128, block, 0)
    residual = hid[...].astype(f32) + (dot(ctx_ref[...], w[...]) + vec[4:5, :])
    h_ref[...] = residual
    scaled, _ = norm_parts(residual)
    second_ref[...] = (scaled * vec[5:6, :] + vec[6:7, :]).astype(bf16)


def kernel_up(fs, rows, info, second, bias, own, near, far, slope_ref, g_ref, w, sems):
    width, hidden = w.shape
    copies = piece_copies(info, fs, rows, (near, far), w, sems, False)
    for copy in copies:
        copy.start()
    w[pl.ds(pl.multiple_of(info[0] * rows, 16), rows), :] = own[...]
    for copy in copies:
        copy.wait()

    def block(index, carry):
        cols = pl.ds(index * 512, 512)
        value = dot(second[...], w[:, cols]) + bias[:, cols]
        square = value * value
        inner = jnp.tanh(gelu_scale * (value + gelu_cube * value * square))
        slope = 0.5 * (1.0 + inner) + (0.5 * gelu_scale) * value * (1.0 - inner * inner) * (1.0 + (3.0 * gelu_cube) * square)
        slope_ref[:, cols] = slope.astype(bf16)
        g_ref[:, cols] = (0.5 * value * (1.0 + inner)).astype(bf16)
        return carry

    for index in range(hidden // 512):
        block(index, 0)


def kernel_down(fs, rows, info, g, h, vec, lens, keep, own, near, far, near_images, far_images, *rest):
    out_ref, pooled_ref, inv_ref, logit_ref, stat_ref, images, tags, w, sems, image_sem, tag_sem = rest
    tokens, width = h.shape
    captions = tokens // SEQ
    copies = piece_copies(info, fs, rows, (near, far), w, sems, True)
    picture_copies(info, fs, captions, (near_images, far_images), images, tags, image_sem, tag_sem)
    for copy in copies:
        copy.start()
    w[pl.ds(pl.multiple_of(info[0] * 4 * rows, 16), 4 * rows), :] = own[...]
    for copy in copies:
        copy.wait()
    block_rows = h[...] + (dot(g[...], w[...]) + vec[7:8, :])
    out_ref[...] = block_rows.astype(bf16)
    pooled = jnp.sum((block_rows * keep[...]).reshape(captions, SEQ, width), axis=1) / lens[...]
    inv = lax.rsqrt(jnp.sum(pooled * pooled, axis=-1, keepdims=True) + norm_epsilon)
    pooled_ref[...] = pooled
    inv_ref[...] = inv
    texts = (pooled * inv).astype(bf16)
    pltpu.make_async_copy(images, images, image_sem).wait()
    pltpu.make_async_copy(tags, tags, tag_sem).wait()
    logits = dot_nt(texts, images[...])
    logit_ref[...] = logits
    top = jnp.max(logits, axis=0, keepdims=True)
    stat_ref[0:1, :] = top
    stat_ref[1:2, :] = jnp.sum(jnp.exp(logits - top), axis=0, keepdims=True)


def put(info, half, place, value, mine, theirs):
    rows = value.shape[0]

    @pl.when(info[1] == half)
    def _():
        mine[place[0], pl.ds(place[1], rows), :] = value

    @pl.when(info[1] != half)
    def _():
        theirs[place[0], pl.ds(place[1], rows), :] = value


def kernel_loss(rows, info, logits, stats, labels, images, pooled, inv, lens, keep, g, dpl_ref, dy_ref, bias_ref, mine, theirs):
    captions, width = pooled.shape
    hidden, tokens = g.shape
    lse = stats[0:1, :] + jnp.log(stats[1:2, :])
    number = lax.broadcasted_iota(jnp.int32, logits.shape, 0) + info[2] * captions
    onehot = (labels[...] == number).astype(f32)
    slopes = (jnp.exp(logits[...] - lse) - onehot).astype(bf16)
    text_grad = dot(slopes, images[...])
    pool, inv_v = pooled[...], inv[...]
    d_pooled = inv_v * text_grad - inv_v**3 * pool * jnp.sum(pool * text_grad, axis=-1, keepdims=True)
    dpl = d_pooled / lens[...]
    dpl_ref[...] = dpl
    d_out = jnp.broadcast_to(dpl[:, None, :], (captions, SEQ, width)).reshape(tokens, width) * keep[...]
    dy = d_out.astype(bf16)
    dy_ref[...] = dy
    bias_ref[...] = jnp.sum(dy.astype(f32), axis=0, keepdims=True)
    for part in range(hidden // width):
        grad = dot(g[part * width : (part + 1) * width, :], dy).astype(bf16)
        for sub in range(width // rows):
            first = part * width + sub * rows
            shard, quarter = first // (4 * rows), (first % (4 * rows)) // rows
            for half in range(2):
                value = grad[sub * rows : (sub + 1) * rows, half * PIECE : (half + 1) * PIECE]
                put(info, half, (quarter, shard * rows), value, mine, theirs)


def kernel_gelu_back(dy, slope, w_down, du_ref, bias_ref):
    tokens, hidden = slope.shape
    for part in range(hidden // 768):
        cols = slice(part * 768, (part + 1) * 768)
        du = (dot_nt(dy[...], w_down[cols, :]) * slope[:, cols].astype(f32)).astype(bf16)
        du_ref[:, cols] = du
        bias_ref[:, cols] = jnp.sum(du.astype(f32), axis=0, keepdims=True)


def kernel_up_grad(info, du, second, mine, theirs):
    turned = second[...]
    for pair in range(du.shape[1] // PIECE // 2):
        grad = dot(turned, du[:, 2 * pair * PIECE : 2 * (pair + 1) * PIECE]).astype(bf16)
        for part in range(2):
            place = 2 * pair + part
            put(info, place // 4, (place % 4, 0), grad[:, part * PIECE : (part + 1) * PIECE], mine, theirs)


def kernel_mid_back(dpl, keep, du, h, vec, w_up, w_out, dh_ref, da_ref, dctx_ref, grads_ref):
    tokens, width = h.shape
    captions = tokens // SEQ
    d_second = dot_nt(du[...], w_up[...])
    scaled, inv = norm_parts(h[...])
    d_out = jnp.broadcast_to(dpl[...][:, None, :], (captions, SEQ, width)).reshape(tokens, width) * keep[...]
    dh = d_out + norm_back(d_second, scaled, inv, vec[5:6, :])
    dh_ref[...] = dh
    da = dh.astype(bf16)
    da_ref[...] = da
    grads_ref[0:1, :] = jnp.sum(da.astype(f32), axis=0, keepdims=True)
    grads_ref[1:2, :] = jnp.sum(d_second * scaled, axis=0, keepdims=True)
    grads_ref[2:3, :] = jnp.sum(d_second, axis=0, keepdims=True)
    dctx_ref[...] = dot_nt(da, w_out[...]).astype(bf16)


def kernel_attention_back(dctx, qkv, keep, dqkv_ref, grads_ref):
    tokens, width = dctx.shape
    low_f, low, high = lane_halves()
    row = lax.broadcasted_iota(jnp.int32, (128, 256), 0)
    col = lax.broadcasted_iota(jnp.int32, (128, 256), 1)
    same = (row // SEQ) == ((col & 127) // SEQ)

    def block(index, carry):
        at = pl.ds(pl.multiple_of(index * 128, 128), 128)
        mask = same & (keep[at, :] > 0.0)
        for pair in range(width // 128):
            here = pair * 128
            queries = qkv[at, here : here + 128]
            keys = qkv[at, width + here : width + here + 128]
            values = qkv[at, 2 * width + here : 2 * width + here + 128]
            d_context = dctx[at, here : here + 128]
            both_q = jnp.concatenate([queries * low, queries * high], axis=0)
            both_d = jnp.concatenate([d_context * low, d_context * high], axis=0)
            scores = jnp.where(mask, dot_nt(keys, both_q) * 0.125, masked_score)
            raised = jnp.exp(scores - jnp.max(scores, axis=0, keepdims=True))
            probs = raised / jnp.sum(raised, axis=0, keepdims=True)
            weighted = probs * dot_nt(values, both_d)
            d_scores = (weighted - probs * jnp.sum(weighted, axis=0, keepdims=True)).astype(bf16)
            d_both = dot_tn(d_scores, keys) * 0.125
            d_queries = jnp.where(low_f > 0.0, d_both[:128], d_both[128:])
            dqkv_ref[at, here : here + 128] = d_queries.astype(bf16)
            dqkv_ref[at, width + here : width + here + 128] = (dot(d_scores, both_q) * 0.125).astype(bf16)
            dqkv_ref[at, 2 * width + here : 2 * width + here + 128] = dot(probs.astype(bf16), both_d).astype(bf16)
        return carry

    lax.fori_loop(0, tokens // 128, block, 0)
    grads_ref[0:1, :] = jnp.sum(dqkv_ref[:, :width].astype(f32), axis=0, keepdims=True)
    grads_ref[1:2, :] = jnp.sum(dqkv_ref[:, 2 * width :].astype(f32), axis=0, keepdims=True)


def kernel_attention_grad(fs, info, hid, vec, ctx, dqkv, da, *refs):
    *vectors, up_bias, mine, theirs, held, block = refs
    width = hid.shape[1]
    scaled, _ = norm_parts(hid[...].astype(f32))
    turned = (scaled * vec[0:1, :] + vec[1:2, :]).astype(bf16).T
    for third in range(3):
        grad = dot(turned, dqkv[:, third * width : (third + 1) * width]).astype(bf16)
        for part in range(2):
            place = third * 2 + part
            put(info, place // 4, (place % 4, 0), grad[:, part * PIECE : (part + 1) * PIECE], mine, theirs)
    grad = dot(ctx[...], da[...]).astype(bf16)
    for part in range(2):
        put(info, 1, (2 + part, 0), grad[:, part * PIECE : (part + 1) * PIECE], mine, theirs)
    held[...] = jnp.zeros_like(held)
    row = 0
    for ref in vectors:
        held[row : row + ref.shape[0], :] = ref[...]
        row += ref.shape[0]
    for part in range(4):
        held[row + part : row + part + 1, :] = up_bias[:, part * width : (part + 1) * width]
    block[...] = jnp.zeros_like(block)
    step = width // fs
    for shard in range(fs):
        block[:, :step] = held[:, shard * step : (shard + 1) * step].astype(bf16)
        for spot in range(4):
            for ref in (mine, theirs):
                ref[spot, width + 16 * shard : width + 16 * (shard + 1), :] = block[...]


def kernel_input_back(dqkv, dh, hid, vec, w_att, out_ref, grads_ref):
    width = hid.shape[1]
    d_normed = dot_nt(dqkv[...], w_att[:, : 3 * width])
    scaled, inv = norm_parts(hid[...].astype(f32))
    out_ref[...] = dh[...] + norm_back(d_normed, scaled, inv, vec[0:1, :])
    grads_ref[0:1, :] = jnp.sum(d_normed * scaled, axis=0, keepdims=True)
    grads_ref[1:2, :] = jnp.sum(d_normed, axis=0, keepdims=True)


def renew_state(master, momentum, average, gradient):
    momentum_new = momentum_decay * momentum + gradient
    master_new = master - learn_rate * (gradient + momentum_decay * momentum_new)
    average_new = average_decay * average + (1.0 - average_decay) * master_new
    return (master_new, momentum_new, average_new, master_new.astype(bf16))


def kernel_renew(fs, column, skip, info, near, far, *refs):
    states, outs = refs[:3], refs[3 + skip : 7 + skip]
    *vectors, token, buf, new_f, new_h, in_sem, out_sem = refs[7 + skip :]
    rows = buf.shape[2]
    token[...] = jnp.zeros_like(token)
    if vectors:
        grad, *old = refs[3:7]
        new = renew_state(*(ref[...] for ref in old), grad[: old[0].shape[0], : old[0].shape[1]])
        for ref, value in zip(vectors, new):
            ref[...] = value

    def at(k):
        spot = info[3 + fs + k]
        if column is None:
            row, col = pl.multiple_of((spot % 4) * rows, 16), (spot // 4) * PIECE
        else:
            row, col = 0, (column + spot) * PIECE
        return pl.ds(row, rows), pl.ds(pl.multiple_of(col, 128), PIECE)

    def read(k, i):
        return pltpu.make_async_copy(states[i].at[at(k)], buf.at[k, i], in_sem.at[k, i])

    def write(k, i):
        source = new_h.at[k] if i == 3 else new_f.at[k, i]
        return pltpu.make_async_copy(source, outs[i].at[at(k)], out_sem.at[k, i])

    for k in range(GROUP):
        for i in range(3):
            read(k, i).start()
    for k in range(GROUP):
        for i in range(3):
            read(k, i).wait()
        source = far if k % 2 else near

        def step(index, carry):
            at = pl.ds(pl.multiple_of(index * 16, 16), 16)
            grad = source[pl.ds(pl.multiple_of(k // 2 * rows + index * 16, 16), 16), :].astype(f32)
            *new, half = renew_state(buf[k, 0, at], buf[k, 1, at], buf[k, 2, at], grad)
            for i in range(3):
                new_f[k, i, at] = new[i]
            new_h[k, at] = half
            return carry

        lax.fori_loop(0, rows // 16, step, 0, unroll=True)
        for i in range(4):
            write(k, i).start()
    for k in range(GROUP):
        for i in range(4):
            write(k, i).wait()


def renew(order, info, fs, rows, grads, master, momentum, average, column, earlier=(), vectors=()):
    skip = len(earlier) + len(order.last) + len(vectors)
    kinds = (f32, f32, f32, bf16)
    *outs, token = pl.pallas_call(
        functools.partial(kernel_renew, fs, column, skip),
        in_specs=[SMEM] + [VMEM] * 2 + [HBM] * 3 + [VMEM] * len(vectors) + [HBM] * len(earlier) + [ANY] * len(order.last),
        out_specs=[HBM] * 4 + [VMEM] * len(vectors) + [VMEM],
        out_shape=[shape(master.shape, kind) for kind in kinds]
        + [shape(vectors[1].shape, kind) for kind in kinds if vectors]
        + [shape((8, 128), f32)],
        scratch_shapes=[
            pltpu.VMEM((GROUP, 3, rows, PIECE), f32),
            pltpu.VMEM((GROUP, 3, rows, PIECE), f32),
            pltpu.VMEM((GROUP, rows, PIECE), bf16),
            pltpu.SemaphoreType.DMA((GROUP, 3)),
            pltpu.SemaphoreType.DMA((GROUP, 4)),
        ],
        input_output_aliases={6 + i: i for i in range(len(earlier))},
        compiler_params=pltpu.CompilerParams(vmem_limit_bytes=60 * 1024 * 1024),
        cost_estimate=order.weight(),
    )(info, *grads, master, momentum, average, *vectors, *earlier, *order.last)
    order.last = (token,)
    return outs


def flip(count, bit):
    return [(i, i ^ bit) for i in range(count)]


def send(value, axis, count, bit):
    return lax.ppermute(value, axis, flip(count, bit))


def kernel_pack(rows, *refs):
    *refs, own, near, piece = refs
    piece[...] = own[...]
    for j, ref in enumerate(refs):
        near[j * rows : (j + 1) * rows, :] = ref[:rows, :]


def kernel_cast(wide, down, out_a, out_b, out_c):
    cols = out_a.shape[1]
    out_a[...] = wide[:, :cols].astype(bf16)
    out_b[...] = wide[:, cols:].astype(bf16)
    out_c[...] = down[...].astype(bf16)


def kernel_join(*refs):
    *parts, out = refs
    row = 0
    for part in parts:
        out[row : row + part.shape[0], :] = part[...]
        row += part.shape[0]


def kernel_pack_first(fs, rows, info, own, *refs):
    *refs, near, vec, bias, wide = refs
    width = vec.shape[1]
    wide[...] = jnp.zeros_like(wide)
    total = jnp.zeros(vec.shape, f32)
    for j, ref in enumerate([own, *refs]):
        if j:
            near[(j - 1) * rows : j * rows, :] = ref[:rows, :]
        wide[:, :PIECE] = ref[rows:, :].astype(f32)
        total = total + pltpu.roll(wide[...], info[3 + j] * (width // fs), 1)
    vec[...] = total
    for row in range(4):
        bias[:, row * width : (row + 1) * width] = total[8 + row : 9 + row, :]


def kernel_sorted(rows, places, *refs):
    *parts, out = refs
    for part, of_part in zip(parts, places):
        for i, place in enumerate(of_part):
            out[place * rows : (place + 1) * rows, :] = part[i * rows : (i + 1) * rows, :]


def kernel_halves(over_x, over_y, first, second):
    cut = first.shape[0]
    first[...] = over_x[:cut, :]
    second[...] = over_y[cut:, :]


def kernel_copy(value, out):
    out[...] = value[...]


def total_of(left, right):
    return (left.astype(f32) + right.astype(f32)).astype(bf16)


def kernel_add_core(fs, rows, info, mine, came, *refs):
    to_x, to_y, keep_x, keep_y = refs
    step = to_x.shape[1] * 2 // fs
    x, y = info[info.shape[0] - 2], info[info.shape[0] - 1]
    for other in range(2):
        for ref, spot, first in (
            (to_x, other * 2 + (1 - x), 0),
            (to_y, (1 - y) * 2 + other, fs // 2),
            (keep_x, other * 2 + x, 0),
            (keep_y, y * 2 + other, fs // 2),
        ):
            for shard in range(fs // 2):
                at = pl.ds((first + shard) * rows, rows)
                ref[other, pl.ds(shard * step, rows), :] = total_of(mine[spot, at, :], came[spot, at, :])
                if step > rows:
                    at = pl.ds(fs * rows + (first + shard) * 16, 16)
                    ref[other, pl.ds(shard * step + rows, 16), :] = total_of(mine[spot, at, :], came[spot, at, :])


def kernel_add_first(info, keep_x, keep_y, came_x, came_y, to_y, to_x, left_x, left_y):
    x, y = info[info.shape[0] - 2], info[info.shape[0] - 1]
    to_y[...] = total_of(keep_x[1 - y], came_x[1 - y])
    to_x[...] = total_of(keep_y[1 - x], came_y[1 - x])
    left_x[...] = total_of(keep_x[y], came_x[y])
    left_y[...] = total_of(keep_y[x], came_y[x])


def kernel_add_second(fs, rows, info, left_x, left_y, came_y, came_x, *refs):
    *outs, own = refs
    half = left_x.shape[0]
    own[:half, :] = total_of(left_x[...], came_y[...])
    own[half:, :] = total_of(left_y[...], came_x[...])
    for j, ref in enumerate(outs):
        ref[...] = own[pl.ds(pl.multiple_of(info[3 + j] * rows, 16), rows), :]


def kernel_add_second_half(fs, rows, info, left_x, left_y, came_y, came_x, keep, give, own):
    half = left_x.shape[0]
    own[:half, :] = total_of(left_x[...], came_y[...])
    own[half:, :] = total_of(left_y[...], came_x[...])
    for j in range(fs):
        ref = give if j % 2 else keep
        block = own[pl.ds(pl.multiple_of(info[3 + j] * rows, 16), rows), :]
        ref[j // 2 * rows : (j // 2 + 1) * rows, :] = block


def kernel_fold(rows, keep, came, left, give):
    for j in range(keep.shape[0] // rows):
        ref = give if j % 2 else left
        at = slice(j * rows, (j + 1) * rows)
        ref[j // 2 * rows : (j // 2 + 1) * rows, :] = total_of(keep[at, :], came[at, :])


def kernel_add_z(fs, *refs):
    parts, (out, *vectors) = refs[:fs], refs[fs:]
    rows = out.shape[0]
    out[...] = sum(part[:rows, :].astype(f32) for part in parts).astype(bf16)
    for ref in vectors:
        ref[...] = sum(part[rows:, :].astype(f32) for part in parts)


class Reduction:
    def __init__(self, order, info, fs, dp, rows, mine, theirs):
        self.order, self.info, self.fs, self.dp, self.rows = order, info, fs, dp, rows
        self.width = mine.shape[1]
        mine, theirs = self.beyond(mine), self.beyond(theirs)
        self.mine = [mine, send(theirs, "dp", dp, 1)]

    def beyond(self, value):
        bit = GROUP
        while bit < self.dp:
            value = total_of(value, send(value, "dp", self.dp, bit))
            bit *= 2
        return value

    def core(self):
        rows, self.rows = self.rows, self.width // self.fs
        to_x, to_y, *self.keep = self.order(
            functools.partial(kernel_add_core, self.fs, rows),
            [SMEM] + [VMEM] * 2,
            [shape((2, self.width // 2, PIECE), bf16)] * 4,
            (self.info, *self.mine),
        )
        self.came = send(to_x, "dp", self.dp, 2), send(to_y, "dp", self.dp, 4)

    def first(self):
        half = self.width // 2
        to_y, to_x, *self.keep = self.order(
            kernel_add_first,
            [SMEM] + [VMEM] * 4,
            [shape((half, PIECE), bf16)] * 4,
            (self.info, *self.keep, *self.came),
            moved=3e6,
        )
        self.came = send(to_y, "dp", self.dp, 4), send(to_x, "dp", self.dp, 2)

    def second(self):
        parts = self.order(
            functools.partial(kernel_add_second, self.fs, self.rows),
            [SMEM] + [VMEM] * 4,
            [shape((self.rows, PIECE), bf16)] * self.fs,
            (self.info, *self.keep, *self.came),
            scratch=[pltpu.VMEM((self.width, PIECE), bf16)],
            moved=2e6,
        )
        self.came = [parts[0]] + [send(parts[j], "fsdp", self.fs, j) for j in range(1, self.fs)]

    def second_half(self):
        self.bit, count = 1, self.fs // 2
        keep, give = self.order(
            functools.partial(kernel_add_second_half, self.fs, self.rows),
            [SMEM] + [VMEM] * 4,
            [shape((count * self.rows, PIECE), bf16)] * 2,
            (self.info, *self.keep, *self.came),
            scratch=[pltpu.VMEM((self.width, PIECE), bf16)],
        )
        self.came = [keep, send(give, "fsdp", self.fs, 1)]

    def fold(self):
        while 2 * self.bit < self.fs:
            self.bit *= 2
            count = self.fs // self.bit // 2
            keep, give = self.order(
                functools.partial(kernel_fold, self.rows),
                [VMEM] * 2,
                [shape((count * self.rows, PIECE), bf16)] * 2,
                self.came,
            )
            self.came = [keep, send(give, "fsdp", self.fs, self.bit)]

    def line(self, grad_rows):
        count = len(self.came)
        extra = [shape((self.rows - grad_rows, PIECE), f32)] if self.rows > grad_rows else []
        piece, *self.vectors = self.order(
            functools.partial(kernel_add_z, count), [VMEM] * count, [shape((grad_rows, PIECE), bf16)] + extra, self.came
        )
        self.rows, self.piece = grad_rows, piece

    def share_first(self):
        self.came = [self.piece, send(self.piece, "dp", self.dp, 2)]

    def share_second(self):
        (pair,) = self.order(kernel_join, [VMEM] * 2, [shape((2 * self.rows, PIECE), bf16)], self.came)
        self.came = [pair, send(pair, "dp", self.dp, 4)]

    def share_all(self):
        self.came = [self.piece] + [send(self.piece, "dp", self.dp, k) for k in (2, 4, 6)]

    def share(self):
        (side,) = self.order(kernel_join, [VMEM] * len(self.came), [shape((4 * self.rows, PIECE), bf16)], self.came)
        self.pieces = side, send(side, "dp", self.dp, 1)


def merge_stats(group):
    top = functools.reduce(jnp.maximum, [top for top, _ in group])
    return top, sum(mass * jnp.exp(old - top) for old, mass in group)


def kernel_merge(*refs):
    *parts, out = refs
    top, mass = merge_stats([(part[0:1, :], part[1:2, :]) for part in parts])
    out[0:1, :] = top
    out[1:2, :] = mass


def kernel_turn(*refs):
    half = len(refs) // 2
    for value, out in zip(refs[:half], refs[half:]):
        out[...] = value[...].T


def body(
    fs,
    dp,
    hidden_in,
    lengths,
    images,
    labels,
    wide_master,
    down_master,
    vector_master,
    wide_momentum,
    down_momentum,
    vector_momentum,
    wide_average,
    down_average,
    vector_average,
):
    tokens, width = hidden_in.shape
    captions = lengths.shape[0]
    rows = wide_master.shape[0]
    hidden = wide_master.shape[1] - 4 * width
    rank, z = lax.axis_index("dp"), lax.axis_index("fsdp")
    core, x, y = rank % 2, rank // 2 % 2, rank // 4 % 2
    member = [rank ^ k for k in range(GROUP)]
    spots = [(m % 2) * 4 + (m // 4 % 2) * 2 + (m // 2 % 2) for m in member]
    info = jnp.stack([z, core, rank * fs + z] + [z ^ j for j in range(fs)] + spots + [rank, x, y]).astype(jnp.int32)

    place = jnp.arange(SEQ)
    keep = (place[None, :] < lengths[:, None]).astype(f32).reshape(tokens)
    valid, keep = keep[None, :], keep[:, None]
    lens = lengths.astype(f32)[:, None]

    order = Order(LIGHT)
    piece_shape = shape((rows, PIECE), bf16)
    near_shape = shape(((fs - 1) * rows, PIECE), bf16)

    def along_z(piece):
        return [send(piece, "fsdp", fs, j) for j in range(1, fs)]

    def pack(came, following):
        return order(
            functools.partial(kernel_pack, rows), [VMEM] * fs, [near_shape, piece_shape], (*came, following)
        )

    def hold(value):
        return order(kernel_copy, [VMEM], [shape(value.shape, bf16)], (value,))[0]

    def joined(parts):
        length = sum(part.shape[0] for part in parts)
        return order(kernel_join, [VMEM] * len(parts), [shape((length, PIECE), bf16)], parts)[0]

    def z_first(piece):
        bit = fs // 2
        return [piece, send(piece, "fsdp", fs, bit)], [[0], [bit]], bit

    def z_next(state):
        parts, places, bit = state
        while bit > 1:
            bit //= 2
            parts = parts + [send(joined(parts), "fsdp", fs, bit)]
            places = places + [[place ^ bit for of_part in places for place in of_part]]
        return parts, places

    def z_last(state):
        parts, places = state
        places = [[place - 1 for place in of_part] for of_part in places[1:]]
        return order(
            functools.partial(kernel_sorted, rows, places), [VMEM] * (len(parts) - 1), [near_shape], parts[1:]
        )[0]

    def over_plane(near):
        return near, send(near, "dp", dp, 2), send(near, "dp", dp, 4)

    def corner(near, over_x, over_y):
        cut = near.shape[0] // 32 * 16
        diag_a, diag_b = order(
            kernel_halves,
            [VMEM] * 2,
            [shape((cut, PIECE), bf16), shape((near.shape[0] - cut, PIECE), bf16)],
            (over_x, over_y),
        )
        return near, over_x, over_y, send(diag_a, "dp", dp, 4), send(diag_b, "dp", dp, 2)

    def join(parts):
        side = joined(parts)
        return side, send(side, "dp", dp, 1)

    spot = spots[0]

    def piece_of(values, column):
        return lax.dynamic_slice(values, (0, column + spot * PIECE), (rows, PIECE)).astype(bf16)

    total = captions * fs * dp
    tags = jnp.pad(jnp.stack([labels // 128, labels % 128]), ((0, PICTURE_TAGS - 2), (0, PIECE - captions)))
    picture = hold(jnp.concatenate([images[:, :PIECE], images[:, PIECE:], tags.astype(bf16)], axis=0))
    pictures = [picture, send(picture, "dp", dp, 2)]

    own_vec = jnp.pad(vector_master.astype(bf16), ((0, 4), (0, PIECE - vector_master.shape[1])))
    piece = hold(jnp.concatenate([piece_of(wide_master, 0), own_vec], axis=0))
    piece_b = piece_of(wide_master, 4 * width)
    piece_c = lax.dynamic_slice(down_master, ((spot % 4) * rows, (spot // 4) * PIECE), (rows, PIECE)).astype(bf16)
    came = along_z(piece)
    own_a, own_b, own_c = order(
        kernel_cast,
        [VMEM] * 2,
        [shape((rows, 4 * width), bf16), shape((rows, hidden), bf16), shape(down_master.shape, bf16)],
        (wide_master, down_master),
        limit=28,
    )
    bit = 4
    while bit < dp:
        picture = joined(pictures)
        pictures = [picture, send(picture, "dp", dp, bit)]
        bit *= 2
    near_a, vec, up_bias = order(
        functools.partial(kernel_pack_first, fs, rows),
        [SMEM] + [VMEM] * fs,
        [near_shape, shape((16, width), f32), shape((1, hidden), f32)],
        (info, piece, *came),
        scratch=[pltpu.VMEM((16, width), f32)],
    )
    plane_a = over_plane(near_a)
    came = along_z(hold(piece_b))
    corner_a = corner(*plane_a)
    near_b, piece_c = pack(came, piece_c)
    plane_b = over_plane(near_b)
    line_c = z_first(piece_c)
    parts_a = join(corner_a)
    gather_scratch = [pltpu.SemaphoreType.DMA((GROUP * fs * 2,))]

    qkv, w_att, w_out = order(
        functools.partial(kernel_qkv, fs, rows),
        [SMEM, VMEM, VMEM, VMEM] + [ANY] * 2,
        [shape((tokens, 3 * width), bf16), shape((width, 4 * width), bf16), shape((width, width), bf16)],
        (info, hidden_in, vec, own_a, *parts_a),
        scratch=gather_scratch,
        flops=6 * tokens * width * width,
        moved=10e6,
    )
    line_c = z_next(line_c)
    pictures = joined(pictures)
    pictures = [pictures] + along_z(pictures)
    corner_b = corner(*plane_b)
    ctx, h, second = order(
        kernel_attention,
        [VMEM] * 5,
        [shape((tokens, width), bf16), shape((tokens, width), f32), shape((tokens, width), bf16)],
        (hidden_in, valid, vec, qkv, w_out),
        flops=4 * tokens * width * width,
        moved=10e6,
    )
    near_c = z_last(line_c)
    plane_c = over_plane(near_c)
    parts_b = join(corner_b)
    slope, g, w_up = order(
        functools.partial(kernel_up, fs, rows),
        [SMEM, VMEM, VMEM, VMEM] + [ANY] * 2,
        [shape((tokens, hidden), bf16)] * 2 + [shape((width, hidden), bf16)],
        (info, second, up_bias, own_b, *parts_b),
        scratch=gather_scratch,
        flops=2 * tokens * width * hidden,
        moved=20e6,
    )
    corner_c = corner(*plane_c)
    pictures = join(pictures)
    parts_c = join(corner_c)
    block_out, pooled, inv, logits, stats, pictures, tags, w_down = order(
        functools.partial(kernel_down, fs, rows),
        [SMEM] + [VMEM] * 6 + [ANY] * 4,
        [
            shape((tokens, width), bf16),
            shape((captions, width), f32),
            shape((captions, 1), f32),
            shape((captions, total), f32),
            shape((2, total), f32),
            shape((total, width), bf16),
            shape((fs * dp * PICTURE_TAGS, 128), bf16),
            shape((hidden, width), bf16),
        ],
        (info, g, h, vec, lens, keep, own_c, *parts_c, *pictures),
        scratch=gather_scratch + [pltpu.SemaphoreType.DMA] * 2,
        limit=16 + (3 * total * width >> 20),
        flops=2 * tokens * width * hidden,
        moved=20e6,
    )

    tags = tags.reshape(fs * dp, PICTURE_TAGS, 128)[:, :2, :captions].astype(jnp.int32)
    all_labels = (tags[:, 0] * 128 + tags[:, 1]).reshape(1, total)

    def merged(came):
        return order(kernel_merge, [VMEM] * len(came), [shape((2, total), f32)], came, limit=16 + (total >> 9))[0]

    def turned(values):
        return order(kernel_turn, [VMEM] * len(values), [shape(value.shape[::-1], bf16) for value in values], values)

    came = [stats, send(stats, "dp", dp, 1)]
    g_turned = turned([g])[0]
    stats = merged(came)
    came = [stats] + [send(stats, "fsdp", fs, j) for j in range(1, fs)]
    (second_turned,) = turned([second])
    stats = merged(came)
    came = [stats] + [send(stats, "dp", dp, j) for j in range(2, dp, 2)]
    (ctx_turned,) = turned([ctx])
    stats = merged(came)

    halves = [shape((4, width, PIECE), bf16)] * 2
    dpl, dy, down_bias_grad, mine, theirs = order(
        functools.partial(kernel_loss, rows),
        [SMEM] + [VMEM] * 9,
        [shape((captions, width), f32), shape((tokens, width), bf16), shape((1, width), f32)] + halves,
        (info, logits, stats, all_labels, pictures, pooled, inv, lens, keep, g_turned),
        limit=16 + (3 * total * width >> 20),
        flops=2 * tokens * width * hidden,
        moved=10e6,
    )
    group_c = Reduction(order, info, fs, dp, rows, mine, theirs)
    du, up_bias_grad = order(
        kernel_gelu_back,
        [VMEM] * 3,
        [shape((tokens, hidden), bf16), shape((1, hidden), f32)],
        (dy, slope, w_down),
        flops=2 * tokens * width * hidden,
        moved=20e6,
    )
    group_c.core()
    mine, theirs = order(
        kernel_up_grad,
        [SMEM] + [VMEM] * 2,
        halves,
        (info, du, second_turned),
        flops=2 * tokens * width * hidden,
        moved=10e6,
    )
    group_b = Reduction(order, info, fs, dp, rows, mine, theirs)
    dh, da, dctx, mid_grads = order(
        kernel_mid_back,
        [VMEM] * 7,
        [
            shape((tokens, width), f32),
            shape((tokens, width), bf16),
            shape((tokens, width), bf16),
            shape((3, width), f32),
        ],
        (dpl, keep, du, h, vec, w_up, w_out),
        flops=10 * tokens * width * width,
        moved=20e6,
    )
    group_b.core()
    dqkv, bias_grads = order(
        kernel_attention_back,
        [VMEM] * 3,
        [shape((tokens, 3 * width), bf16), shape((2, width), f32)],
        (dctx, qkv, keep),
        flops=10 * tokens * width * width,
        moved=10e6,
    )
    input_grad, norm_grads = order(
        kernel_input_back,
        [VMEM] * 5,
        [shape((tokens, width), f32), shape((2, width), f32)],
        (dqkv, dh, hidden_in, vec, w_att),
        flops=6 * tokens * width * width,
        moved=10e6,
    )
    group_c.first()
    mine, theirs = order(
        functools.partial(kernel_attention_grad, fs),
        [SMEM] + [VMEM] * 10,
        [shape((4, width + 16 * fs, PIECE), bf16)] * 2,
        (info, hidden_in, vec, ctx_turned, dqkv, da, norm_grads, bias_grads, mid_grads, down_bias_grad, up_bias_grad),
        scratch=[pltpu.VMEM((16, width), f32), pltpu.VMEM((16, PIECE), bf16)],
        flops=8 * tokens * width * width,
        moved=10e6,
    )
    group_a = Reduction(order, info, fs, dp, rows, mine, theirs)
    group_b.first()
    group_c.second_half()
    group_a.core()
    group_c.fold()
    group_b.second_half()
    group_c.line(rows)
    group_a.first()
    group_c.share_first()
    group_b.fold()
    group_c.share_second()
    group_b.line(rows)
    group_b.share_first()
    group_a.second()
    group_c.share()
    group_b.share_second()
    down_state = renew(order, info, fs, rows, group_c.pieces, down_master, down_momentum, down_average, None)
    group_b.share()
    group_a.line(rows)
    group_a.share_all()
    vectors = (*group_a.vectors, vector_master, vector_momentum, vector_average)
    wide_state = renew(
        order, info, fs, rows, group_b.pieces, wide_master, wide_momentum, wide_average, GROUP, vectors=vectors
    )
    wide_state, vector_state = wide_state[:4], wide_state[4:]
    group_a.share()
    wide_state = renew(order, info, fs, rows, group_a.pieces, wide_master, wide_momentum, wide_average, 0, wide_state)

    return (
        block_out,
        input_grad,
        wide_state[0],
        down_state[0],
        vector_state[0],
        wide_state[1],
        down_state[1],
        vector_state[1],
        wide_state[2],
        down_state[2],
        vector_state[2],
        wide_state[3],
        down_state[3],
        vector_state[3],
    )


def solution(mesh):
    tokens = P(("dp", "fsdp"), None)
    each = P(("dp", "fsdp"))
    by_row = P("fsdp", None)
    by_col = P(None, "fsdp")
    states = (by_row, by_row, by_col)
    return jax.shard_map(
        functools.partial(body, mesh.shape["fsdp"], mesh.shape["dp"]),
        mesh=mesh,
        in_specs=(tokens, each, tokens, each) + states * 3,
        out_specs=(tokens, tokens) + states * 4,
        check_vma=False,
    )
```
